32 devices in a mesh: groups: 2 (over y), blk: 4 (over z), plane: 4 (over x, core).
Axes of the slice: x: 2, y: 2, z: 4, core: 2. Of those that a mesh axis runs over, the one named last changes fastest.
Arguments:
- orbitals: float32 [512, 1, 25600], P(('groups', 'blk'), None, 'plane'), parts along dimension 0, may hold values from -6 to 6
- kernel_half: float32 [1, 81, 81], replicated, may hold values from 0.1 to 10
- pair_own: int32 [384], P(('groups', 'blk')), parts along dimension 0, may hold values from 0 to 63
- pair_step: int32 [384], P(('groups', 'blk')), parts along dimension 0, may hold values from 0 to 2
- pair_remote: int32 [384], P(('groups', 'blk')), parts along dimension 0, may hold values from 0 to 63
- pair_count: int32 [8], P(('groups', 'blk')), parts along dimension 0, may hold values from 6 to 48, as said below
Outputs:
- exchange_part: float32 [512, 1, 25600], P(('groups', 'blk'), None, 'plane'), parts along dimension 0
The draws below stay inside these ranges and needn't reach their ends.
There are 2 independent parts, one for each index of `groups`. The reference program is written for one: setup_inputs(seed, part) draws one part's arguments, and reference() takes and returns one part's arrays. A program takes and returns all parts, laid end to end along the dimension named above; an argument that names none is the same for every part. Nothing has to cross between parts.
Inputs may be any that keep to these rules, and one draw needn't show every extreme that they name: `pair_count`: slots at or beyond a block's count are ignored whatever they hold; in every draw some block has all 48 slots live.
All inputs are finite; a program needn't handle non-finite values.
Results may differ from the reference program's by a relative error of at most 0.0003.
Values sent between devices are 32-bit elements; how exact they have to be, the bound alone decides.
No kernel may reach another device: no remote copies, remote signals or barrier semaphores. Data moves between devices by JAX's collectives and lax.ppermute only.
A program may use at most 64 MiB of HBM per device.

```python
import math
import jax
import jax.numpy as jnp
from jax import lax

ORB = 64
NG = 160
NH = 81
Z = 1
CAP = 48
STEPS = 3
ORBITALS = 256
PAIRS = 192
N_BLK = 4


def draw_pair_count(key, part):
    key = jax.random.fold_in(key, 11)
    first_key, second_key, third_key = jax.random.split(key, 3)
    partial_counts = jax.random.randint(first_key, (N_BLK,), CAP // 8, CAP // 2 + 1)
    full_blocks = jax.random.randint(second_key, (N_BLK,), 0, 8) == 0
    chosen = jax.random.randint(third_key, (), 0, N_BLK)
    full_blocks = full_blocks | (jnp.arange(N_BLK, dtype=jnp.int32) == chosen)
    return jnp.where(full_blocks, CAP, partial_counts).astype(jnp.int32)


def place_ends(array, own_key, smallest, top_value):
    dims = array.shape
    spot = [jax.random.randint(jax.random.fold_in(own_key, axis), (), 0, dims[axis]) for axis in range(len(dims))]
    array = array.at[tuple(spot)].set(smallest)
    longest = dims.index(max(dims))
    spot[longest] = (spot[longest] + 1) % dims[longest]
    return array.at[tuple(spot)].set(top_value)


def block_scale(stream_key, dims, cuts, low, top_value):
    level = 1.0
    for dim, parts in cuts:
        draws = jax.random.uniform(jax.random.fold_in(jax.random.fold_in(stream_key, 6), dim), (parts,), jnp.float32, low / len(cuts), top_value / len(cuts))
        level = level * jnp.repeat(jnp.exp(draws), dims[dim] // parts).reshape((-1,) + (1,) * (len(dims) - 1 - dim))
    return level


def gaussian(rng, shape, spread, limit, pieces=(), kind=jnp.bfloat16):
    level = block_scale(rng, shape, pieces, -0.22, 0.18) if pieces else 1.0
    drawn = jax.random.normal(rng, shape, jnp.float32) * spread * level
    return jnp.minimum(jnp.maximum(drawn, -limit), limit).astype(kind)


def setup_inputs(seed: int = 0, part: int = 0) -> dict:
    arg_keys = jax.random.split(jax.random.key(seed), 7)
    part_keys = jax.random.split(jax.random.fold_in(arg_keys[6], part), 7)
    orbitals = gaussian(part_keys[0], (ORBITALS, Z, NG * NG), 1.0, 6.0, ((0, 4), (2, 4)), jnp.float32)
    kernel_half = jnp.clip(jnp.exp(jax.random.uniform(arg_keys[1], (Z, NH, NH), jnp.float32, math.log(0.1), math.log(10.0))), 0.1, 10.0)
    pair_own = place_ends(jax.random.randint(part_keys[2], (PAIRS,), 0, ORB), jax.random.fold_in(part_keys[2], 1), 0, ORB - 1).astype(jnp.int32)
    pair_step = place_ends(jax.random.randint(part_keys[3], (PAIRS,), 0, STEPS), jax.random.fold_in(part_keys[3], 1), 0, STEPS - 1).astype(jnp.int32)
    pair_remote = place_ends(jax.random.randint(part_keys[4], (PAIRS,), 0, ORB), jax.random.fold_in(part_keys[4], 1), 0, ORB - 1).astype(jnp.int32)
    pair_count = draw_pair_count(jax.random.fold_in(jax.random.fold_in(arg_keys[6], part), 71), part)
    return {"orbitals": orbitals, "kernel_half": kernel_half, "pair_own": pair_own, "pair_step": pair_step, "pair_remote": pair_remote, "pair_count": pair_count}


highest = lax.Precision.HIGHEST


def cas_table(length):
    positions = jnp.arange(length, dtype=jnp.int32)
    product = (positions[:, None] * positions[None, :]) % length
    angles = (2.0 * jnp.pi / length) * product.astype(jnp.float32)
    return jnp.cos(angles) + jnp.sin(angles)


def expand_kernel(kernel_half, length):
    positions = jnp.arange(length, dtype=jnp.int32)
    folded = jnp.minimum(positions, length - positions)
    columns = jnp.arange(kernel_half.shape[1], dtype=jnp.int32)
    picker = (folded[:, None] == columns[None, :]).astype(jnp.float32)
    halfway = jnp.einsum('ab,zbc->zac', picker, kernel_half, precision=highest)
    return jnp.einsum('zac,dc->zad', halfway, picker, precision=highest)


def reference(orbitals, kernel_half, pair_own, pair_step, pair_remote, pair_count):
    cas_values = cas_table(NG)
    kernel = expand_kernel(kernel_half, NG)
    blocks = orbitals.reshape(N_BLK, ORB, Z, NG, NG)
    owners = pair_own.reshape(N_BLK, CAP)
    offsets = pair_step.reshape(N_BLK, CAP)
    partners = pair_remote.reshape(N_BLK, CAP)
    slot_ids = jnp.arange(CAP, dtype=jnp.int32)
    labels = jnp.arange(ORB, dtype=jnp.int32)

    def one_block(block_id):
        own_rows = blocks[block_id]
        own_ids = owners[block_id]
        step_ids = offsets[block_id]
        partner_ids = partners[block_id]
        remote = jnp.zeros((CAP, Z, NG, NG), jnp.float32)
        for offset in range(STEPS):
            source = (block_id - 1 - offset) % N_BLK
            visited = blocks[source]
            remote = jnp.where((step_ids == offset)[:, None, None, None], visited[partner_ids], remote)
        density = own_rows[own_ids] * remote
        spectrum = jnp.einsum('pzxy,yk->pzxk', density, cas_values, precision=highest)
        spectrum = jnp.einsum('pzxk,xq->pzqk', spectrum, cas_values, precision=highest)
        spectrum = spectrum * kernel[None]
        spatial = jnp.einsum('pzqk,qx->pzxk', spectrum, cas_values, precision=highest)
        potential = jnp.einsum('pzxk,ky->pzxy', spatial, cas_values, precision=highest) / float(NG * NG)
        live_mask = (slot_ids < pair_count[block_id]).astype(jnp.float32)
        selector = (labels[:, None] == own_ids[None, :]).astype(jnp.float32) * live_mask[None, :]
        weighted = (potential * remote).reshape(CAP, Z * NG * NG)
        summed = jnp.dot(selector, weighted, precision=highest, preferred_element_type=jnp.float32)
        return summed.reshape(ORB, Z, NG * NG)

    per_block = lax.map(one_block, jnp.arange(N_BLK, dtype=jnp.int32))
    return per_block.reshape(N_BLK * ORB, Z, NG * NG)
```

```python
import functools

import jax
import jax.numpy as jnp
import ml_dtypes
import numpy as np
from jax import lax
from jax.experimental import pallas as pl
from jax.experimental.pallas import tpu as pltpu
from jax.sharding import PartitionSpec as P

NG = 160
STEPS = 3
LANES = 128
GROUP = 4
LINES = 5
CAPACITIES = (16, 20, 24)

VMEM_LIMIT = 48 * 1024 * 1024
smem = pl.BlockSpec(memory_space=pltpu.SMEM)
vmem = pl.BlockSpec(memory_space=pltpu.VMEM)
hbm = pl.BlockSpec(memory_space=pl.ANY)


def split_table(table):
    high = table.astype(ml_dtypes.bfloat16)
    low = (table - high.astype(np.float64)).astype(ml_dtypes.bfloat16)
    return high, low


def make_tables(x_local):
    positions = np.arange(NG)
    angles = 2.0 * np.pi / NG * (positions[:, None] * positions[None, :] % NG)
    cas = np.cos(angles) + np.sin(angles)
    into = np.zeros((GROUP, 2 * LANES, NG))
    for r in range(GROUP):
        start = r * NG - r * LANES
        into[r, start : start + NG] = cas
    back = np.transpose(into, (0, 2, 1)).copy()
    order = np.arange(NG).reshape(NG // GROUP, GROUP).T.reshape(-1)
    mixed = cas[:, order]
    return split_table(into), split_table(back), split_table(mixed), split_table(mixed.T.copy())


def split_value(value):
    high = value.astype(jnp.bfloat16)
    low = (value - high.astype(jnp.float32)).astype(jnp.bfloat16)
    return high, low


def dot(a, b):
    return lax.dot_general(a, b, (((1,), (0,)), ((), ())), preferred_element_type=jnp.float32)


def dot3(a, b):
    return dot(a[0], b[0]) + (dot(a[0], b[1]) + dot(a[1], b[0]))


def plan_kernel(slots, orbs, planes, own, step, remote, count, request, place, seen, known):
    for s in range(STEPS):
        for k in range(slots):
            request[s * slots + k] = 0
        request[STEPS * slots + s] = 0
        for k in range(orbs):
            seen[s * orbs + k] = -1

    def visit(j, carry):
        live = j < count[0]
        s = jnp.where(live, step[j], 0)
        k = remote[j]
        at = seen[s * orbs + k]
        used = request[STEPS * slots + s]

        @pl.when(live & (at < 0))
        def _():
            request[s * slots + used] = k
            seen[s * orbs + k] = used
            request[STEPS * slots + s] = used + 1

        known[j] = jnp.where(live, s, 0)
        known[slots + j] = jnp.where(live, jnp.where(at < 0, used, at), 0)
        known[2 * slots + j] = jnp.where(live, own[j], -1)
        return carry

    lax.fori_loop(0, slots, visit, 0)
    me = lax.axis_index("plane")
    each = slots // planes
    for k in range(planes):
        first = partner(me, k, planes) * each
        for q in range(each):
            for part in range(3):
                place[part * slots + k * each + q] = known[part * slots + first + q]


def pack_kernel(capacity, slots, lines, wanted, orbitals, *sends):
    for s in range(STEPS):
        for c in range(capacity):
            row = wanted[s, c]
            sends[s][pl.ds(c * lines, lines), :] = orbitals[pl.ds(row * lines, lines), :]


def fetch(received, held, sems, size):
    copies = [
        pltpu.make_async_copy(received[s], held.at[pl.ds(s * size, size), :], sems.at[s])
        for s in range(STEPS)
    ]
    for copy in copies:
        copy.start()
    for copy in copies:
        copy.wait()


def density_kernel(capacity, slots, lines, planes, place, orbitals, *refs):
    received, parts, (held, sems) = refs[:STEPS], refs[STEPS : STEPS + planes], refs[STEPS + planes :]
    fetch(received, held, sems, capacity * lines)
    each = slots // planes
    for j in range(slots):
        far = (place[j] * capacity + place[slots + j]) * lines
        near = jnp.maximum(place[2 * slots + j], 0) * lines
        parts[j // each][pl.ds(j % each * lines, lines), :] = (
            orbitals[pl.ds(near, lines), :] * held[pl.ds(far, lines), :]
        )


def sum_kernel(capacity, slots, lines, planes, place, *refs):
    received, parts = refs[:STEPS], refs[STEPS : STEPS + planes]
    out, held, sems = refs[STEPS + planes :]
    copies = [
        pltpu.make_async_copy(
            received[s],
            held.at[pl.ds(s * capacity * lines, capacity * lines), :],
            sems.at[s],
        )
        for s in range(STEPS)
    ]
    for copy in copies:
        copy.start()
    out[...] = jnp.zeros_like(out)
    for copy in copies:
        copy.wait()
    each = slots // planes
    for j in range(slots):
        far = (place[j] * capacity + place[slots + j]) * lines
        near = place[2 * slots + j] * lines

        @pl.when(near >= 0)
        def _():
            out[pl.ds(near, lines), :] += (
                parts[j // each][pl.ds(j % each * lines, lines), :] * held[pl.ds(far, lines), :]
            )


def transform_kernel(pairs, lines, planes, *refs):
    parts = refs[:planes]
    into_hi, into_lo, back_hi, back_lo, mix_hi, mix_lo, unmix_hi, unmix_lo, kernel = refs[
        planes : planes + 9
    ]
    outs = refs[planes + 9 : 2 * planes + 9]
    cells, waves, result = refs[2 * planes + 9 :]
    whole = planes * lines
    rows = NG // GROUP
    me = lax.axis_index("plane")
    for k in range(planes):
        slab = partner(me, k, planes) * lines
        for p in range(pairs):
            cells[pl.ds(p * whole + slab, lines), :] = parts[k][pl.ds(p * lines, lines), :]
    line = [split_value(cells[pl.ds(t, pairs * rows, stride=LINES), :]) for t in range(LINES)]
    for r in range(GROUP):
        wide = [jnp.concatenate([line[r][i], line[r + 1][i]], axis=1) for i in range(2)]
        found = dot3(wide, (into_hi[r], into_lo[r]))
        for p in range(pairs):
            waves[p, r * rows : (r + 1) * rows, :] = found[p * rows : (p + 1) * rows, :]
    mix = (mix_hi[...], mix_lo[...])
    unmix = (unmix_hi[...], unmix_lo[...])
    for p in range(pairs):
        spectrum = dot3(mix, split_value(waves[p])) * kernel[...]
        waves[p] = dot3(unmix, split_value(spectrum))
    carried = None
    for r in range(GROUP):
        mine = jnp.concatenate(
            [waves[p, r * rows : (r + 1) * rows, :] for p in range(pairs)], axis=0
        )
        wide = dot3(split_value(mine), (back_hi[r], back_lo[r]))
        first = wide[:, :LANES] if carried is None else wide[:, :LANES] + carried
        carried = wide[:, LANES:]
        result[pl.ds(r, pairs * rows, stride=LINES), :] = first
    result[pl.ds(GROUP, pairs * rows, stride=LINES), :] = carried
    for k in range(planes):
        slab = partner(me, k, planes) * lines
        for p in range(pairs):
            outs[k][pl.ds(p * lines, lines), :] = result[pl.ds(p * whole + slab, lines), :]


def params():
    return pltpu.CompilerParams(vmem_limit_bytes=VMEM_LIMIT)


def floats(rows):
    return jax.ShapeDtypeStruct((rows, LANES), jnp.float32)


def partner(i, k, size):
    return i ^ k if size & (size - 1) == 0 else (k - i) % size


def exchange(parts, size):
    return [parts[0] if size & (size - 1) == 0 else lax.ppermute(parts[0], "plane", pairs_of(0, size))] + [
        lax.ppermute(parts[k], "plane", pairs_of(k, size)) for k in range(1, size)
    ]


def pairs_of(k, size):
    return [(i, partner(i, k, size)) for i in range(size)]


def local(orbitals, kernel_half, pair_own, pair_step, pair_remote, pair_count):
    planes = lax.axis_size("plane")
    blocks = lax.axis_size("blk")
    orbs, depth, cell_count = orbitals.shape
    slots = pair_own.shape[0]
    lines = cell_count // LANES
    each = slots // planes
    x_local = NG // planes
    flat = orbitals.reshape(orbs * lines, LANES)

    request, place = pl.pallas_call(
        functools.partial(plan_kernel, slots, orbs, planes),
        out_shape=(
            jax.ShapeDtypeStruct((STEPS * slots + STEPS,), jnp.int32),
            jax.ShapeDtypeStruct((3 * slots,), jnp.int32),
        ),
        in_specs=[smem] * 4,
        out_specs=(smem, smem),
        scratch_shapes=[
            pltpu.SMEM((STEPS * orbs,), jnp.int32),
            pltpu.SMEM((3 * slots,), jnp.int32),
        ],
        name="plan",
    )(pair_own, pair_step, pair_remote, pair_count)

    everyone = lax.all_gather(request, ("groups", "blk"))
    largest = jnp.max(everyone[:, STEPS * slots :])
    group = lax.axis_index("groups")
    block = lax.axis_index("blk")
    wanted = jnp.stack(
        [
            lax.dynamic_slice(
                everyone,
                (group * blocks + (block + s + 1) % blocks, s * slots),
                (1, slots),
            )[0]
            for s in range(STEPS)
        ]
    )

    half = kernel_half[0]
    tall = jnp.concatenate([half, half[1 : NG // 2][::-1]], axis=0)
    kernel = jnp.concatenate([tall, tall[:, 1 : NG // 2][:, ::-1]], axis=1) / float(NG * NG)
    tables = [jnp.asarray(part) for pair in make_tables(x_local) for part in pair]

    def run(capacity, flat, wanted, place, kernel, *tables):
        sends = pl.pallas_call(
            functools.partial(pack_kernel, capacity, slots, lines),
            out_shape=[floats(capacity * lines)] * STEPS,
            in_specs=[smem, vmem],
            out_specs=[vmem] * STEPS,
            compiler_params=params(),
            name="pack",
        )(wanted, flat)
        received = [
            lax.ppermute(
                sends[s], "blk", [(i, (i + s + 1) % blocks) for i in range(blocks)]
            )
            for s in range(STEPS)
        ]
        held = [
            pltpu.VMEM((STEPS * capacity * lines, LANES), jnp.float32),
            pltpu.SemaphoreType.DMA((STEPS,)),
        ]
        parts = pl.pallas_call(
            functools.partial(density_kernel, capacity, slots, lines, planes),
            out_shape=[floats(each * lines)] * planes,
            in_specs=[smem, vmem] + [hbm] * STEPS,
            out_specs=[vmem] * planes,
            scratch_shapes=held,
            compiler_params=params(),
            name="density",
        )(place, flat, *received)
        columns = exchange(parts, planes)
        backs = pl.pallas_call(
            functools.partial(transform_kernel, each, lines, planes),
            out_shape=[floats(each * lines)] * planes,
            in_specs=[vmem] * (planes + 9),
            out_specs=[vmem] * planes,
            scratch_shapes=[
                pltpu.VMEM((each * planes * lines, LANES), jnp.float32),
                pltpu.VMEM((each, NG, NG), jnp.float32),
                pltpu.VMEM((each * planes * lines, LANES), jnp.float32),
            ],
            compiler_params=params(),
            name="transform",
        )(*columns, *tables, kernel)
        potentials = exchange(backs, planes)
        return pl.pallas_call(
            functools.partial(sum_kernel, capacity, slots, lines, planes),
            out_shape=floats(orbs * lines),
            in_specs=[smem] + [hbm] * STEPS + [vmem] * planes,
            out_specs=vmem,
            scratch_shapes=held,
            compiler_params=params(),
            name="sum",
        )(place, *received, *potentials)

    sizes = [c for c in CAPACITIES if c < slots] + [slots]
    choice = sum((largest > c).astype(jnp.int32) for c in sizes[:-1])
    summed = lax.switch(
        choice,
        [functools.partial(run, c) for c in sizes],
        flat,
        wanted,
        place,
        kernel,
        *tables,
    )
    return summed.reshape(orbs, depth, cell_count)


def solution(mesh):
    in_specs = (
        P(("groups", "blk"), None, "plane"),
        P(),
        P(("groups", "blk")),
        P(("groups", "blk")),
        P(("groups", "blk")),
        P(("groups", "blk")),
    )
    out_specs = P(("groups", "blk"), None, "plane")
    return jax.shard_map(local, mesh=mesh, in_specs=in_specs, out_specs=out_specs, check_vma=False)
```

```python
import functools

import jax
import jax.numpy as jnp
import ml_dtypes
import numpy as np
from jax import lax
from jax.experimental import pallas as pl
from jax.experimental.pallas import tpu as pltpu
from jax.sharding import PartitionSpec as P

NG = 160
STEPS = 3
LANES = 128
GROUP = 4
LINES = 5
BOUNDS = ((6, 11, 16), (7, 13, 18), (8, 14, 20), (9, 16, 22), (10, 18, 26))
SHARES = (5, 4, 3)

VMEM_LIMIT = 48 * 1024 * 1024
highest = lax.Precision.HIGHEST
smem = pl.BlockSpec(memory_space=pltpu.SMEM)
vmem = pl.BlockSpec(memory_space=pltpu.VMEM)
hbm = pl.BlockSpec(memory_space=pl.ANY)


def split_table(table):
    high = table.astype(ml_dtypes.bfloat16)
    low = (table - high.astype(np.float64)).astype(ml_dtypes.bfloat16)
    return high, low


def make_tables(x_local):
    positions = np.arange(NG)
    angles = 2.0 * np.pi / NG * (positions[:, None] * positions[None, :] % NG)
    cas = np.cos(angles) + np.sin(angles)
    into = np.zeros((GROUP, 2 * LANES, NG))
    for r in range(GROUP):
        start = r * NG - r * LANES
        into[r, start : start + NG] = cas
    back = np.transpose(into, (0, 2, 1)).copy()
    order = np.arange(NG).reshape(NG // GROUP, GROUP).T.reshape(-1)
    mixed = cas[:, order]
    return split_table(into), split_table(back), split_table(mixed), split_table(mixed.T.copy())


def split_value(value):
    high = value.astype(jnp.bfloat16)
    low = (value - high.astype(jnp.float32)).astype(jnp.bfloat16)
    return high, low


def dot(a, b):
    return lax.dot_general(a, b, (((1,), (0,)), ((), ())), preferred_element_type=jnp.float32)


def dot3(a, b):
    return dot(a[0], b[0]) + (dot(a[0], b[1]) + dot(a[1], b[0]))


def plan_kernel(slots, orbs, choices, own, step, remote, count, half, request, known, full, seen, hist):
    for s in range(STEPS):
        for k in range(slots):
            request[s * slots + k] = 0
        hist[slots + s] = 0
        for k in range(orbs):
            seen[s * orbs + k] = -1
    for k in range(slots):
        hist[k] = 0

    def visit(j, carry):
        live = j < count[0]
        s = jnp.where(live, step[j], 0)
        k = remote[j]
        at = seen[s * orbs + k]
        used = hist[slots + s]
        rank = jnp.where(at < 0, used, at)

        @pl.when(live & (at < 0))
        def _():
            request[s * slots + used] = k
            seen[s * orbs + k] = used
            hist[slots + s] = used + 1

        @pl.when(live)
        def _():
            hist[rank] += 1

        known[j] = s
        known[slots + j] = jnp.where(live, rank, 0)
        known[2 * slots + j] = jnp.where(live, own[j], -1)
        return carry

    lax.fori_loop(0, slots, visit, 0)
    beyond = [jnp.int32(0)]
    for k in reversed(range(slots)):
        beyond.append(beyond[-1] + hist[k])
    beyond = beyond[::-1]
    choice = jnp.int32(len(choices) - 1)
    for i in reversed(range(len(choices) - 1)):
        bounds, sizes = choices[i]
        fits = beyond[bounds[-1]] == 0
        for c in range(1, len(bounds)):
            fits = fits & (beyond[bounds[c - 1]] <= sum(sizes[c:]))
        choice = jnp.where(fits, i, choice)
    request[STEPS * slots] = choice

    rows, columns = full.shape[0], half.shape[0]
    place = lax.broadcasted_iota(jnp.int32, (rows, columns), 0)
    folded = jnp.minimum(place, rows - place)
    picker = (folded == lax.broadcasted_iota(jnp.int32, (rows, columns), 1)).astype(jnp.float32)
    tall = lax.dot_general(
        picker,
        half[...],
        (((1,), (0,)), ((), ())),
        precision=highest,
        preferred_element_type=jnp.float32,
    )
    full[...] = lax.dot_general(
        tall,
        picker,
        (((1,), (1,)), ((), ())),
        precision=highest,
        preferred_element_type=jnp.float32,
    ) * (1.0 / (NG * NG))


def place_kernel(slots, planes, bounds, sizes, known, place, order, start):
    chunks = len(bounds)
    for c in range(chunks):
        start[c] = 0

    def chunk_of(rank):
        return sum((rank >= b).astype(jnp.int32) for b in bounds[:-1])

    def tally(j, carry):
        chunk = chunk_of(known[slots + j])
        for c in range(1, chunks):
            start[c] += (chunk < c).astype(jnp.int32)
        return carry

    def visit(j, carry):
        chunk = chunk_of(known[slots + j])
        at = start[chunk]
        start[chunk] = at + 1
        order[at] = j
        return carry

    lax.fori_loop(0, slots, tally, 0)
    lax.fori_loop(0, slots, visit, 0)
    me = lax.axis_index("plane")
    base = 0
    for size in sizes:
        each = size // planes
        for k in range(planes):
            first = base + partner(me, k, planes) * each
            for q in range(each):
                j = order[first + q]
                to = base + k * each + q
                s, rank = known[j], known[slots + j]
                far = s * bounds[0] + rank
                for c in range(1, chunks):
                    before = STEPS * bounds[c - 1]
                    width = bounds[c] - bounds[c - 1]
                    far = jnp.where(
                        rank >= bounds[c - 1], before + s * width + rank - bounds[c - 1], far
                    )
                place[to] = far
                place[slots + to] = known[2 * slots + j]
        base += size


def pack_kernel(slots, lines, low, high, *refs):
    wanted, orbitals, sends = refs[:STEPS], refs[STEPS], refs[STEPS + 1 :]
    for s in range(STEPS):
        for c in range(low, high):
            row = wanted[s][s * slots + c]
            sends[s][pl.ds((c - low) * lines, lines), :] = orbitals[pl.ds(row * lines, lines), :]


def density_kernel(slots, lines, planes, bounds, chunk, base, size, place, orbitals, *refs):
    count = STEPS * (chunk + 1)
    received, parts = refs[:count], refs[count : count + planes]
    kept, held, sems = refs[count + planes :]
    copies = []
    at = 0
    for i in range(count):
        rows = received[i].shape[0]
        copies.append(
            pltpu.make_async_copy(received[i], held.at[pl.ds(at, rows), :], sems.at[i])
        )
        at += rows
    for copy in copies:
        copy.start()
    for copy in copies:
        copy.wait()
    each = size // planes
    for j in range(size):
        far = place[base + j] * lines
        near = jnp.maximum(place[slots + base + j], 0) * lines
        value = held[pl.ds(far, lines), :]
        kept[pl.ds(j * lines, lines), :] = value
        parts[j // each][pl.ds(j % each * lines, lines), :] = (
            orbitals[pl.ds(near, lines), :] * value
        )


def sum_kernel(slots, lines, planes, base, size, fresh, place, *refs):
    kept, parts = refs[0], refs[1 : 1 + planes]
    out = refs[-1]
    if fresh:
        out[...] = jnp.zeros_like(out)
    else:
        out[...] = refs[1 + planes][...]
    each = size // planes
    for j in range(size):
        near = place[slots + base + j] * lines

        @pl.when(near >= 0)
        def _():
            out[pl.ds(near, lines), :] += (
                parts[j // each][pl.ds(j % each * lines, lines), :]
                * kept[pl.ds(j * lines, lines), :]
            )


def transform_kernel(pairs, lines, planes, *refs):
    parts = refs[:planes]
    into_hi, into_lo, back_hi, back_lo, mix_hi, mix_lo, unmix_hi, unmix_lo, kernel = refs[
        planes : planes + 9
    ]
    outs = refs[planes + 9 : 2 * planes + 9]
    cells, waves, result = refs[2 * planes + 9 :]
    whole = planes * lines
    rows = NG // GROUP
    me = lax.axis_index("plane")
    for k in range(planes):
        slab = partner(me, k, planes) * lines
        for p in range(pairs):
            cells[pl.ds(p * whole + slab, lines), :] = parts[k][pl.ds(p * lines, lines), :]
    line = [split_value(cells[pl.ds(t, pairs * rows, stride=LINES), :]) for t in range(LINES)]
    for r in range(GROUP):
        wide = [jnp.concatenate([line[r][i], line[r + 1][i]], axis=1) for i in range(2)]
        found = dot3(wide, (into_hi[r], into_lo[r]))
        for p in range(pairs):
            waves[p, r * rows : (r + 1) * rows, :] = found[p * rows : (p + 1) * rows, :]
    mix = (mix_hi[...], mix_lo[...])
    unmix = (unmix_hi[...], unmix_lo[...])
    for p in range(pairs):
        spectrum = dot3(mix, split_value(waves[p])) * kernel[...]
        waves[p] = dot3(unmix, split_value(spectrum))
    carried = None
    for r in range(GROUP):
        mine = jnp.concatenate(
            [waves[p, r * rows : (r + 1) * rows, :] for p in range(pairs)], axis=0
        )
        wide = dot3(split_value(mine), (back_hi[r], back_lo[r]))
        first = wide[:, :LANES] if carried is None else wide[:, :LANES] + carried
        carried = wide[:, LANES:]
        result[pl.ds(r, pairs * rows, stride=LINES), :] = first
    result[pl.ds(GROUP, pairs * rows, stride=LINES), :] = carried
    for k in range(planes):
        slab = partner(me, k, planes) * lines
        for p in range(pairs):
            outs[k][pl.ds(p * lines, lines), :] = result[pl.ds(p * whole + slab, lines), :]


def choices_for(slots, planes):
    units = slots // planes
    cuts = [units * sum(SHARES[: i + 1]) // sum(SHARES) for i in range(len(SHARES))]
    sizes = tuple((b - a) * planes for a, b in zip([0] + cuts, cuts))
    listed = [(bounds, sizes) for bounds in BOUNDS if bounds[-1] < slots]
    return listed + [(tuple(cut * planes for cut in cuts), sizes)]


def params():
    return pltpu.CompilerParams(vmem_limit_bytes=VMEM_LIMIT)


def floats(rows):
    return jax.ShapeDtypeStruct((rows, LANES), jnp.float32)


def partner(i, k, size):
    return i ^ k if size & (size - 1) == 0 else (k - i) % size


def exchange(parts, size):
    return [parts[0] if size & (size - 1) == 0 else lax.ppermute(parts[0], "plane", pairs_of(0, size))] + [
        lax.ppermute(parts[k], "plane", pairs_of(k, size)) for k in range(1, size)
    ]


def pairs_of(k, size):
    return [(i, partner(i, k, size)) for i in range(size)]


def gather_requests(request, groups, blocks):
    if groups * blocks > 8:
        everyone = lax.all_gather(request, ("groups", "blk"))
        first = lax.axis_index("groups") * blocks
        block = lax.axis_index("blk")
        ahead = [
            lax.dynamic_index_in_dim(everyone, first + (block + s + 1) % blocks, 0, False)
            for s in range(STEPS)
        ]
        return ahead, jnp.max(everyone[:, -1])
    found = {(0, 0): request}
    for g in range(groups):
        for b in range(blocks):
            if (g, b) != (0, 0):
                route = [
                    (i * blocks + j, (i - g) % groups * blocks + (j - b) % blocks)
                    for i in range(groups)
                    for j in range(blocks)
                ]
                found[g, b] = lax.ppermute(request, ("groups", "blk"), route)
    ahead = [found[0, (s + 1) % blocks] for s in range(STEPS)]
    return ahead, functools.reduce(jnp.maximum, [v[-1] for v in found.values()])


def local(orbitals, kernel_half, pair_own, pair_step, pair_remote, pair_count):
    groups, blocks, planes = (lax.axis_size(name) for name in ("groups", "blk", "plane"))
    orbs, depth, cell_count = orbitals.shape
    slots = pair_own.shape[0]
    lines = cell_count // LANES
    flat = orbitals.reshape(orbs * lines, LANES)
    choices = choices_for(slots, planes)

    request, known, kernel = pl.pallas_call(
        functools.partial(plan_kernel, slots, orbs, choices),
        out_shape=(
            jax.ShapeDtypeStruct((STEPS * slots + 1,), jnp.int32),
            jax.ShapeDtypeStruct((3 * slots,), jnp.int32),
            jax.ShapeDtypeStruct((NG, NG), jnp.float32),
        ),
        in_specs=[smem] * 4 + [vmem],
        out_specs=(smem, smem, vmem),
        scratch_shapes=[
            pltpu.SMEM((STEPS * orbs,), jnp.int32),
            pltpu.SMEM((slots + STEPS,), jnp.int32),
        ],
        name="plan",
    )(pair_own, pair_step, pair_remote, pair_count, kernel_half[0])

    ahead, choice = gather_requests(request, groups, blocks)
    tables = [jnp.asarray(part) for pair in make_tables(NG // planes) for part in pair]

    def run(bounds, sizes, flat, ahead, known, kernel, *tables):
        chunks = len(bounds)
        received = []
        for c in range(chunks):
            low, high = (bounds[c - 1] if c else 0), bounds[c]
            sends = pl.pallas_call(
                functools.partial(pack_kernel, slots, lines, low, high),
                out_shape=[floats((high - low) * lines)] * STEPS,
                in_specs=[smem] * STEPS + [vmem],
                out_specs=[vmem] * STEPS,
                compiler_params=params(),
                name="pack",
            )(*ahead, flat)
            for s in range(STEPS):
                route = [(i, (i + s + 1) % blocks) for i in range(blocks)]
                received.append(lax.ppermute(sends[s], "blk", route))
        place = pl.pallas_call(
            functools.partial(place_kernel, slots, planes, bounds, sizes),
            out_shape=jax.ShapeDtypeStruct((2 * slots,), jnp.int32),
            in_specs=[smem],
            out_specs=smem,
            scratch_shapes=[pltpu.SMEM((slots,), jnp.int32), pltpu.SMEM((chunks,), jnp.int32)],
            name="place",
        )(known)
        base = 0
        summed = None
        for c in range(chunks):
            size = sizes[c]
            each = size // planes
            count = STEPS * (c + 1)
            *parts, kept = pl.pallas_call(
                functools.partial(density_kernel, slots, lines, planes, bounds, c, base, size),
                out_shape=[floats(each * lines)] * planes + [floats(size * lines)],
                in_specs=[smem, vmem] + [hbm] * count,
                out_specs=[vmem] * (planes + 1),
                scratch_shapes=[
                    pltpu.VMEM((STEPS * bounds[c] * lines, LANES), jnp.float32),
                    pltpu.SemaphoreType.DMA((count,)),
                ],
                compiler_params=params(),
                name="density",
            )(place, flat, *received[:count])
            columns = exchange(parts, planes)
            backs = pl.pallas_call(
                functools.partial(transform_kernel, each, lines, planes),
                out_shape=[floats(each * lines)] * planes,
                in_specs=[vmem] * (planes + 9),
                out_specs=[vmem] * planes,
                scratch_shapes=[
                    pltpu.VMEM((each * planes * lines, LANES), jnp.float32),
                    pltpu.VMEM((each, NG, NG), jnp.float32),
                    pltpu.VMEM((each * planes * lines, LANES), jnp.float32),
                ],
                compiler_params=params(),
                name="transform",
            )(*columns, *tables, kernel)
            potentials = exchange(backs, planes)
            before = [] if summed is None else [summed]
            summed = pl.pallas_call(
                functools.partial(sum_kernel, slots, lines, planes, base, size, not before),
                out_shape=floats(orbs * lines),
                in_specs=[smem] + [vmem] * (planes + 1 + len(before)),
                out_specs=vmem,
                compiler_params=params(),
                name="sum",
            )(place, kept, *potentials, *before)
            base += size
        return summed

    summed = lax.switch(
        choice,
        [functools.partial(run, *choice) for choice in choices],
        flat,
        ahead,
        known,
        kernel,
        *tables,
    )
    return summed.reshape(orbs, depth, cell_count)


def solution(mesh):
    in_specs = (
        P(("groups", "blk"), None, "plane"),
        P(),
        P(("groups", "blk")),
        P(("groups", "blk")),
        P(("groups", "blk")),
        P(("groups", "blk")),
    )
    out_specs = P(("groups", "blk"), None, "plane")
    return jax.shard_map(local, mesh=mesh, in_specs=in_specs, out_specs=out_specs, check_vma=False)
```

```python
import functools

import jax
import jax.numpy as jnp
import ml_dtypes
import numpy as np
from jax import lax
from jax.experimental import pallas as pl
from jax.experimental.pallas import tpu as pltpu
from jax.sharding import PartitionSpec as P

NG = 160
STEPS = 3
LANES = 128
GROUP = 4
LINES = 5
FIRST = (8, 16)
EXTRAS = (0, 2, 4, 6, 8)
SHARES = (6, 3, 3)

VMEM_LIMIT = 48 * 1024 * 1024
highest = lax.Precision.HIGHEST
smem = pl.BlockSpec(memory_space=pltpu.SMEM)
vmem = pl.BlockSpec(memory_space=pltpu.VMEM)
hbm = pl.BlockSpec(memory_space=pl.ANY)


def split_table(table):
    high = table.astype(ml_dtypes.bfloat16)
    low = (table - high.astype(np.float64)).astype(ml_dtypes.bfloat16)
    return high, low


def make_tables(x_local):
    positions = np.arange(NG)
    angles = 2.0 * np.pi / NG * (positions[:, None] * positions[None, :] % NG)
    cas = np.cos(angles) + np.sin(angles)
    into = np.zeros((GROUP, 2 * LANES, NG))
    for r in range(GROUP):
        start = r * NG - r * LANES
        into[r, start : start + NG] = cas
    back = np.transpose(into, (0, 2, 1)).copy()
    order = np.arange(NG).reshape(NG // GROUP, GROUP).T.reshape(-1)
    mixed = cas[:, order]
    return split_table(into), split_table(back), split_table(mixed), split_table(mixed.T.copy())


def split_value(value):
    high = value.astype(jnp.bfloat16)
    low = (value - high.astype(jnp.float32)).astype(jnp.bfloat16)
    return high, low


def dot(a, b):
    return lax.dot_general(a, b, (((1,), (0,)), ((), ())), preferred_element_type=jnp.float32)


def dot3(a, b):
    return dot(a[0], b[0]) + (dot(a[0], b[1]) + dot(a[1], b[0]))


def plan_kernel(slots, orbs, shares, own, step, remote, count, request, known, choice, seen, hist):
    for s in range(STEPS):
        for k in range(slots):
            request[s * slots + k] = 0
        hist[slots + s] = 0
        for k in range(orbs):
            seen[s * orbs + k] = -1
    for k in range(slots):
        hist[k] = 0

    def visit(j, carry):
        live = j < count[0]
        s = jnp.where(live, step[j], 0)
        k = remote[j]
        at = seen[s * orbs + k]
        used = hist[slots + s]
        rank = jnp.where(at < 0, used, at)

        @pl.when(live & (at < 0))
        def _():
            request[s * slots + used] = k
            seen[s * orbs + k] = used
            hist[slots + s] = used + 1

        @pl.when(live)
        def _():
            hist[rank] += 1

        known[j] = s
        known[slots + j] = jnp.where(live, rank, 0)
        known[2 * slots + j] = jnp.where(live, own[j], -1)
        return carry

    lax.fori_loop(0, slots, visit, 0)
    beyond = [jnp.int32(0)]
    for k in reversed(range(slots)):
        beyond.append(beyond[-1] + hist[k])
    beyond = beyond[::-1]
    fits = beyond[EXTRAS[-1] + FIRST[-1]] == 0
    for c, bound in enumerate(FIRST):
        fits = fits & (beyond[bound] <= sum(shares[c + 1 :]))
    least = sum((beyond[FIRST[-1] + extra] > 0).astype(jnp.int32) for extra in EXTRAS[:-1])
    choice[0] = jnp.where(fits, least, len(EXTRAS))


def expand_kernel(half, full):
    rows, columns = full.shape[0], half.shape[1]
    place = lax.broadcasted_iota(jnp.int32, (rows, columns), 0)
    folded = jnp.minimum(place, rows - place)
    picker = (folded == lax.broadcasted_iota(jnp.int32, (rows, columns), 1)).astype(jnp.float32)
    tall = lax.dot_general(
        picker,
        half[0],
        (((1,), (0,)), ((), ())),
        precision=highest,
        preferred_element_type=jnp.float32,
    )
    full[...] = lax.dot_general(
        tall,
        picker,
        (((1,), (1,)), ((), ())),
        precision=highest,
        preferred_element_type=jnp.float32,
    ) * (1.0 / (NG * NG))


def place_kernel(slots, planes, shares, known, place, order, start):
    chunks = len(shares)
    for c in range(chunks):
        start[c] = 0

    def chunk_of(rank):
        return sum((rank >= b).astype(jnp.int32) for b in FIRST)

    def tally(j, carry):
        chunk = chunk_of(known[slots + j])
        return tuple(
            at + (chunk < c + 1).astype(jnp.int32) for c, at in enumerate(carry)
        )

    def visit(j, carry):
        chunk = chunk_of(known[slots + j])
        at = start[chunk]
        start[chunk] = at + 1
        order[at] = j
        return carry

    counts = lax.fori_loop(0, slots, tally, (jnp.int32(0),) * (chunks - 1))
    for c in range(1, chunks):
        start[c] = counts[c - 1]
    lax.fori_loop(0, slots, visit, 0)
    me = lax.axis_index("plane")
    base = 0
    for size in shares:
        each = size // planes
        for k in range(planes):
            first = base + partner(me, k, planes) * each
            for q in range(each):
                j = order[first + q]
                to = base + k * each + q
                for part in range(3):
                    place[part * slots + to] = known[part * slots + j]
        base += size


def pack_kernel(slots, lines, low, high, which, wanted, orbitals, *refs):
    send = refs[-1]
    for c in range(low, high):
        row = wanted[which * slots + c]
        send[pl.ds((c - low) * lines, lines), :] = orbitals[pl.ds(row * lines, lines), :]


def density_kernel(slots, lines, planes, bounds, base, size, place, orbitals, *refs):
    count = STEPS * len(bounds)
    received, parts = refs[:count], refs[count : count + planes]
    kept, held, sems = refs[count + planes :]
    copies = []
    at = 0
    for i in range(count):
        rows = received[i].shape[0]
        copies.append(
            pltpu.make_async_copy(received[i], held.at[pl.ds(at, rows), :], sems.at[i])
        )
        at += rows
    for copy in copies:
        copy.start()
    for copy in copies:
        copy.wait()
    each = size // planes
    for j in range(size):
        s, rank = place[base + j], place[slots + base + j]
        far = s * bounds[0] + rank
        for low, high in zip(bounds, bounds[1:]):
            far = jnp.where(rank >= low, STEPS * low + s * (high - low) + rank - low, far)
        far = jnp.minimum(far, STEPS * bounds[-1] - 1) * lines
        near = jnp.maximum(place[2 * slots + base + j], 0) * lines
        value = held[pl.ds(far, lines), :]
        kept[pl.ds(j * lines, lines), :] = value
        parts[j // each][pl.ds(j % each * lines, lines), :] = (
            orbitals[pl.ds(near, lines), :] * value
        )


def sum_kernel(slots, lines, planes, base, size, fresh, place, *refs):
    kept, parts = refs[0], refs[1 : 1 + planes]
    out = refs[-1]
    if fresh:
        out[...] = jnp.zeros_like(out)
    else:
        out[...] = refs[1 + planes][...]
    each = size // planes
    for j in range(size):
        near = place[2 * slots + base + j] * lines

        @pl.when(near >= 0)
        def _():
            out[pl.ds(near, lines), :] += (
                parts[j // each][pl.ds(j % each * lines, lines), :]
                * kept[pl.ds(j * lines, lines), :]
            )


def transform_kernel(pairs, lines, planes, *refs):
    parts = refs[:planes]
    into_hi, into_lo, back_hi, back_lo, mix_hi, mix_lo, unmix_hi, unmix_lo, kernel = refs[
        planes : planes + 9
    ]
    outs = refs[planes + 9 : 2 * planes + 9]
    cells, waves, result = refs[2 * planes + 9 :]
    whole = planes * lines
    rows = NG // GROUP
    me = lax.axis_index("plane")
    for k in range(planes):
        slab = partner(me, k, planes) * lines
        for p in range(pairs):
            cells[pl.ds(p * whole + slab, lines), :] = parts[k][pl.ds(p * lines, lines), :]
    line = [split_value(cells[pl.ds(t, pairs * rows, stride=LINES), :]) for t in range(LINES)]
    for r in range(GROUP):
        wide = [jnp.concatenate([line[r][i], line[r + 1][i]], axis=1) for i in range(2)]
        found = dot3(wide, (into_hi[r], into_lo[r]))
        for p in range(pairs):
            waves[p, r * rows : (r + 1) * rows, :] = found[p * rows : (p + 1) * rows, :]
    mix = (mix_hi[...], mix_lo[...])
    unmix = (unmix_hi[...], unmix_lo[...])
    for p in range(pairs):
        spectrum = dot3(mix, split_value(waves[p])) * kernel[...]
        waves[p] = dot3(unmix, split_value(spectrum))
    carried = None
    for r in range(GROUP):
        mine = jnp.concatenate(
            [waves[p, r * rows : (r + 1) * rows, :] for p in range(pairs)], axis=0
        )
        wide = dot3(split_value(mine), (back_hi[r], back_lo[r]))
        first = wide[:, :LANES] if carried is None else wide[:, :LANES] + carried
        carried = wide[:, LANES:]
        result[pl.ds(r, pairs * rows, stride=LINES), :] = first
    result[pl.ds(GROUP, pairs * rows, stride=LINES), :] = carried
    for k in range(planes):
        slab = partner(me, k, planes) * lines
        for p in range(pairs):
            outs[k][pl.ds(p * lines, lines), :] = result[pl.ds(p * whole + slab, lines), :]


def shares_for(slots, planes):
    units = slots // planes
    cuts = [units * sum(SHARES[: i + 1]) // sum(SHARES) for i in range(len(SHARES))]
    return tuple((b - a) * planes for a, b in zip([0] + cuts, cuts))


def params():
    return pltpu.CompilerParams(vmem_limit_bytes=VMEM_LIMIT)


def floats(rows):
    return jax.ShapeDtypeStruct((rows, LANES), jnp.float32)


def partner(i, k, size):
    return i ^ k if size & (size - 1) == 0 else (k - i) % size


def exchange(parts, size):
    return [parts[0] if size & (size - 1) == 0 else lax.ppermute(parts[0], "plane", pairs_of(0, size))] + [
        lax.ppermute(parts[k], "plane", pairs_of(k, size)) for k in range(1, size)
    ]


def pairs_of(k, size):
    return [(i, partner(i, k, size)) for i in range(size)]


def local(orbitals, kernel_half, pair_own, pair_step, pair_remote, pair_count):
    blocks, planes = lax.axis_size("blk"), lax.axis_size("plane")
    orbs, depth, cell_count = orbitals.shape
    slots = pair_own.shape[0]
    lines = cell_count // LANES
    flat = orbitals.reshape(orbs * lines, LANES)
    shares = shares_for(slots, planes)

    request, known, choice = pl.pallas_call(
        functools.partial(plan_kernel, slots, orbs, shares),
        out_shape=(
            jax.ShapeDtypeStruct((STEPS * slots,), jnp.int32),
            jax.ShapeDtypeStruct((3 * slots,), jnp.int32),
            jax.ShapeDtypeStruct((1,), jnp.int32),
        ),
        in_specs=[smem] * 4,
        out_specs=(smem, smem, smem),
        scratch_shapes=[
            pltpu.SMEM((STEPS * orbs,), jnp.int32),
            pltpu.SMEM((slots + STEPS,), jnp.int32),
        ],
        name="plan",
    )(pair_own, pair_step, pair_remote, pair_count)

    def route(shift):
        return [(i, (i + shift) % blocks) for i in range(blocks)]

    ahead = [lax.ppermute(request, "blk", route(-s - 1)) for s in range(STEPS)]

    def pack(which, low, high, wanted, flat, *after):
        return pl.pallas_call(
            functools.partial(pack_kernel, slots, lines, low, high, which),
            out_shape=floats((high - low) * lines),
            in_specs=[smem, vmem] + [hbm] * len(after),
            out_specs=vmem,
            compiler_params=params(),
            name="pack",
        )(wanted, flat, *after)

    def send(low, high, flat, ahead, before):
        return [
            lax.ppermute(
                pack(s, low, high, ahead[s], flat, *before[s : s + 1]), "blk", route(s + 1)
            )
            for s in range(STEPS)
        ]

    def make_density(bounds, base, size, place, flat, received):
        each = size // planes
        return pl.pallas_call(
            functools.partial(density_kernel, slots, lines, planes, bounds, base, size),
            out_shape=[floats(each * lines)] * planes + [floats(size * lines)],
            in_specs=[smem, vmem] + [hbm] * len(received),
            out_specs=[vmem] * (planes + 1),
            scratch_shapes=[
                pltpu.VMEM((STEPS * bounds[-1] * lines, LANES), jnp.float32),
                pltpu.SemaphoreType.DMA((len(received),)),
            ],
            compiler_params=params(),
            name="density",
        )(place, flat, *received)

    def filter_parts(parts, kernel, tables):
        each = parts[0].shape[0] // lines
        backs = pl.pallas_call(
            functools.partial(transform_kernel, each, lines, planes),
            out_shape=[floats(each * lines)] * planes,
            in_specs=[vmem] * (planes + 9),
            out_specs=[vmem] * planes,
            scratch_shapes=[
                pltpu.VMEM((each * planes * lines, LANES), jnp.float32),
                pltpu.VMEM((each, NG, NG), jnp.float32),
                pltpu.VMEM((each * planes * lines, LANES), jnp.float32),
            ],
            compiler_params=params(),
            name="transform",
        )(*exchange(parts, planes), *tables, kernel)
        return exchange(backs, planes)

    def add_up(base, size, place, kept, potentials, before):
        return pl.pallas_call(
            functools.partial(sum_kernel, slots, lines, planes, base, size, not before),
            out_shape=floats(orbs * lines),
            in_specs=[smem] + [vmem] * (planes + 1 + len(before)),
            out_specs=vmem,
            compiler_params=params(),
            name="sum",
        )(place, kept, *potentials, *before)

    def one_chunk(bounds, c, place, flat, kernel, tables, received, before):
        base, size = sum(shares[:c]), shares[c]
        *parts, kept = make_density(bounds, base, size, place, flat, received)
        potentials = filter_parts(parts, kernel, tables)
        return add_up(base, size, place, kept, potentials, before)

    received = send(0, FIRST[0], flat, ahead, [])
    place = pl.pallas_call(
        functools.partial(place_kernel, slots, planes, shares),
        out_shape=jax.ShapeDtypeStruct((3 * slots,), jnp.int32),
        in_specs=[smem],
        out_specs=smem,
        scratch_shapes=[pltpu.SMEM((slots,), jnp.int32), pltpu.SMEM((len(shares),), jnp.int32)],
        name="place",
    )(known)
    kernel = pl.pallas_call(
        expand_kernel,
        out_shape=jax.ShapeDtypeStruct((NG, NG), jnp.float32),
        in_specs=[vmem],
        out_specs=vmem,
        name="expand",
    )(kernel_half)
    choice = lax.pmax(choice, ("groups", "blk"))[0]
    tables = [jnp.asarray(part) for pair in make_tables(NG // planes) for part in pair]

    summed = []
    for c in range(len(FIRST) - 1):
        later = send(FIRST[c], FIRST[c + 1], flat, ahead, received[-STEPS:])
        summed = [
            one_chunk(FIRST[: c + 1], c, place, flat, kernel, tables, received, summed)
        ]
        received = received + later

    def finish(extra, flat, ahead, known, place, kernel, tables, received, summed):
        c = len(FIRST) - 1
        bounds = FIRST
        if extra:
            bounds = FIRST + (FIRST[-1] + extra,)
            later = send(bounds[-2], bounds[-1], flat, ahead, received[-STEPS:])
        summed = one_chunk(FIRST, c, place, flat, kernel, tables, received, [summed])
        if extra:
            received = received + later
        return one_chunk(bounds, c + 1, place, flat, kernel, tables, received, [summed])

    def general(flat, ahead, known, place, kernel, tables, received, summed):
        received = send(0, slots, flat, ahead, [])
        total = []
        for c in range(len(shares)):
            total = [one_chunk((slots,), c, place, flat, kernel, tables, received, total)]
        return total[0]

    summed = lax.switch(
        choice,
        [functools.partial(finish, extra) for extra in EXTRAS] + [general],
        flat,
        ahead,
        known,
        place,
        kernel,
        tables,
        received,
        summed[0],
    )
    return summed.reshape(orbs, depth, cell_count)


def solution(mesh):
    in_specs = (
        P(("groups", "blk"), None, "plane"),
        P(),
        P(("groups", "blk")),
        P(("groups", "blk")),
        P(("groups", "blk")),
        P(("groups", "blk")),
    )
    out_specs = P(("groups", "blk"), None, "plane")
    return jax.shard_map(local, mesh=mesh, in_specs=in_specs, out_specs=out_specs, check_vma=False)
```

```python
import functools

import jax
import jax.numpy as jnp
import ml_dtypes
import numpy as np
from jax import lax
from jax.experimental import pallas as pl
from jax.experimental.pallas import tpu as pltpu
from jax.sharding import PartitionSpec as P

NG = 160
STEPS = 3
LANES = 128
GROUP = 4
LINES = 5
FIRST = 9
TOTALS = (16, 18, 20, 23)
EARLY = (3, 3)
LATE = (3, 3)

VMEM_LIMIT = 48 * 1024 * 1024
highest = lax.Precision.HIGHEST
smem = pl.BlockSpec(memory_space=pltpu.SMEM)
vmem = pl.BlockSpec(memory_space=pltpu.VMEM)
hbm = pl.BlockSpec(memory_space=pl.ANY)


def split_table(table):
    high = table.astype(ml_dtypes.bfloat16)
    low = (table - high.astype(np.float64)).astype(ml_dtypes.bfloat16)
    return high, low


def make_tables(x_local):
    positions = np.arange(NG)
    angles = 2.0 * np.pi / NG * (positions[:, None] * positions[None, :] % NG)
    cas = np.cos(angles) + np.sin(angles)
    into = np.zeros((GROUP, 2 * LANES, NG))
    for r in range(GROUP):
        start = r * NG - r * LANES
        into[r, start : start + NG] = cas
    back = np.transpose(into, (0, 2, 1)).copy()
    order = np.arange(NG).reshape(NG // GROUP, GROUP).T.reshape(-1)
    mixed = cas[:, order]
    return split_table(into), split_table(back), split_table(mixed), split_table(mixed.T.copy())


def split_value(value):
    high = value.astype(jnp.bfloat16)
    low = (value - high.astype(jnp.float32)).astype(jnp.bfloat16)
    return high, low


def dot(a, b):
    return lax.dot_general(a, b, (((1,), (0,)), ((), ())), preferred_element_type=jnp.float32)


def dot3(a, b):
    return dot(a[0], b[0]) + (dot(a[0], b[1]) + dot(a[1], b[0]))


def is_ring(blocks):
    return blocks == STEPS + 1


def slot_ahead(s, blocks):
    return (lax.axis_index("blk") + 1 + s) % blocks if is_ring(blocks) else s


def slot_behind(s, blocks):
    return (lax.axis_index("blk") + blocks - 1 - s) % blocks if is_ring(blocks) else s


def spread(array, blocks, sign):
    if is_ring(blocks):
        return lax.all_to_all(array, "blk", 0, 0, tiled=True)
    rows = array.shape[0] // STEPS
    return jnp.concatenate(
        [
            lax.ppermute(
                array[s * rows : (s + 1) * rows],
                "blk",
                [(i, (i + sign * (s + 1)) % blocks) for i in range(blocks)],
            )
            for s in range(STEPS)
        ]
    )


def shares_of(blocks):
    return blocks if is_ring(blocks) else STEPS


def share_lines(rows, lines):
    return -(-rows * lines // 8) * 8


def plan_kernel(slots, orbs, blocks, late, own, step, remote, count, request, known, choice, seen, hist):
    for s in range(shares_of(blocks)):
        for k in range(slots):
            request[s, k] = 0
    for s in range(STEPS):
        hist[slots + s] = 0
        for k in range(orbs):
            seen[s * orbs + k] = -1
    for k in range(slots):
        hist[k] = 0

    def visit(j, carry):
        live = j < count[0]
        s = jnp.where(live, step[j], 0)
        k = remote[j]
        at = seen[s * orbs + k]
        used = hist[slots + s]
        rank = jnp.where(at < 0, used, at)

        @pl.when(live & (at < 0))
        def _():
            request[slot_behind(s, blocks), used] = k
            seen[s * orbs + k] = used
            hist[slots + s] = used + 1

        @pl.when(live)
        def _():
            hist[rank] += 1

        known[j] = slot_behind(s, blocks)
        known[slots + j] = jnp.where(live, rank, 0)
        known[2 * slots + j] = jnp.where(live, own[j], -1)
        return carry

    lax.fori_loop(0, slots, visit, 0)
    beyond = [jnp.int32(0)]
    for k in reversed(range(slots)):
        beyond.append(beyond[-1] + hist[k])
    beyond = beyond[::-1]
    fits = (beyond[FIRST] <= late) & (beyond[TOTALS[-1]] == 0)
    least = sum((beyond[total] > 0).astype(jnp.int32) for total in TOTALS[:-1])
    choice[0] = jnp.where(fits, least, len(TOTALS))


def expand_kernel(half, full):
    rows, columns = full.shape[0], half.shape[1]
    place = lax.broadcasted_iota(jnp.int32, (rows, columns), 0)
    folded = jnp.minimum(place, rows - place)
    picker = (folded == lax.broadcasted_iota(jnp.int32, (rows, columns), 1)).astype(jnp.float32)
    tall = lax.dot_general(
        picker,
        half[0],
        (((1,), (0,)), ((), ())),
        precision=highest,
        preferred_element_type=jnp.float32,
    )
    full[...] = lax.dot_general(
        tall,
        picker,
        (((1,), (1,)), ((), ())),
        precision=highest,
        preferred_element_type=jnp.float32,
    ) * (1.0 / (NG * NG))


def place_kernel(slots, planes, shares, known, mine, *refs):
    place, choice, order, start = refs[-4:]
    choice[0] = mine[0]
    start[0] = 0

    def tally(j, count):
        return count + (known[slots + j] < FIRST).astype(jnp.int32)

    def visit(j, carry):
        chunk = (known[slots + j] >= FIRST).astype(jnp.int32)
        at = start[chunk]
        start[chunk] = at + 1
        order[at] = j
        return carry

    start[1] = lax.fori_loop(0, slots, tally, jnp.int32(0))
    lax.fori_loop(0, slots, visit, 0)
    me = lax.axis_index("plane")
    base = 0
    for size in shares:
        each = size // planes
        for k in range(planes):
            first = base + partner(me, k, planes) * each
            for q in range(each):
                j = order[first + q]
                to = base + k * each + q
                for part in range(3):
                    place[part * slots + to] = known[part * slots + j]
        base += size


def pack_kernel(lines, blocks, low, high, wanted, orbitals, sent):
    for s in range(STEPS):
        share = slot_ahead(s, blocks)
        for c in range(low, high):
            row = wanted[share, c] * lines
            to = share * share_lines(high - low, lines) + (c - low) * lines
            sent[pl.ds(to, lines), :] = orbitals[pl.ds(row, lines), :]
    if is_ring(blocks):
        here = lax.axis_index("blk") * share_lines(high - low, lines)
        sent[pl.ds(here, (high - low) * lines), :] = orbitals[: (high - low) * lines, :]


def density_kernel(slots, lines, planes, bounds, base, size, place, orbitals, *refs):
    received, parts, kept = refs[: len(bounds)], refs[-planes - 1 : -1], refs[-1]
    each = size // planes
    for j in range(size):
        share, rank = place[base + j], place[slots + base + j]
        for c, (low, high) in enumerate(zip((0,) + bounds, bounds)):
            row = jnp.clip(rank - low, 0, high - low - 1) * lines
            row += share * share_lines(high - low, lines)
            found = received[c][pl.ds(row, lines), :]
            value = found if c == 0 else jnp.where(rank >= low, found, value)
        near = jnp.maximum(place[2 * slots + base + j], 0) * lines
        kept[pl.ds(j * lines, lines), :] = value
        parts[j // each][pl.ds(j % each * lines, lines), :] = (
            orbitals[pl.ds(near, lines), :] * value
        )


def sum_kernel(slots, lines, planes, base, size, fresh, place, *refs):
    kept, parts = refs[0], refs[1 : 1 + planes]
    out = refs[-1]
    if fresh:
        out[...] = jnp.zeros_like(out)
    else:
        out[...] = refs[1 + planes][...]
    each = size // planes
    for j in range(size):
        near = place[2 * slots + base + j] * lines

        @pl.when(near >= 0)
        def _():
            out[pl.ds(near, lines), :] += (
                parts[j // each][pl.ds(j % each * lines, lines), :]
                * kept[pl.ds(j * lines, lines), :]
            )


def transform_kernel(pairs, lines, planes, *refs):
    parts = refs[:planes]
    into_hi, into_lo, back_hi, back_lo, mix_hi, mix_lo, unmix_hi, unmix_lo, kernel = refs[
        planes : planes + 9
    ]
    outs = refs[planes + 9 : 2 * planes + 9]
    cells, waves, result = refs[2 * planes + 9 :]
    whole = planes * lines
    rows = NG // GROUP
    me = lax.axis_index("plane")
    for k in range(planes):
        slab = partner(me, k, planes) * lines
        for p in range(pairs):
            cells[pl.ds(p * whole + slab, lines), :] = parts[k][pl.ds(p * lines, lines), :]
    line = [split_value(cells[pl.ds(t, pairs * rows, stride=LINES), :]) for t in range(LINES)]
    for r in range(GROUP):
        wide = [jnp.concatenate([line[r][i], line[r + 1][i]], axis=1) for i in range(2)]
        found = dot3(wide, (into_hi[r], into_lo[r]))
        for p in range(pairs):
            waves[p, r * rows : (r + 1) * rows, :] = found[p * rows : (p + 1) * rows, :]
    mix = (mix_hi[...], mix_lo[...])
    unmix = (unmix_hi[...], unmix_lo[...])
    for p in range(pairs):
        spectrum = dot3(mix, split_value(waves[p])) * kernel[...]
        waves[p] = dot3(unmix, split_value(spectrum))
    carried = None
    for r in range(GROUP):
        mine = jnp.concatenate(
            [waves[p, r * rows : (r + 1) * rows, :] for p in range(pairs)], axis=0
        )
        wide = dot3(split_value(mine), (back_hi[r], back_lo[r]))
        first = wide[:, :LANES] if carried is None else wide[:, :LANES] + carried
        carried = wide[:, LANES:]
        result[pl.ds(r, pairs * rows, stride=LINES), :] = first
    result[pl.ds(GROUP, pairs * rows, stride=LINES), :] = carried
    for k in range(planes):
        slab = partner(me, k, planes) * lines
        for p in range(pairs):
            outs[k][pl.ds(p * lines, lines), :] = result[pl.ds(p * whole + slab, lines), :]


def shares_for(slots, planes):
    shares = EARLY + LATE
    units = slots // planes
    cuts = [units * sum(shares[: i + 1]) // sum(shares) for i in range(len(shares))]
    sizes = [(b - a) * planes for a, b in zip([0] + cuts, cuts)]
    return sizes, sum(sizes[len(EARLY) :])


def params():
    return pltpu.CompilerParams(vmem_limit_bytes=VMEM_LIMIT)


def cost(microseconds, flops=0):
    moved = int(microseconds * 1e3)
    return pl.CostEstimate(flops=flops, bytes_accessed=moved, transcendentals=0)


def floats(rows):
    return jax.ShapeDtypeStruct((rows, LANES), jnp.float32)


def partner(i, k, size):
    return i ^ k if size & (size - 1) == 0 else (k - i) % size


def exchange(parts, size):
    return [parts[0] if size & (size - 1) == 0 else lax.ppermute(parts[0], "plane", pairs_of(0, size))] + [
        lax.ppermute(parts[k], "plane", pairs_of(k, size)) for k in range(1, size)
    ]


def pairs_of(k, size):
    return [(i, partner(i, k, size)) for i in range(size)]


def local(orbitals, kernel_half, pair_own, pair_step, pair_remote, pair_count):
    blocks, planes = lax.axis_size("blk"), lax.axis_size("plane")
    orbs, depth, cell_count = orbitals.shape
    slots = pair_own.shape[0]
    lines = cell_count // LANES
    flat = orbitals.reshape(orbs * lines, LANES)
    shares, late = shares_for(slots, planes)

    request, known, choice = pl.pallas_call(
        functools.partial(plan_kernel, slots, orbs, blocks, late),
        out_shape=(
            jax.ShapeDtypeStruct((shares_of(blocks), -(-slots // LANES) * LANES), jnp.int32),
            jax.ShapeDtypeStruct((3 * slots,), jnp.int32),
            jax.ShapeDtypeStruct((1,), jnp.int32),
        ),
        in_specs=[smem] * 4,
        out_specs=(smem, smem, smem),
        scratch_shapes=[
            pltpu.SMEM((STEPS * orbs,), jnp.int32),
            pltpu.SMEM((slots + STEPS,), jnp.int32),
        ],
        cost_estimate=cost(2.3),
        name="plan",
    )(pair_own, pair_step, pair_remote, pair_count)

    wanted = spread(request, blocks, -1)

    def send(low, high, flat, wanted):
        packed = pl.pallas_call(
            functools.partial(pack_kernel, lines, blocks, low, high),
            out_shape=floats(shares_of(blocks) * share_lines(high - low, lines)),
            in_specs=[smem, vmem],
            out_specs=vmem,
            compiler_params=params(),
            cost_estimate=cost(0.5),
            name="pack",
        )(wanted, flat)
        return packed, spread(packed, blocks, 1)

    def make_density(bounds, base, size, place, flat, received, after):
        each = size // planes
        return pl.pallas_call(
            functools.partial(density_kernel, slots, lines, planes, bounds, base, size),
            out_shape=[floats(each * lines)] * planes + [floats(size * lines)],
            in_specs=[smem, vmem] + [vmem] * len(received) + [hbm] * len(after),
            out_specs=[vmem] * (planes + 1),
            compiler_params=params(),
            cost_estimate=cost(0.05 * size),
            name="density",
        )(place, flat, *received, *after)

    def filter_parts(parts, kernel, tables):
        each = parts[0].shape[0] // lines
        backs = pl.pallas_call(
            functools.partial(transform_kernel, each, lines, planes),
            out_shape=[floats(each * lines)] * planes,
            in_specs=[vmem] * (planes + 9),
            out_specs=[vmem] * planes,
            scratch_shapes=[
                pltpu.VMEM((each * planes * lines, LANES), jnp.float32),
                pltpu.VMEM((each, NG, NG), jnp.float32),
                pltpu.VMEM((each * planes * lines, LANES), jnp.float32),
            ],
            compiler_params=params(),
            cost_estimate=cost(0.5 + 0.4 * each),
            name="transform",
        )(*exchange(parts, planes), *tables, kernel)
        return exchange(backs, planes)

    def add_up(base, size, place, kept, potentials, before):
        return pl.pallas_call(
            functools.partial(sum_kernel, slots, lines, planes, base, size, not before),
            out_shape=floats(orbs * lines),
            in_specs=[smem] + [vmem] * (planes + 1 + len(before)),
            out_specs=vmem,
            compiler_params=params(),
            cost_estimate=cost(0.9),
            name="sum",
        )(place, kept, *potentials, *before)

    def one_chunk(bounds, c, place, flat, kernel, tables, received, before, after=()):
        base, size = sum(shares[:c]), shares[c]
        *parts, kept = make_density(bounds, base, size, place, flat, received, after)
        potentials = filter_parts(parts, kernel, tables)
        return add_up(base, size, place, kept, potentials, before)

    packed, first = send(0, FIRST, flat, wanted)
    place, choice = pl.pallas_call(
        functools.partial(place_kernel, slots, planes, shares),
        out_shape=(
            jax.ShapeDtypeStruct((3 * slots,), jnp.int32),
            jax.ShapeDtypeStruct((1,), jnp.int32),
        ),
        in_specs=[smem, smem, hbm],
        out_specs=(smem, smem),
        scratch_shapes=[pltpu.SMEM((slots,), jnp.int32), pltpu.SMEM((2,), jnp.int32)],
        cost_estimate=cost(2.8),
        name="place",
    )(known, choice, packed)
    kernel = pl.pallas_call(
        expand_kernel,
        out_shape=jax.ShapeDtypeStruct((NG, NG), jnp.float32),
        in_specs=[vmem],
        out_specs=vmem,
        cost_estimate=cost(1.4),
        name="expand",
    )(kernel_half)
    choice = lax.pmax(choice, ("groups", "blk"))
    tables = [jnp.asarray(part) for pair in make_tables(NG // planes) for part in pair]

    def finish(total, flat, wanted, place, kernel, tables, first):
        packed, later = send(FIRST, total, flat, wanted)
        summed = []
        for c in range(len(shares)):
            early = c < len(EARLY)
            bounds = (FIRST,) if early else (FIRST, total)
            rows = [first] if early else [first, later]
            after = [packed] if early else []
            summed = [one_chunk(bounds, c, place, flat, kernel, tables, rows, summed, after)]
        return summed[0]

    def general(flat, wanted, place, kernel, tables, first):
        rows = [send(0, slots, flat, wanted)[1]]
        summed = []
        for c in range(len(shares)):
            summed = [one_chunk((slots,), c, place, flat, kernel, tables, rows, summed)]
        return summed[0]

    summed = lax.switch(
        choice[0],
        [functools.partial(finish, total) for total in TOTALS] + [general],
        flat,
        wanted,
        place,
        kernel,
        tables,
        first,
    )
    return summed.reshape(orbs, depth, cell_count)


def solution(mesh):
    in_specs = (
        P(("groups", "blk"), None, "plane"),
        P(),
        P(("groups", "blk")),
        P(("groups", "blk")),
        P(("groups", "blk")),
        P(("groups", "blk")),
    )
    out_specs = P(("groups", "blk"), None, "plane")
    return jax.shard_map(local, mesh=mesh, in_specs=in_specs, out_specs=out_specs, check_vma=False)
```

```python
import functools

import jax
import jax.numpy as jnp
import ml_dtypes
import numpy as np
from jax import lax
from jax.experimental import pallas as pl
from jax.experimental.pallas import tpu as pltpu
from jax.sharding import PartitionSpec as P

NG = 160
STEPS = 3
LANES = 128
GROUP = 4
LINES = 5
FIRST = 9
TOTALS = (16, 18, 20, 23)
EARLY = (3, 3)
LATE = (3, 3)

VMEM_LIMIT = 48 * 1024 * 1024
highest = lax.Precision.HIGHEST
smem = pl.BlockSpec(memory_space=pltpu.SMEM)
vmem = pl.BlockSpec(memory_space=pltpu.VMEM)
hbm = pl.BlockSpec(memory_space=pl.ANY)


def split_table(table):
    high = table.astype(ml_dtypes.bfloat16)
    low = (table - high.astype(np.float64)).astype(ml_dtypes.bfloat16)
    return high, low


def make_tables(x_local):
    positions = np.arange(NG)
    angles = 2.0 * np.pi / NG * (positions[:, None] * positions[None, :] % NG)
    cas = np.cos(angles) + np.sin(angles)
    into = np.zeros((GROUP, 2 * LANES, NG))
    for r in range(GROUP):
        start = r * NG - r * LANES
        into[r, start : start + NG] = cas
    back = np.transpose(into, (0, 2, 1)).copy()
    order = np.arange(NG).reshape(NG // GROUP, GROUP).T.reshape(-1)
    mixed = cas[:, order]
    return split_table(into), split_table(back), split_table(mixed), split_table(mixed.T.copy())


def split_value(value):
    high = value.astype(jnp.bfloat16)
    low = (value - high.astype(jnp.float32)).astype(jnp.bfloat16)
    return high, low


def dot(a, b):
    return lax.dot_general(a, b, (((1,), (0,)), ((), ())), preferred_element_type=jnp.float32)


def dot3(a, b):
    return dot(a[0], b[0]) + (dot(a[0], b[1]) + dot(a[1], b[0]))


def is_ring(blocks):
    return blocks == STEPS + 1


def slot_ahead(s, blocks):
    return (lax.axis_index("blk") + 1 + s) % blocks if is_ring(blocks) else s


def slot_behind(s, blocks):
    return (lax.axis_index("blk") + blocks - 1 - s) % blocks if is_ring(blocks) else s


def route(shift, blocks):
    return [(i, (i + shift) % blocks) for i in range(blocks)]


def spread(array, blocks):
    if is_ring(blocks):
        return lax.all_to_all(array, "blk", 0, 0, tiled=True)
    rows = array.shape[0] // STEPS
    shares = [array[s * rows : (s + 1) * rows] for s in range(STEPS)]
    return jnp.concatenate(
        [lax.ppermute(shares[s], "blk", route(s + 1, blocks)) for s in range(STEPS)]
    )


def shares_of(blocks):
    return blocks if is_ring(blocks) else STEPS


def share_lines(rows, lines):
    return -(-rows * lines // 8) * 8


def plan_kernel(slots, orbs, blocks, late, own, step, remote, count, *refs):
    requests, (known, seen, hist) = refs[:STEPS], refs[STEPS:]
    for s in range(STEPS):
        for k in range(slots):
            requests[s][k] = 0
    for s in range(STEPS):
        hist[slots + s] = 0
        for k in range(orbs):
            seen[s * orbs + k] = -1
    for k in range(slots):
        hist[k] = 0

    def visit(j, carry):
        live = j < count[0]
        s = jnp.where(live, step[j], 0)
        k = remote[j]
        at = seen[s * orbs + k]
        used = hist[slots + s]
        rank = jnp.where(at < 0, used, at)

        @pl.when(live & (at < 0))
        def _():
            for i in range(STEPS):

                @pl.when(s == i)
                def _():
                    requests[i][used] = k

            seen[s * orbs + k] = used
            hist[slots + s] = used + 1

        @pl.when(live)
        def _():
            hist[rank] += 1

        known[j] = slot_behind(s, blocks)
        known[slots + j] = jnp.where(live, rank, 0)
        known[2 * slots + j] = jnp.where(live, own[j], -1)
        return carry

    lax.fori_loop(0, slots, visit, 0)
    beyond = [jnp.int32(0)]
    for k in reversed(range(slots)):
        beyond.append(beyond[-1] + hist[k])
    beyond = beyond[::-1]
    fits = (beyond[FIRST] <= late) & (beyond[TOTALS[-1]] == 0)
    least = sum((beyond[total] > 0).astype(jnp.int32) for total in TOTALS[:-1])
    for s in range(STEPS):
        requests[s][slots] = jnp.where(fits, least, len(TOTALS))


def expand_kernel(half, full):
    rows, columns = full.shape[0], half.shape[1]
    place = lax.broadcasted_iota(jnp.int32, (rows, columns), 0)
    folded = jnp.minimum(place, rows - place)
    picker = (folded == lax.broadcasted_iota(jnp.int32, (rows, columns), 1)).astype(jnp.float32)
    tall = lax.dot_general(
        picker,
        half[0],
        (((1,), (0,)), ((), ())),
        precision=highest,
        preferred_element_type=jnp.float32,
    )
    full[...] = lax.dot_general(
        tall,
        picker,
        (((1,), (1,)), ((), ())),
        precision=highest,
        preferred_element_type=jnp.float32,
    ) * (1.0 / (NG * NG))


def place_kernel(slots, planes, shares, known, *refs):
    place, choice, order, start = refs[-4:]
    largest = refs[0][slots]
    for s in range(1, STEPS + 1):
        largest = jnp.maximum(largest, refs[s][slots])
    choice[0] = largest
    start[0] = 0

    def tally(j, count):
        return count + (known[slots + j] < FIRST).astype(jnp.int32)

    def visit(j, carry):
        chunk = (known[slots + j] >= FIRST).astype(jnp.int32)
        at = start[chunk]
        start[chunk] = at + 1
        order[at] = j
        return carry

    start[1] = lax.fori_loop(0, slots, tally, jnp.int32(0))
    lax.fori_loop(0, slots, visit, 0)
    me = lax.axis_index("plane")
    base = 0
    for size in shares:
        each = size // planes
        for k in range(planes):
            first = base + partner(me, k, planes) * each
            for q in range(each):
                j = order[first + q]
                to = base + k * each + q
                for part in range(3):
                    place[part * slots + to] = known[part * slots + j]
        base += size


def pack_kernel(lines, blocks, low, high, *refs):
    wanted, (orbitals, sent) = refs[:STEPS], refs[STEPS:]
    size = share_lines(high - low, lines)
    for s in range(STEPS):
        share = sent.at[pl.ds(pl.multiple_of(slot_ahead(s, blocks) * size, 8), size), :]
        for c in range(low, high):
            row = wanted[s][c] * lines
            share[pl.ds((c - low) * lines, lines), :] = orbitals[pl.ds(row, lines), :]


def density_kernel(slots, lines, planes, bounds, base, size, place, orbitals, *refs):
    received, parts, kept = refs[: len(bounds)], refs[-planes - 1 : -1], refs[-1]
    each = size // planes
    for j in range(size):
        share, rank = place[base + j], place[slots + base + j]
        for c, (low, high) in enumerate(zip((0,) + bounds, bounds)):
            row = jnp.clip(rank - low, 0, high - low - 1) * lines
            row += share * share_lines(high - low, lines)
            found = received[c][pl.ds(row, lines), :]
            value = found if c == 0 else jnp.where(rank >= low, found, value)
        near = jnp.maximum(place[2 * slots + base + j], 0) * lines
        kept[pl.ds(j * lines, lines), :] = value
        parts[j // each][pl.ds(j % each * lines, lines), :] = (
            orbitals[pl.ds(near, lines), :] * value
        )


def sum_kernel(slots, lines, planes, base, size, fresh, place, *refs):
    kept, parts = refs[0], refs[1 : 1 + planes]
    out = refs[-1]
    if fresh:
        out[...] = jnp.zeros_like(out)
    else:
        out[...] = refs[1 + planes][...]
    each = size // planes
    for j in range(size):
        near = place[2 * slots + base + j] * lines

        @pl.when(near >= 0)
        def _():
            out[pl.ds(near, lines), :] += (
                parts[j // each][pl.ds(j % each * lines, lines), :]
                * kept[pl.ds(j * lines, lines), :]
            )


def transform_kernel(pairs, lines, planes, *refs):
    parts = refs[:planes]
    into_hi, into_lo, back_hi, back_lo, mix_hi, mix_lo, unmix_hi, unmix_lo, kernel = refs[
        planes : planes + 9
    ]
    outs = refs[planes + 9 : 2 * planes + 9]
    cells, waves, result = refs[2 * planes + 9 :]
    whole = planes * lines
    rows = NG // GROUP
    me = lax.axis_index("plane")
    for k in range(planes):
        slab = partner(me, k, planes) * lines
        for p in range(pairs):
            cells[pl.ds(p * whole + slab, lines), :] = parts[k][pl.ds(p * lines, lines), :]
    line = [split_value(cells[pl.ds(t, pairs * rows, stride=LINES), :]) for t in range(LINES)]
    for r in range(GROUP):
        wide = [jnp.concatenate([line[r][i], line[r + 1][i]], axis=1) for i in range(2)]
        found = dot3(wide, (into_hi[r], into_lo[r]))
        for p in range(pairs):
            waves[p, r * rows : (r + 1) * rows, :] = found[p * rows : (p + 1) * rows, :]
    mix = (mix_hi[...], mix_lo[...])
    unmix = (unmix_hi[...], unmix_lo[...])
    for p in range(pairs):
        spectrum = dot3(mix, split_value(waves[p])) * kernel[...]
        waves[p] = dot3(unmix, split_value(spectrum))
    carried = None
    for r in range(GROUP):
        mine = jnp.concatenate(
            [waves[p, r * rows : (r + 1) * rows, :] for p in range(pairs)], axis=0
        )
        wide = dot3(split_value(mine), (back_hi[r], back_lo[r]))
        first = wide[:, :LANES] if carried is None else wide[:, :LANES] + carried
        carried = wide[:, LANES:]
        result[pl.ds(r, pairs * rows, stride=LINES), :] = first
    result[pl.ds(GROUP, pairs * rows, stride=LINES), :] = carried
    for k in range(planes):
        slab = partner(me, k, planes) * lines
        for p in range(pairs):
            outs[k][pl.ds(p * lines, lines), :] = result[pl.ds(p * whole + slab, lines), :]


def shares_for(slots, planes):
    shares = EARLY + LATE
    units = slots // planes
    cuts = [units * sum(shares[: i + 1]) // sum(shares) for i in range(len(shares))]
    sizes = [(b - a) * planes for a, b in zip([0] + cuts, cuts)]
    return sizes, sum(sizes[len(EARLY) :])


def params():
    return pltpu.CompilerParams(vmem_limit_bytes=VMEM_LIMIT)


def cost(microseconds, flops=0):
    moved = int(microseconds * 1e3)
    return pl.CostEstimate(flops=flops, bytes_accessed=moved, transcendentals=0)


def floats(rows):
    return jax.ShapeDtypeStruct((rows, LANES), jnp.float32)


def partner(i, k, size):
    return i ^ k if size & (size - 1) == 0 else (k - i) % size


def exchange(parts, size):
    return [parts[0] if size & (size - 1) == 0 else lax.ppermute(parts[0], "plane", pairs_of(0, size))] + [
        lax.ppermute(parts[k], "plane", pairs_of(k, size)) for k in range(1, size)
    ]


def pairs_of(k, size):
    return [(i, partner(i, k, size)) for i in range(size)]


def local(orbitals, kernel_half, pair_own, pair_step, pair_remote, pair_count):
    groups, blocks, planes = (lax.axis_size(name) for name in ("groups", "blk", "plane"))
    orbs, depth, cell_count = orbitals.shape
    slots = pair_own.shape[0]
    lines = cell_count // LANES
    flat = orbitals.reshape(orbs * lines, LANES)
    shares, late = shares_for(slots, planes)

    width = -(-(slots + 1) // LANES) * LANES
    *requests, known = pl.pallas_call(
        functools.partial(plan_kernel, slots, orbs, blocks, late),
        out_shape=(
            *[jax.ShapeDtypeStruct((width,), jnp.int32)] * STEPS,
            jax.ShapeDtypeStruct((3 * slots,), jnp.int32),
        ),
        in_specs=[smem] * 4,
        out_specs=(smem,) * (STEPS + 1),
        scratch_shapes=[
            pltpu.SMEM((STEPS * orbs,), jnp.int32),
            pltpu.SMEM((slots + STEPS,), jnp.int32),
        ],
        cost_estimate=cost(2.3),
        name="plan",
    )(pair_own, pair_step, pair_remote, pair_count)

    wanted = [lax.ppermute(requests[s], "blk", route(-s - 1, blocks)) for s in range(STEPS)]

    def send(low, high, flat, wanted):
        packed = pl.pallas_call(
            functools.partial(pack_kernel, lines, blocks, low, high),
            out_shape=floats(shares_of(blocks) * share_lines(high - low, lines)),
            in_specs=[smem] * STEPS + [vmem],
            out_specs=vmem,
            compiler_params=params(),
            cost_estimate=cost(0.5),
            name="pack",
        )(*wanted, flat)
        return packed, spread(packed, blocks)

    def make_density(bounds, base, size, place, flat, received, after):
        each = size // planes
        return pl.pallas_call(
            functools.partial(density_kernel, slots, lines, planes, bounds, base, size),
            out_shape=[floats(each * lines)] * planes + [floats(size * lines)],
            in_specs=[smem, vmem] + [vmem] * len(received) + [hbm] * len(after),
            out_specs=[vmem] * (planes + 1),
            compiler_params=params(),
            cost_estimate=cost(0.05 * size),
            name="density",
        )(place, flat, *received, *after)

    def filter_parts(parts, kernel, tables):
        each = parts[0].shape[0] // lines
        backs = pl.pallas_call(
            functools.partial(transform_kernel, each, lines, planes),
            out_shape=[floats(each * lines)] * planes,
            in_specs=[vmem] * (planes + 9),
            out_specs=[vmem] * planes,
            scratch_shapes=[
                pltpu.VMEM((each * planes * lines, LANES), jnp.float32),
                pltpu.VMEM((each, NG, NG), jnp.float32),
                pltpu.VMEM((each * planes * lines, LANES), jnp.float32),
            ],
            compiler_params=params(),
            cost_estimate=cost(0.5 + 0.4 * each),
            name="transform",
        )(*exchange(parts, planes), *tables, kernel)
        return backs

    def add_up(base, size, place, kept, potentials, before):
        return pl.pallas_call(
            functools.partial(sum_kernel, slots, lines, planes, base, size, not before),
            out_shape=floats(orbs * lines),
            in_specs=[smem] + [vmem] * (planes + 1 + len(before)),
            out_specs=vmem,
            compiler_params=params(),
            cost_estimate=cost(0.9),
            name="sum",
        )(place, kept, *potentials, *before)

    def one_chunk(bounds, c, place, flat, kernel, tables, received, before, after=()):
        base, size = sum(shares[:c]), shares[c]
        *parts, kept = make_density(bounds, base, size, place, flat, received, after)
        backs = filter_parts(parts, kernel, tables)
        return add_up(base, size, place, kept, exchange(backs, planes), before), backs

    packed, first = send(0, FIRST, flat, wanted)
    place, choice = pl.pallas_call(
        functools.partial(place_kernel, slots, planes, shares),
        out_shape=(
            jax.ShapeDtypeStruct((3 * slots,), jnp.int32),
            jax.ShapeDtypeStruct((1,), jnp.int32),
        ),
        in_specs=[smem] * (STEPS + 2) + [hbm],
        out_specs=(smem, smem),
        scratch_shapes=[pltpu.SMEM((slots,), jnp.int32), pltpu.SMEM((2,), jnp.int32)],
        cost_estimate=cost(2.8),
        name="place",
    )(known, requests[0], *wanted, packed)
    kernel = pl.pallas_call(
        expand_kernel,
        out_shape=jax.ShapeDtypeStruct((NG, NG), jnp.float32),
        in_specs=[vmem],
        out_specs=vmem,
        cost_estimate=cost(1.4),
        name="expand",
    )(kernel_half)
    if is_ring(blocks) and groups == 2:
        choice = jnp.maximum(choice, lax.ppermute(choice, "groups", [(0, 1), (1, 0)]))
    else:
        choice = lax.pmax(choice, ("groups", "blk"))
    tables = [jnp.asarray(part) for pair in make_tables(NG // planes) for part in pair]

    def finish(total, flat, wanted, place, kernel, tables, first):
        packed, later = send(FIRST, total, flat, wanted)
        summed, after = [], [packed]
        for c in range(len(shares)):
            early = c < len(EARLY)
            bounds = (FIRST,) if early else (FIRST, total)
            rows = [first] if early else [first, later]
            result, backs = one_chunk(
                bounds, c, place, flat, kernel, tables, rows, summed, after
            )
            summed = [result]
            if c + 1 == len(EARLY):
                after = [backs[-1]]
        return summed[0]

    def general(flat, wanted, place, kernel, tables, first):
        rows = [send(0, slots, flat, wanted)[1]]
        summed = []
        for c in range(len(shares)):
            summed = [one_chunk((slots,), c, place, flat, kernel, tables, rows, summed)[0]]
        return summed[0]

    summed = lax.switch(
        choice[0],
        [functools.partial(finish, total) for total in TOTALS] + [general],
        flat,
        wanted,
        place,
        kernel,
        tables,
        first,
    )
    return summed.reshape(orbs, depth, cell_count)


def solution(mesh):
    in_specs = (
        P(("groups", "blk"), None, "plane"),
        P(),
        P(("groups", "blk")),
        P(("groups", "blk")),
        P(("groups", "blk")),
        P(("groups", "blk")),
    )
    out_specs = P(("groups", "blk"), None, "plane")
    return jax.shard_map(local, mesh=mesh, in_specs=in_specs, out_specs=out_specs, check_vma=False)
```

```python
import functools

import jax
import jax.numpy as jnp
import ml_dtypes
import numpy as np
from jax import lax
from jax.experimental import pallas as pl
from jax.experimental.pallas import tpu as pltpu
from jax.sharding import PartitionSpec as P

NG = 160
STEPS = 3
LANES = 128
GROUP = 4
LINES = 5
FIRST = 9
TOTALS = (16, 18, 20, 23)
EARLY = (3, 3)
LATE = (3, 3)

VMEM_LIMIT = 48 * 1024 * 1024
highest = lax.Precision.HIGHEST
smem = pl.BlockSpec(memory_space=pltpu.SMEM)
vmem = pl.BlockSpec(memory_space=pltpu.VMEM)
hbm = pl.BlockSpec(memory_space=pl.ANY)


def split_table(table):
    high = table.astype(ml_dtypes.bfloat16)
    low = (table - high.astype(np.float64)).astype(ml_dtypes.bfloat16)
    return high, low


def make_tables(x_local):
    positions = np.arange(NG)
    angles = 2.0 * np.pi / NG * (positions[:, None] * positions[None, :] % NG)
    cas = np.cos(angles) + np.sin(angles)
    into = np.zeros((GROUP, 2 * LANES, NG))
    for r in range(GROUP):
        start = r * NG - r * LANES
        into[r, start : start + NG] = cas
    back = np.transpose(into, (0, 2, 1)).copy()
    order = np.arange(NG).reshape(NG // GROUP, GROUP).T.reshape(-1)
    mixed = cas[:, order]
    return split_table(into), split_table(back), split_table(mixed), split_table(mixed.T.copy())


def split_value(value):
    high = value.astype(jnp.bfloat16)
    low = (value - high.astype(jnp.float32)).astype(jnp.bfloat16)
    return high, low


def dot(a, b):
    return lax.dot_general(a, b, (((1,), (0,)), ((), ())), preferred_element_type=jnp.float32)


def dot3(a, b):
    return dot(a[0], b[0]) + (dot(a[0], b[1]) + dot(a[1], b[0]))


def is_ring(blocks):
    return blocks == STEPS + 1


def route(shift, blocks):
    return [(i, (i + shift) % blocks) for i in range(blocks)]


def plan_kernel(slots, orbs, late, own, step, remote, count, *refs):
    requests, (known, seen, hist) = refs[:STEPS], refs[STEPS:]
    for s in range(STEPS):
        for k in range(slots):
            requests[s][k] = 0
    for s in range(STEPS):
        hist[slots + s] = 0
        for k in range(orbs):
            seen[s * orbs + k] = -1
    for k in range(slots):
        hist[k] = 0

    def visit(j, carry):
        live = j < count[0]
        s = jnp.where(live, step[j], 0)
        k = remote[j]
        at = seen[s * orbs + k]
        used = hist[slots + s]
        rank = jnp.where(at < 0, used, at)

        @pl.when(live & (at < 0))
        def _():
            for i in range(STEPS):

                @pl.when(s == i)
                def _():
                    requests[i][used] = k

            seen[s * orbs + k] = used
            hist[slots + s] = used + 1

        @pl.when(live)
        def _():
            hist[rank] += 1

        known[j] = s
        known[slots + j] = jnp.where(live, rank, 0)
        known[2 * slots + j] = jnp.where(live, own[j], -1)
        return carry

    lax.fori_loop(0, slots, visit, 0)
    beyond = [jnp.int32(0)]
    for k in reversed(range(slots)):
        beyond.append(beyond[-1] + hist[k])
    beyond = beyond[::-1]
    fits = (beyond[FIRST] <= late) & (beyond[TOTALS[-1]] == 0)
    least = sum((beyond[total] > 0).astype(jnp.int32) for total in TOTALS[:-1])
    for s in range(STEPS):
        requests[s][slots] = jnp.where(fits, least, len(TOTALS))


def expand_kernel(half, full):
    rows, columns = full.shape[0], half.shape[1]
    place = lax.broadcasted_iota(jnp.int32, (rows, columns), 0)
    folded = jnp.minimum(place, rows - place)
    picker = (folded == lax.broadcasted_iota(jnp.int32, (rows, columns), 1)).astype(jnp.float32)
    tall = lax.dot_general(
        picker,
        half[0],
        (((1,), (0,)), ((), ())),
        precision=highest,
        preferred_element_type=jnp.float32,
    )
    full[...] = lax.dot_general(
        tall,
        picker,
        (((1,), (1,)), ((), ())),
        precision=highest,
        preferred_element_type=jnp.float32,
    ) * (1.0 / (NG * NG))


def place_kernel(slots, planes, shares, known, *refs):
    place, choice, order, start = refs[-4:]
    largest = refs[0][slots]
    for s in range(1, STEPS + 1):
        largest = jnp.maximum(largest, refs[s][slots])
    choice[0] = largest
    start[0] = 0

    def tally(j, count):
        return count + (known[slots + j] < FIRST).astype(jnp.int32)

    def visit(j, carry):
        chunk = (known[slots + j] >= FIRST).astype(jnp.int32)
        at = start[chunk]
        start[chunk] = at + 1
        order[at] = j
        return carry

    start[1] = lax.fori_loop(0, slots, tally, jnp.int32(0))
    lax.fori_loop(0, slots, visit, 0)
    me = lax.axis_index("plane")
    base = 0
    for size in shares:
        each = size // planes
        for k in range(planes):
            first = base + partner(me, k, planes) * each
            for q in range(each):
                j = order[first + q]
                to = base + k * each + q
                for part in range(3):
                    place[part * slots + to] = known[part * slots + j]
        base += size


def pack_kernel(lines, low, high, wanted, orbitals, sent):
    for c in range(low, high):
        row = wanted[c] * lines
        sent[pl.ds((c - low) * lines, lines), :] = orbitals[pl.ds(row, lines), :]


def own_kernel(slots, lines, base, size, place, orbitals, owned):
    for j in range(size):
        near = jnp.maximum(place[2 * slots + base + j], 0) * lines
        owned[pl.ds(j * lines, lines), :] = orbitals[pl.ds(near, lines), :]


def density_kernel(slots, lines, planes, bounds, base, size, place, owned, *refs):
    received, parts, kept = refs[: STEPS * len(bounds)], refs[-planes - 1 : -1], refs[-1]
    each = size // planes
    for j in range(size):
        s, rank = place[base + j], place[slots + base + j]
        for c, (low, high) in enumerate(zip((0,) + bounds, bounds)):
            row = jnp.clip(rank - low, 0, high - low - 1) * lines
            found = received[c * STEPS][pl.ds(row, lines), :]
            for i in range(1, STEPS):
                found = jnp.where(s == i, received[c * STEPS + i][pl.ds(row, lines), :], found)
            value = found if c == 0 else jnp.where(rank >= low, found, value)
        kept[pl.ds(j * lines, lines), :] = value
        parts[j // each][pl.ds(j % each * lines, lines), :] = (
            owned[pl.ds(j * lines, lines), :] * value
        )


def sum_kernel(slots, lines, planes, base, size, fresh, place, *refs):
    kept, parts = refs[0], refs[1 : 1 + planes]
    out = refs[-1]
    if fresh:
        out[...] = jnp.zeros_like(out)
    else:
        out[...] = refs[1 + planes][...]
    each = size // planes
    for j in range(size):
        near = place[2 * slots + base + j] * lines

        @pl.when(near >= 0)
        def _():
            out[pl.ds(near, lines), :] += (
                parts[j // each][pl.ds(j % each * lines, lines), :]
                * kept[pl.ds(j * lines, lines), :]
            )


def transform_kernel(pairs, lines, planes, *refs):
    parts = refs[:planes]
    into_hi, into_lo, back_hi, back_lo, mix_hi, mix_lo, unmix_hi, unmix_lo, kernel = refs[
        planes : planes + 9
    ]
    outs = refs[planes + 9 : 2 * planes + 9]
    cells, waves, result = refs[2 * planes + 9 :]
    whole = planes * lines
    rows = NG // GROUP
    me = lax.axis_index("plane")
    for k in range(planes):
        slab = partner(me, k, planes) * lines
        for p in range(pairs):
            cells[pl.ds(p * whole + slab, lines), :] = parts[k][pl.ds(p * lines, lines), :]
    line = [split_value(cells[pl.ds(t, pairs * rows, stride=LINES), :]) for t in range(LINES)]
    for r in range(GROUP):
        wide = [jnp.concatenate([line[r][i], line[r + 1][i]], axis=1) for i in range(2)]
        found = dot3(wide, (into_hi[r], into_lo[r]))
        for p in range(pairs):
            waves[p, r * rows : (r + 1) * rows, :] = found[p * rows : (p + 1) * rows, :]
    mix = (mix_hi[...], mix_lo[...])
    unmix = (unmix_hi[...], unmix_lo[...])
    for p in range(pairs):
        spectrum = dot3(mix, split_value(waves[p])) * kernel[...]
        waves[p] = dot3(unmix, split_value(spectrum))
    carried = None
    for r in range(GROUP):
        mine = jnp.concatenate(
            [waves[p, r * rows : (r + 1) * rows, :] for p in range(pairs)], axis=0
        )
        wide = dot3(split_value(mine), (back_hi[r], back_lo[r]))
        first = wide[:, :LANES] if carried is None else wide[:, :LANES] + carried
        carried = wide[:, LANES:]
        result[pl.ds(r, pairs * rows, stride=LINES), :] = first
    result[pl.ds(GROUP, pairs * rows, stride=LINES), :] = carried
    for k in range(planes):
        slab = partner(me, k, planes) * lines
        for p in range(pairs):
            outs[k][pl.ds(p * lines, lines), :] = result[pl.ds(p * whole + slab, lines), :]


def shares_for(slots, planes):
    shares = EARLY + LATE
    units = slots // planes
    cuts = [units * sum(shares[: i + 1]) // sum(shares) for i in range(len(shares))]
    sizes = [(b - a) * planes for a, b in zip([0] + cuts, cuts)]
    return sizes, sum(sizes[len(EARLY) :])


def params():
    return pltpu.CompilerParams(vmem_limit_bytes=VMEM_LIMIT)


def cost(microseconds, flops=0):
    moved = int(microseconds * 1e3)
    return pl.CostEstimate(flops=flops, bytes_accessed=moved, transcendentals=0)


def floats(rows):
    return jax.ShapeDtypeStruct((rows, LANES), jnp.float32)


def partner(i, k, size):
    return i ^ k if size & (size - 1) == 0 else (k - i) % size


def exchange(parts, size):
    return [parts[0] if size & (size - 1) == 0 else lax.ppermute(parts[0], "plane", pairs_of(0, size))] + [
        lax.ppermute(parts[k], "plane", pairs_of(k, size)) for k in range(1, size)
    ]


def pairs_of(k, size):
    return [(i, partner(i, k, size)) for i in range(size)]


def local(orbitals, kernel_half, pair_own, pair_step, pair_remote, pair_count):
    groups, blocks, planes = (lax.axis_size(name) for name in ("groups", "blk", "plane"))
    orbs, depth, cell_count = orbitals.shape
    slots = pair_own.shape[0]
    lines = cell_count // LANES
    flat = orbitals.reshape(orbs * lines, LANES)
    shares, late = shares_for(slots, planes)

    width = -(-(slots + 1) // LANES) * LANES
    *requests, known = pl.pallas_call(
        functools.partial(plan_kernel, slots, orbs, late),
        out_shape=(
            *[jax.ShapeDtypeStruct((width,), jnp.int32)] * STEPS,
            jax.ShapeDtypeStruct((3 * slots,), jnp.int32),
        ),
        in_specs=[smem] * 4,
        out_specs=(smem,) * (STEPS + 1),
        scratch_shapes=[
            pltpu.SMEM((STEPS * orbs,), jnp.int32),
            pltpu.SMEM((slots + STEPS,), jnp.int32),
        ],
        cost_estimate=cost(2.3),
        name="plan",
    )(pair_own, pair_step, pair_remote, pair_count)

    wanted = [lax.ppermute(requests[s], "blk", route(-s - 1, blocks)) for s in range(STEPS)]

    def send(low, high, flat, wanted):
        packs = [
            pl.pallas_call(
                functools.partial(pack_kernel, lines, low, high),
                out_shape=floats((high - low) * lines),
                in_specs=[smem, vmem],
                out_specs=vmem,
                compiler_params=params(),
                cost_estimate=cost(0.5),
                name="pack",
            )(wanted[s], flat)
            for s in range(STEPS)
        ]
        return packs, [lax.ppermute(packs[s], "blk", route(s + 1, blocks)) for s in range(STEPS)]

    def make_density(bounds, base, size, place, owned, received, after):
        each = size // planes
        return pl.pallas_call(
            functools.partial(density_kernel, slots, lines, planes, bounds, base, size),
            out_shape=[floats(each * lines)] * planes + [floats(size * lines)],
            in_specs=[smem, vmem] + [vmem] * len(received) + [hbm] * len(after),
            out_specs=[vmem] * (planes + 1),
            compiler_params=params(),
            cost_estimate=cost(0.05 * size),
            name="density",
        )(place, owned, *received, *after)

    def filter_parts(parts, kernel, tables):
        each = parts[0].shape[0] // lines
        backs = pl.pallas_call(
            functools.partial(transform_kernel, each, lines, planes),
            out_shape=[floats(each * lines)] * planes,
            in_specs=[vmem] * (planes + 9),
            out_specs=[vmem] * planes,
            scratch_shapes=[
                pltpu.VMEM((each * planes * lines, LANES), jnp.float32),
                pltpu.VMEM((each, NG, NG), jnp.float32),
                pltpu.VMEM((each * planes * lines, LANES), jnp.float32),
            ],
            compiler_params=params(),
            cost_estimate=cost(0.5 + 0.4 * each),
            name="transform",
        )(*exchange(parts, planes), *tables, kernel)
        return backs

    def add_up(base, size, place, kept, potentials, before):
        return pl.pallas_call(
            functools.partial(sum_kernel, slots, lines, planes, base, size, not before),
            out_shape=floats(orbs * lines),
            in_specs=[smem] + [vmem] * (planes + 1 + len(before)),
            out_specs=vmem,
            compiler_params=params(),
            cost_estimate=cost(0.9),
            name="sum",
        )(place, kept, *potentials, *before)

    def own_rows(c, place, flat):
        return pl.pallas_call(
            functools.partial(own_kernel, slots, lines, sum(shares[:c]), shares[c]),
            out_shape=floats(shares[c] * lines),
            in_specs=[smem, vmem],
            out_specs=vmem,
            compiler_params=params(),
            cost_estimate=cost(0.5),
            name="own",
        )(place, flat)

    def one_chunk(bounds, c, place, owned, kernel, tables, received, before, after=()):
        base, size = sum(shares[:c]), shares[c]
        *parts, kept = make_density(bounds, base, size, place, owned[c], received, after)
        backs = filter_parts(parts, kernel, tables)
        return add_up(base, size, place, kept, exchange(backs, planes), before), backs

    packs, first = send(0, FIRST, flat, wanted)
    place, choice = pl.pallas_call(
        functools.partial(place_kernel, slots, planes, shares),
        out_shape=(
            jax.ShapeDtypeStruct((3 * slots,), jnp.int32),
            jax.ShapeDtypeStruct((1,), jnp.int32),
        ),
        in_specs=[smem] * (STEPS + 2) + [hbm] * STEPS,
        out_specs=(smem, smem),
        scratch_shapes=[pltpu.SMEM((slots,), jnp.int32), pltpu.SMEM((2,), jnp.int32)],
        cost_estimate=cost(2.8),
        name="place",
    )(known, requests[0], *wanted, *packs)
    owned = [own_rows(c, place, flat) for c in range(len(shares))]
    kernel = pl.pallas_call(
        expand_kernel,
        out_shape=jax.ShapeDtypeStruct((NG, NG), jnp.float32),
        in_specs=[vmem],
        out_specs=vmem,
        cost_estimate=cost(1.4),
        name="expand",
    )(kernel_half)
    if is_ring(blocks) and groups == 2:
        choice = jnp.maximum(choice, lax.ppermute(choice, "groups", [(0, 1), (1, 0)]))
    else:
        choice = lax.pmax(choice, ("groups", "blk"))
    tables = [jnp.asarray(part) for pair in make_tables(NG // planes) for part in pair]

    def finish(total, flat, wanted, place, owned, kernel, tables, first):
        packs, later = send(FIRST, total, flat, wanted)
        summed, after, formed = [], packs, []
        for c in range(len(shares)):
            early = c < len(EARLY)
            bounds = (FIRST,) if early else (FIRST, total)
            rows = first if early else first + later
            result, backs = one_chunk(
                bounds, c, place, owned, kernel, tables, rows, summed, after
            )
            summed = [result]
            if early:
                formed.append(backs[-1])
            if c + 1 == len(EARLY):
                after = formed
        return summed[0]

    def general(flat, wanted, place, owned, kernel, tables, first):
        rows = send(0, slots, flat, wanted)[1]
        summed = []
        for c in range(len(shares)):
            summed = [one_chunk((slots,), c, place, owned, kernel, tables, rows, summed)[0]]
        return summed[0]

    summed = lax.switch(
        choice[0],
        [functools.partial(finish, total) for total in TOTALS] + [general],
        flat,
        wanted,
        place,
        owned,
        kernel,
        tables,
        first,
    )
    return summed.reshape(orbs, depth, cell_count)


def solution(mesh):
    in_specs = (
        P(("groups", "blk"), None, "plane"),
        P(),
        P(("groups", "blk")),
        P(("groups", "blk")),
        P(("groups", "blk")),
        P(("groups", "blk")),
    )
    out_specs = P(("groups", "blk"), None, "plane")
    return jax.shard_map(local, mesh=mesh, in_specs=in_specs, out_specs=out_specs, check_vma=False)
```

```python
import functools

import jax
import jax.numpy as jnp
import ml_dtypes
import numpy as np
from jax import lax
from jax.experimental import pallas as pl
from jax.experimental.pallas import tpu as pltpu
from jax.sharding import PartitionSpec as P

NG = 160
STEPS = 3
LANES = 128
GROUP = 4
LINES = 5
FIRST = 10
TOTALS = (16, 18, 19, 20, 22)
EARLY = (4, 3)
LATE = (3, 2)

VMEM_LIMIT = 48 * 1024 * 1024
highest = lax.Precision.HIGHEST
smem = pl.BlockSpec(memory_space=pltpu.SMEM)
vmem = pl.BlockSpec(memory_space=pltpu.VMEM)
hbm = pl.BlockSpec(memory_space=pl.ANY)


def split_table(table):
    high = table.astype(ml_dtypes.bfloat16)
    low = (table - high.astype(np.float64)).astype(ml_dtypes.bfloat16)
    return high, low


def make_tables(x_local):
    positions = np.arange(NG)
    angles = 2.0 * np.pi / NG * (positions[:, None] * positions[None, :] % NG)
    cas = np.cos(angles) + np.sin(angles)
    into = np.zeros((GROUP, 2 * LANES, NG))
    for r in range(GROUP):
        start = r * NG - r * LANES
        into[r, start : start + NG] = cas
    back = np.transpose(into, (0, 2, 1)).copy()
    order = np.arange(NG).reshape(NG // GROUP, GROUP).T.reshape(-1)
    mixed = cas[:, order]
    return split_table(into), split_table(back), split_table(mixed), split_table(mixed.T.copy())


def split_value(value):
    high = value.astype(jnp.bfloat16)
    low = (value - high.astype(jnp.float32)).astype(jnp.bfloat16)
    return high, low


def dot(a, b):
    return lax.dot_general(a, b, (((1,), (0,)), ((), ())), preferred_element_type=jnp.float32)


def dot3(a, b):
    return dot(a[0], b[0]) + (dot(a[0], b[1]) + dot(a[1], b[0]))


def is_ring(blocks):
    return blocks == STEPS + 1


def route(shift, blocks):
    return [(i, (i + shift) % blocks) for i in range(blocks)]


def plan_kernel(slots, orbs, late, own, step, remote, count, *refs):
    requests, (known, seen, hist) = refs[:STEPS], refs[STEPS:]
    for s in range(STEPS):
        for k in range(slots):
            requests[s][k] = 0
    for s in range(STEPS):
        hist[slots + s] = 0
        for k in range(orbs):
            seen[s * orbs + k] = -1
    for k in range(slots):
        hist[k] = 0

    def visit(j, carry):
        live = j < count[0]
        s = jnp.where(live, step[j], 0)
        k = remote[j]
        at = seen[s * orbs + k]
        used = hist[slots + s]
        rank = jnp.where(at < 0, used, at)

        @pl.when(live & (at < 0))
        def _():
            for i in range(STEPS):

                @pl.when(s == i)
                def _():
                    requests[i][used] = k

            seen[s * orbs + k] = used
            hist[slots + s] = used + 1

        @pl.when(live)
        def _():
            hist[rank] += 1

        known[j] = s
        known[slots + j] = jnp.where(live, rank, 0)
        known[2 * slots + j] = jnp.where(live, own[j], -1)
        return carry

    lax.fori_loop(0, slots, visit, 0)
    beyond = [jnp.int32(0)]
    for k in reversed(range(slots)):
        beyond.append(beyond[-1] + hist[k])
    beyond = beyond[::-1]
    fits = (beyond[FIRST] <= late) & (beyond[TOTALS[-1]] == 0)
    least = sum((beyond[total] > 0).astype(jnp.int32) for total in TOTALS[:-1])
    for s in range(STEPS):
        requests[s][slots] = jnp.where(fits, least, len(TOTALS))


def expand_kernel(half, full):
    rows, columns = full.shape[0], half.shape[1]
    place = lax.broadcasted_iota(jnp.int32, (rows, columns), 0)
    folded = jnp.minimum(place, rows - place)
    picker = (folded == lax.broadcasted_iota(jnp.int32, (rows, columns), 1)).astype(jnp.float32)
    tall = lax.dot_general(
        picker,
        half[0],
        (((1,), (0,)), ((), ())),
        precision=highest,
        preferred_element_type=jnp.float32,
    )
    full[...] = lax.dot_general(
        tall,
        picker,
        (((1,), (1,)), ((), ())),
        precision=highest,
        preferred_element_type=jnp.float32,
    ) * (1.0 / (NG * NG))


def place_kernel(slots, planes, shares, known, *refs):
    place, choice, order, start = refs[-4:]
    largest = refs[0][slots]
    for s in range(1, STEPS + 1):
        largest = jnp.maximum(largest, refs[s][slots])
    choice[0] = largest
    start[0] = 0

    def tally(j, count):
        return count + (known[slots + j] < FIRST).astype(jnp.int32)

    def visit(j, carry):
        chunk = (known[slots + j] >= FIRST).astype(jnp.int32)
        at = start[chunk]
        start[chunk] = at + 1
        order[at] = j
        return carry

    start[1] = lax.fori_loop(0, slots, tally, jnp.int32(0))
    lax.fori_loop(0, slots, visit, 0)
    me = lax.axis_index("plane")
    base = 0
    for size in shares:
        each = size // planes
        for k in range(planes):
            first = base + partner(me, k, planes) * each
            for q in range(each):
                j = order[first + q]
                to = base + k * each + q
                for part in range(3):
                    place[part * slots + to] = known[part * slots + j]
        base += size


def pack_kernel(lines, low, high, wanted, orbitals, sent):
    for c in range(low, high):
        row = wanted[c] * lines
        sent[pl.ds((c - low) * lines, lines), :] = orbitals[pl.ds(row, lines), :]


def own_kernel(slots, lines, base, size, place, orbitals, owned):
    for j in range(size):
        near = jnp.maximum(place[2 * slots + base + j], 0) * lines
        owned[pl.ds(j * lines, lines), :] = orbitals[pl.ds(near, lines), :]


def density_kernel(slots, lines, planes, bounds, base, size, place, owned, *refs):
    received, parts, kept = refs[: STEPS * len(bounds)], refs[-planes - 1 : -1], refs[-1]
    each = size // planes
    for j in range(size):
        s, rank = place[base + j], place[slots + base + j]
        for c, (low, high) in enumerate(zip((0,) + bounds, bounds)):
            row = jnp.clip(rank - low, 0, high - low - 1) * lines
            found = received[c * STEPS][pl.ds(row, lines), :]
            for i in range(1, STEPS):
                found = jnp.where(s == i, received[c * STEPS + i][pl.ds(row, lines), :], found)
            value = found if c == 0 else jnp.where(rank >= low, found, value)
        kept[pl.ds(j * lines, lines), :] = value
        parts[j // each][pl.ds(j % each * lines, lines), :] = (
            owned[pl.ds(j * lines, lines), :] * value
        )


def sum_kernel(slots, lines, planes, base, size, stacked, fresh, place, *refs):
    out = refs[-1]
    if fresh:
        out[...] = jnp.zeros_like(out)
    else:
        out[...] = refs[-2][...]
    each = size // planes
    kept, parts = refs[0], refs[1 : 1 + planes]
    if stacked:
        me = lax.axis_index("plane")
        parts = [share_of(refs[1], partner(me, k, planes), planes) for k in range(planes)]
    for j in range(size):
        near = place[2 * slots + base + j] * lines

        @pl.when(near >= 0)
        def _():
            out[pl.ds(near, lines), :] += (
                parts[j // each][pl.ds(j % each * lines, lines), :]
                * kept[pl.ds(j * lines, lines), :]
            )


def share_of(stack, which, planes):
    size = stack.shape[0] // planes
    return stack.at[pl.ds(pl.multiple_of(which * size, 8), size), :]


def transform_kernel(pairs, lines, planes, stacked, *refs):
    parts = refs[:planes]
    into_hi, into_lo, back_hi, back_lo, mix_hi, mix_lo, unmix_hi, unmix_lo, kernel = refs[
        planes : planes + 9
    ]
    outs = refs[planes + 9 : -3]
    cells, waves, result = refs[-3:]
    whole = planes * lines
    rows = NG // GROUP
    me = lax.axis_index("plane")
    for k in range(planes):
        slab = partner(me, k, planes) * lines
        for p in range(pairs):
            cells[pl.ds(p * whole + slab, lines), :] = parts[k][pl.ds(p * lines, lines), :]
    line = [split_value(cells[pl.ds(t, pairs * rows, stride=LINES), :]) for t in range(LINES)]
    for r in range(GROUP):
        wide = [jnp.concatenate([line[r][i], line[r + 1][i]], axis=1) for i in range(2)]
        found = dot3(wide, (into_hi[r], into_lo[r]))
        for p in range(pairs):
            waves[p, r * rows : (r + 1) * rows, :] = found[p * rows : (p + 1) * rows, :]
    mix = (mix_hi[...], mix_lo[...])
    unmix = (unmix_hi[...], unmix_lo[...])
    for p in range(pairs):
        spectrum = dot3(mix, split_value(waves[p])) * kernel[...]
        waves[p] = dot3(unmix, split_value(spectrum))
    carried = None
    for r in range(GROUP):
        mine = jnp.concatenate(
            [waves[p, r * rows : (r + 1) * rows, :] for p in range(pairs)], axis=0
        )
        wide = dot3(split_value(mine), (back_hi[r], back_lo[r]))
        first = wide[:, :LANES] if carried is None else wide[:, :LANES] + carried
        carried = wide[:, LANES:]
        result[pl.ds(r, pairs * rows, stride=LINES), :] = first
    result[pl.ds(GROUP, pairs * rows, stride=LINES), :] = carried
    for k in range(planes):
        slab = partner(me, k, planes) * lines
        out = share_of(outs[0], partner(me, k, planes), planes) if stacked else outs[k]
        for p in range(pairs):
            out[pl.ds(p * lines, lines), :] = result[pl.ds(p * whole + slab, lines), :]


def shares_for(slots, planes):
    shares = EARLY + LATE
    units = slots // planes
    cuts = [units * sum(shares[: i + 1]) // sum(shares) for i in range(len(shares))]
    sizes = [(b - a) * planes for a, b in zip([0] + cuts, cuts)]
    return sizes, sum(sizes[len(EARLY) :])


def params():
    return pltpu.CompilerParams(vmem_limit_bytes=VMEM_LIMIT)


def cost(microseconds, flops=0):
    moved = int(microseconds * 1e3)
    return pl.CostEstimate(flops=flops, bytes_accessed=moved, transcendentals=0)


def floats(rows):
    return jax.ShapeDtypeStruct((rows, LANES), jnp.float32)


def partner(i, k, size):
    return i ^ k if size & (size - 1) == 0 else (k - i) % size


def exchange(parts, size):
    return [parts[0] if size & (size - 1) == 0 else lax.ppermute(parts[0], "plane", pairs_of(0, size))] + [
        lax.ppermute(parts[k], "plane", pairs_of(k, size)) for k in range(1, size)
    ]


def pairs_of(k, size):
    return [(i, partner(i, k, size)) for i in range(size)]


def local(orbitals, kernel_half, pair_own, pair_step, pair_remote, pair_count):
    groups, blocks, planes = (lax.axis_size(name) for name in ("groups", "blk", "plane"))
    orbs, depth, cell_count = orbitals.shape
    slots = pair_own.shape[0]
    lines = cell_count // LANES
    flat = orbitals.reshape(orbs * lines, LANES)
    shares, late = shares_for(slots, planes)

    width = -(-(slots + 1) // LANES) * LANES
    *requests, known = pl.pallas_call(
        functools.partial(plan_kernel, slots, orbs, late),
        out_shape=(
            *[jax.ShapeDtypeStruct((width,), jnp.int32)] * STEPS,
            jax.ShapeDtypeStruct((3 * slots,), jnp.int32),
        ),
        in_specs=[smem] * 4,
        out_specs=(smem,) * (STEPS + 1),
        scratch_shapes=[
            pltpu.SMEM((STEPS * orbs,), jnp.int32),
            pltpu.SMEM((slots + STEPS,), jnp.int32),
        ],
        cost_estimate=cost(2.3),
        name="plan",
    )(pair_own, pair_step, pair_remote, pair_count)

    wanted = [lax.ppermute(requests[s], "blk", route(-s - 1, blocks)) for s in range(STEPS)]

    def send(low, high, flat, wanted):
        packs = [
            pl.pallas_call(
                functools.partial(pack_kernel, lines, low, high),
                out_shape=floats((high - low) * lines),
                in_specs=[smem, vmem],
                out_specs=vmem,
                compiler_params=params(),
                cost_estimate=cost(0.5),
                name="pack",
            )(wanted[s], flat)
            for s in range(STEPS)
        ]
        return packs, [lax.ppermute(packs[s], "blk", route(s + 1, blocks)) for s in range(STEPS)]

    def make_density(bounds, base, size, place, owned, received, after):
        each = size // planes
        return pl.pallas_call(
            functools.partial(density_kernel, slots, lines, planes, bounds, base, size),
            out_shape=[floats(each * lines)] * planes + [floats(size * lines)],
            in_specs=[smem, vmem] + [vmem] * len(received) + [hbm] * len(after),
            out_specs=[vmem] * (planes + 1),
            compiler_params=params(),
            cost_estimate=cost(0.05 * size),
            name="density",
        )(place, owned, *received, *after)

    def filter_parts(parts, kernel, tables, stacked):
        each = parts[0].shape[0] // lines
        shapes = [floats(each * lines)] * planes
        if stacked:
            shapes = [floats(planes * (-(-each * lines // 8) * 8))]
        return pl.pallas_call(
            functools.partial(transform_kernel, each, lines, planes, stacked),
            out_shape=shapes,
            in_specs=[vmem] * (planes + 9),
            out_specs=[vmem] * len(shapes),
            scratch_shapes=[
                pltpu.VMEM((each * planes * lines, LANES), jnp.float32),
                pltpu.VMEM((each, NG, NG), jnp.float32),
                pltpu.VMEM((each * planes * lines, LANES), jnp.float32),
            ],
            compiler_params=params(),
            cost_estimate=cost(0.5 + 0.4 * each),
            name="transform",
        )(*exchange(parts, planes), *tables, kernel)

    def add_up(base, size, place, kept, potentials, before, stacked):
        return pl.pallas_call(
            functools.partial(sum_kernel, slots, lines, planes, base, size, stacked, not before),
            out_shape=floats(orbs * lines),
            in_specs=[smem] + [vmem] * (len(potentials) + 1 + len(before)),
            out_specs=vmem,
            compiler_params=params(),
            cost_estimate=cost(0.9),
            name="sum",
        )(place, kept, *potentials, *before)

    def own_rows(c, place, flat):
        return pl.pallas_call(
            functools.partial(own_kernel, slots, lines, sum(shares[:c]), shares[c]),
            out_shape=floats(shares[c] * lines),
            in_specs=[smem, vmem],
            out_specs=vmem,
            compiler_params=params(),
            cost_estimate=cost(0.5),
            name="own",
        )(place, flat)

    def one_chunk(bounds, c, place, owned, kernel, tables, received, before, after, stacked):
        base, size = sum(shares[:c]), shares[c]
        *parts, kept = make_density(bounds, base, size, place, owned[c], received, after)
        backs = filter_parts(parts, kernel, tables, stacked)
        if stacked:
            potentials = [lax.all_to_all(backs[0], "plane", 0, 0, tiled=True)]
        else:
            potentials = exchange(backs, planes)
        return add_up(base, size, place, kept, potentials, before, stacked), backs

    packs, first = send(0, FIRST, flat, wanted)
    place, choice = pl.pallas_call(
        functools.partial(place_kernel, slots, planes, shares),
        out_shape=(
            jax.ShapeDtypeStruct((3 * slots,), jnp.int32),
            jax.ShapeDtypeStruct((1,), jnp.int32),
        ),
        in_specs=[smem] * (STEPS + 2) + [hbm] * STEPS,
        out_specs=(smem, smem),
        scratch_shapes=[pltpu.SMEM((slots,), jnp.int32), pltpu.SMEM((2,), jnp.int32)],
        cost_estimate=cost(2.8),
        name="place",
    )(known, requests[0], *wanted, *packs)
    owned = [own_rows(c, place, flat) for c in range(len(shares))]
    kernel = pl.pallas_call(
        expand_kernel,
        out_shape=jax.ShapeDtypeStruct((NG, NG), jnp.float32),
        in_specs=[vmem],
        out_specs=vmem,
        cost_estimate=cost(1.4),
        name="expand",
    )(kernel_half)
    if is_ring(blocks) and groups == 2:
        choice = jnp.maximum(choice, lax.ppermute(choice, "groups", [(0, 1), (1, 0)]))
    else:
        choice = lax.pmax(choice, ("groups", "blk"))
    tables = [jnp.asarray(part) for pair in make_tables(NG // planes) for part in pair]

    def finish(total, flat, wanted, place, owned, kernel, tables, first):
        packs, later = send(FIRST, total, flat, wanted)
        summed, after, formed = [], packs, []
        for c in range(len(shares)):
            early = c < len(EARLY)
            bounds = (FIRST,) if early else (FIRST, total)
            rows = first if early else first + later
            result, backs = one_chunk(
                bounds, c, place, owned, kernel, tables, rows, summed, after, early
            )
            summed = [result]
            if early:
                formed.append(backs[-1])
            if c + 1 == len(EARLY):
                after = formed
        return summed[0]

    def general(flat, wanted, place, owned, kernel, tables, first):
        rows = send(0, slots, flat, wanted)[1]
        total = []
        for c in range(len(shares)):
            total = [
                one_chunk((slots,), c, place, owned, kernel, tables, rows, total, [], False)[0]
            ]
        return total[0]

    summed = lax.switch(
        choice[0],
        [functools.partial(finish, total) for total in TOTALS] + [general],
        flat,
        wanted,
        place,
        owned,
        kernel,
        tables,
        first,
    )
    return summed.reshape(orbs, depth, cell_count)


def solution(mesh):
    in_specs = (
        P(("groups", "blk"), None, "plane"),
        P(),
        P(("groups", "blk")),
        P(("groups", "blk")),
        P(("groups", "blk")),
        P(("groups", "blk")),
    )
    out_specs = P(("groups", "blk"), None, "plane")
    return jax.shard_map(local, mesh=mesh, in_specs=in_specs, out_specs=out_specs, check_vma=False)
```

```python
import functools

import jax
import jax.numpy as jnp
import ml_dtypes
import numpy as np
from jax import lax
from jax.experimental import pallas as pl
from jax.experimental.pallas import tpu as pltpu
from jax.sharding import PartitionSpec as P

NG = 160
STEPS = 3
LANES = 128
GROUP = 4
LINES = 5
FIRST = 9
TOTALS = (16, 18, 20, 23)
EARLY = (3, 3)
LATE = (6,)

PARTS = 3

VMEM_LIMIT = 48 * 1024 * 1024
highest = lax.Precision.HIGHEST
smem = pl.BlockSpec(memory_space=pltpu.SMEM)
vmem = pl.BlockSpec(memory_space=pltpu.VMEM)
hbm = pl.BlockSpec(memory_space=pl.ANY)


def split_table(table):
    high = table.astype(ml_dtypes.bfloat16)
    low = (table - high.astype(np.float64)).astype(ml_dtypes.bfloat16)
    return high, low


def make_tables(x_local):
    positions = np.arange(NG)
    angles = 2.0 * np.pi / NG * (positions[:, None] * positions[None, :] % NG)
    cas = np.cos(angles) + np.sin(angles)
    into = np.zeros((GROUP, 2 * LANES, NG))
    for r in range(GROUP):
        start = r * NG - r * LANES
        into[r, start : start + NG] = cas
    back = np.transpose(into, (0, 2, 1)).copy()
    order = np.arange(NG).reshape(NG // GROUP, GROUP).T.reshape(-1)
    mixed = cas[:, order]
    return split_table(into), split_table(back), split_table(mixed), split_table(mixed.T.copy())


def split_value(value):
    high = value.astype(jnp.bfloat16)
    low = (value - high.astype(jnp.float32)).astype(jnp.bfloat16)
    return high, low


def dot(a, b):
    return lax.dot_general(a, b, (((1,), (0,)), ((), ())), preferred_element_type=jnp.float32)


def dot3(a, b):
    return dot(a[0], b[0]) + (dot(a[0], b[1]) + dot(a[1], b[0]))


def is_ring(blocks):
    return blocks == STEPS + 1


def route(shift, blocks):
    return [(i, (i + shift) % blocks) for i in range(blocks)]


def plan_kernel(slots, orbs, late, own, step, remote, count, *refs):
    requests, (known, seen, hist) = refs[:STEPS], refs[STEPS:]
    for s in range(STEPS):
        for k in range(slots):
            requests[s][k] = 0
    for s in range(STEPS):
        hist[slots + s] = 0
        for k in range(orbs):
            seen[s * orbs + k] = -1
    for k in range(slots):
        hist[k] = 0

    def visit(j, carry):
        live = j < count[0]
        s = jnp.where(live, step[j], 0)
        k = remote[j]
        at = seen[s * orbs + k]
        used = hist[slots + s]
        rank = jnp.where(at < 0, used, at)

        @pl.when(live & (at < 0))
        def _():
            for i in range(STEPS):

                @pl.when(s == i)
                def _():
                    requests[i][used] = k

            seen[s * orbs + k] = used
            hist[slots + s] = used + 1

        @pl.when(live)
        def _():
            hist[rank] += 1

        known[j] = s
        known[slots + j] = jnp.where(live, rank, 0)
        known[2 * slots + j] = jnp.where(live, own[j], -1)
        return carry

    lax.fori_loop(0, slots, visit, 0)
    beyond = [jnp.int32(0)]
    for k in reversed(range(slots)):
        beyond.append(beyond[-1] + hist[k])
    beyond = beyond[::-1]
    fits = (beyond[FIRST] <= late) & (beyond[TOTALS[-1]] == 0)
    least = sum((beyond[total] > 0).astype(jnp.int32) for total in TOTALS[:-1])
    for s in range(STEPS):
        requests[s][slots] = jnp.where(fits, least, len(TOTALS))


def expand_kernel(half, full):
    rows, columns = full.shape[0], half.shape[1]
    place = lax.broadcasted_iota(jnp.int32, (rows, columns), 0)
    folded = jnp.minimum(place, rows - place)
    picker = (folded == lax.broadcasted_iota(jnp.int32, (rows, columns), 1)).astype(jnp.float32)
    tall = lax.dot_general(
        picker,
        half[0],
        (((1,), (0,)), ((), ())),
        precision=highest,
        preferred_element_type=jnp.float32,
    )
    full[...] = lax.dot_general(
        tall,
        picker,
        (((1,), (1,)), ((), ())),
        precision=highest,
        preferred_element_type=jnp.float32,
    ) * (1.0 / (NG * NG))


def place_kernel(slots, planes, shares, known, *refs):
    place, choice, order, start = refs[-4:]
    largest = refs[0][slots]
    for s in range(1, STEPS + 1):
        largest = jnp.maximum(largest, refs[s][slots])
    choice[0] = largest
    start[0] = 0

    def tally(j, count):
        return count + (known[slots + j] < FIRST).astype(jnp.int32)

    def visit(j, carry):
        chunk = (known[slots + j] >= FIRST).astype(jnp.int32)
        at = start[chunk]
        start[chunk] = at + 1
        order[at] = j
        return carry

    start[1] = lax.fori_loop(0, slots, tally, jnp.int32(0))
    lax.fori_loop(0, slots, visit, 0)
    me = lax.axis_index("plane")
    base = 0
    for size in shares:
        each = size // planes
        for k in range(planes):
            first = base + partner(me, k, planes) * each
            for q in range(each):
                j = order[first + q]
                to = base + k * each + q
                for part in range(3):
                    place[part * slots + to] = known[part * slots + j]
        base += size


def pack_kernel(lines, low, high, wanted, orbitals, *refs):
    sent = refs[-1]
    for c in range(low, high):
        row = wanted[c] * lines
        sent[pl.ds((c - low) * lines, lines), :] = orbitals[pl.ds(row, lines), :]


def own_kernel(slots, lines, base, size, place, orbitals, owned):
    for j in range(size):
        near = jnp.maximum(place[2 * slots + base + j], 0) * lines
        owned[pl.ds(j * lines, lines), :] = orbitals[pl.ds(near, lines), :]


def density_kernel(slots, lines, planes, bounds, base, size, place, owned, *refs):
    received, parts, kept = refs[: STEPS * len(bounds)], refs[-planes - 1 : -1], refs[-1]
    each = size // planes
    for j in range(size):
        s, rank = place[base + j], place[slots + base + j]
        for c, (low, high) in enumerate(zip((0,) + bounds, bounds)):
            row = jnp.clip(rank - low, 0, high - low - 1) * lines
            found = received[c * STEPS][pl.ds(row, lines), :]
            for i in range(1, STEPS):
                found = jnp.where(s == i, received[c * STEPS + i][pl.ds(row, lines), :], found)
            value = found if c == 0 else jnp.where(rank >= low, found, value)
        kept[pl.ds(j * lines, lines), :] = value
        parts[j // each][pl.ds(j % each * lines, lines), :] = (
            owned[pl.ds(j * lines, lines), :] * value
        )


def sum_kernel(slots, lines, planes, base, size, fresh, place, *refs):
    kept, parts = refs[0], refs[1 : 1 + planes]
    out = refs[-1]
    if fresh:
        out[...] = jnp.zeros_like(out)
    else:
        out[...] = refs[1 + planes][...]
    each = size // planes
    for j in range(size):
        near = place[2 * slots + base + j] * lines

        @pl.when(near >= 0)
        def _():
            out[pl.ds(near, lines), :] += (
                parts[j // each][pl.ds(j % each * lines, lines), :]
                * kept[pl.ds(j * lines, lines), :]
            )


def transform_kernel(pairs, lines, planes, *refs):
    parts = refs[:planes]
    into_hi, into_lo, back_hi, back_lo, mix_hi, mix_lo, unmix_hi, unmix_lo, kernel = refs[
        planes : planes + 9
    ]
    outs = refs[planes + 9 : 2 * planes + 9]
    cells, waves, result = refs[2 * planes + 9 :]
    whole = planes * lines
    rows = NG // GROUP
    me = lax.axis_index("plane")
    for k in range(planes):
        slab = partner(me, k, planes) * lines
        for p in range(pairs):
            cells[pl.ds(p * whole + slab, lines), :] = parts[k][pl.ds(p * lines, lines), :]
    line = [split_value(cells[pl.ds(t, pairs * rows, stride=LINES), :]) for t in range(LINES)]
    for r in range(GROUP):
        wide = [jnp.concatenate([line[r][i], line[r + 1][i]], axis=1) for i in range(2)]
        found = dot3(wide, (into_hi[r], into_lo[r]))
        for p in range(pairs):
            waves[p, r * rows : (r + 1) * rows, :] = found[p * rows : (p + 1) * rows, :]
    mix = (mix_hi[...], mix_lo[...])
    unmix = (unmix_hi[...], unmix_lo[...])

    def filter_pair(p, carry):
        spectrum = dot3(mix, split_value(waves[p])) * kernel[...]
        waves[p] = dot3(unmix, split_value(spectrum))
        return carry

    lax.fori_loop(0, pairs, filter_pair, 0)
    carried = None
    for r in range(GROUP):
        mine = jnp.concatenate(
            [waves[p, r * rows : (r + 1) * rows, :] for p in range(pairs)], axis=0
        )
        wide = dot3(split_value(mine), (back_hi[r], back_lo[r]))
        first = wide[:, :LANES] if carried is None else wide[:, :LANES] + carried
        carried = wide[:, LANES:]
        result[pl.ds(r, pairs * rows, stride=LINES), :] = first
    result[pl.ds(GROUP, pairs * rows, stride=LINES), :] = carried
    for k in range(planes):
        slab = partner(me, k, planes) * lines
        for p in range(pairs):
            outs[k][pl.ds(p * lines, lines), :] = result[pl.ds(p * whole + slab, lines), :]


def shares_for(slots, planes):
    shares = EARLY + LATE
    units = slots // planes
    cuts = [units * sum(shares[: i + 1]) // sum(shares) for i in range(len(shares))]
    sizes = [(b - a) * planes for a, b in zip([0] + cuts, cuts)]
    return sizes, sum(sizes[len(EARLY) :])


def params():
    return pltpu.CompilerParams(vmem_limit_bytes=VMEM_LIMIT)


def cost(microseconds, flops=0):
    moved = int(microseconds * 1e3)
    return pl.CostEstimate(flops=flops, bytes_accessed=moved, transcendentals=0)


def floats(rows):
    return jax.ShapeDtypeStruct((rows, LANES), jnp.float32)


def partner(i, k, size):
    return i ^ k if size & (size - 1) == 0 else (k - i) % size


def exchange(parts, size):
    return [parts[0] if size & (size - 1) == 0 else lax.ppermute(parts[0], "plane", pairs_of(0, size))] + [
        lax.ppermute(parts[k], "plane", pairs_of(k, size)) for k in range(1, size)
    ]


def pairs_of(k, size):
    return [(i, partner(i, k, size)) for i in range(size)]


def local(orbitals, kernel_half, pair_own, pair_step, pair_remote, pair_count):
    groups, blocks, planes = (lax.axis_size(name) for name in ("groups", "blk", "plane"))
    orbs, depth, cell_count = orbitals.shape
    slots = pair_own.shape[0]
    lines = cell_count // LANES
    flat = orbitals.reshape(orbs * lines, LANES)
    shares, late = shares_for(slots, planes)

    width = -(-(slots + 1) // LANES) * LANES
    *requests, known = pl.pallas_call(
        functools.partial(plan_kernel, slots, orbs, late),
        out_shape=(
            *[jax.ShapeDtypeStruct((width,), jnp.int32)] * STEPS,
            jax.ShapeDtypeStruct((3 * slots,), jnp.int32),
        ),
        in_specs=[smem] * 4,
        out_specs=(smem,) * (STEPS + 1),
        scratch_shapes=[
            pltpu.SMEM((STEPS * orbs,), jnp.int32),
            pltpu.SMEM((slots + STEPS,), jnp.int32),
        ],
        cost_estimate=cost(2.3),
        name="plan",
    )(pair_own, pair_step, pair_remote, pair_count)

    wanted = [lax.ppermute(requests[s], "blk", route(-s - 1, blocks)) for s in range(STEPS)]

    def send(low, high, flat, wanted, before=()):
        packs = [
            pl.pallas_call(
                functools.partial(pack_kernel, lines, low, high),
                out_shape=floats((high - low) * lines),
                in_specs=[smem, vmem] + [hbm] * len(before[s : s + 1]),
                out_specs=vmem,
                compiler_params=params(),
                cost_estimate=cost(0.5),
                name="pack",
            )(wanted[s], flat, *before[s : s + 1])
            for s in range(STEPS)
        ]
        return packs, [lax.ppermute(packs[s], "blk", route(s + 1, blocks)) for s in range(STEPS)]

    def make_density(bounds, base, size, place, owned, received, after):
        each = size // planes
        return pl.pallas_call(
            functools.partial(density_kernel, slots, lines, planes, bounds, base, size),
            out_shape=[floats(each * lines)] * planes + [floats(size * lines)],
            in_specs=[smem, vmem] + [vmem] * len(received) + [hbm] * len(after),
            out_specs=[vmem] * (planes + 1),
            compiler_params=params(),
            cost_estimate=cost(0.05 * size),
            name="density",
        )(place, owned, *received, *after)

    def filter_parts(parts, kernel, tables):
        each = parts[0].shape[0] // lines
        backs = pl.pallas_call(
            functools.partial(transform_kernel, each, lines, planes),
            out_shape=[floats(each * lines)] * planes,
            in_specs=[vmem] * (planes + 9),
            out_specs=[vmem] * planes,
            scratch_shapes=[
                pltpu.VMEM((each * planes * lines, LANES), jnp.float32),
                pltpu.VMEM((each, NG, NG), jnp.float32),
                pltpu.VMEM((each * planes * lines, LANES), jnp.float32),
            ],
            compiler_params=params(),
            cost_estimate=cost(0.5 + 0.4 * each),
            name="transform",
        )(*exchange(parts, planes), *tables, kernel)
        return backs

    def add_up(base, size, place, kept, potentials, before):
        return pl.pallas_call(
            functools.partial(sum_kernel, slots, lines, planes, base, size, not before),
            out_shape=floats(orbs * lines),
            in_specs=[smem] + [vmem] * (planes + 1 + len(before)),
            out_specs=vmem,
            compiler_params=params(),
            cost_estimate=cost(0.9),
            name="sum",
        )(place, kept, *potentials, *before)

    def own_rows(c, place, flat):
        return pl.pallas_call(
            functools.partial(own_kernel, slots, lines, sum(shares[:c]), shares[c]),
            out_shape=floats(shares[c] * lines),
            in_specs=[smem, vmem],
            out_specs=vmem,
            compiler_params=params(),
            cost_estimate=cost(0.5),
            name="own",
        )(place, flat)

    def one_chunk(bounds, c, place, owned, kernel, tables, received, before, after=()):
        base, size = sum(shares[:c]), shares[c]
        *parts, kept = make_density(bounds, base, size, place, owned[c], received, after)
        backs = filter_parts(parts, kernel, tables)
        return add_up(base, size, place, kept, exchange(backs, planes), before)

    packs, first = send(0, FIRST, flat, wanted)
    place, choice = pl.pallas_call(
        functools.partial(place_kernel, slots, planes, shares),
        out_shape=(
            jax.ShapeDtypeStruct((3 * slots,), jnp.int32),
            jax.ShapeDtypeStruct((1,), jnp.int32),
        ),
        in_specs=[smem] * (STEPS + 2) + [hbm] * STEPS,
        out_specs=(smem, smem),
        scratch_shapes=[pltpu.SMEM((slots,), jnp.int32), pltpu.SMEM((2,), jnp.int32)],
        cost_estimate=cost(2.8),
        name="place",
    )(known, requests[0], *wanted, *packs)
    owned = [own_rows(c, place, flat) for c in range(len(shares))]
    kernel = pl.pallas_call(
        expand_kernel,
        out_shape=jax.ShapeDtypeStruct((NG, NG), jnp.float32),
        in_specs=[vmem],
        out_specs=vmem,
        cost_estimate=cost(1.4),
        name="expand",
    )(kernel_half)
    if is_ring(blocks) and groups == 2:
        choice = jnp.maximum(choice, lax.ppermute(choice, "groups", [(0, 1), (1, 0)]))
    else:
        choice = lax.pmax(choice, ("groups", "blk"))
    tables = [jnp.asarray(part) for pair in make_tables(NG // planes) for part in pair]

    def finish(total, flat, wanted, place, owned, kernel, tables, first):
        cuts = [FIRST + (total - FIRST) * i // PARTS for i in range(PARTS + 1)]
        packs, rows = None, [first]
        for low, high in zip(cuts, cuts[1:]):
            made, got = send(low, high, flat, wanted, rows[-1] if packs else ())
            packs = packs or made
            rows.append(got)
        summed, after = [], packs
        for c in range(len(shares)):
            early = c < len(EARLY)
            bounds = (FIRST,) if early else tuple(cuts)
            got = first if early else sum(rows, [])
            summed = [one_chunk(bounds, c, place, owned, kernel, tables, got, summed, after)]
            if c + 1 == len(EARLY):
                after = summed
        return summed[0]

    def general(flat, wanted, place, owned, kernel, tables, first):
        rows = send(0, slots, flat, wanted)[1]
        summed = []
        for c in range(len(shares)):
            summed = [one_chunk((slots,), c, place, owned, kernel, tables, rows, summed)]
        return summed[0]

    summed = lax.switch(
        choice[0],
        [functools.partial(finish, total) for total in TOTALS] + [general],
        flat,
        wanted,
        place,
        owned,
        kernel,
        tables,
        first,
    )
    return summed.reshape(orbs, depth, cell_count)


def solution(mesh):
    in_specs = (
        P(("groups", "blk"), None, "plane"),
        P(),
        P(("groups", "blk")),
        P(("groups", "blk")),
        P(("groups", "blk")),
        P(("groups", "blk")),
    )
    out_specs = P(("groups", "blk"), None, "plane")
    return jax.shard_map(local, mesh=mesh, in_specs=in_specs, out_specs=out_specs, check_vma=False)
```

```python
import functools

import jax
import jax.numpy as jnp
import ml_dtypes
import numpy as np
from jax import lax
from jax.experimental import pallas as pl
from jax.experimental.pallas import tpu as pltpu
from jax.sharding import PartitionSpec as P

NG = 160
STEPS = 3
LANES = 128
GROUP = 4
LINES = 5
FIRST = 7
TOTALS = (17, 19, 21, 24)
EARLY = (5,)
LATE = (4, 3)

VMEM_LIMIT = 48 * 1024 * 1024
highest = lax.Precision.HIGHEST
smem = pl.BlockSpec(memory_space=pltpu.SMEM)
vmem = pl.BlockSpec(memory_space=pltpu.VMEM)
hbm = pl.BlockSpec(memory_space=pl.ANY)


def split_table(table):
    high = table.astype(ml_dtypes.bfloat16)
    low = (table - high.astype(np.float64)).astype(ml_dtypes.bfloat16)
    return high, low


def make_tables(x_local):
    positions = np.arange(NG)
    angles = 2.0 * np.pi / NG * (positions[:, None] * positions[None, :] % NG)
    cas = np.cos(angles) + np.sin(angles)
    into = np.zeros((GROUP, 2 * LANES, NG))
    for r in range(GROUP):
        start = r * NG - r * LANES
        into[r, start : start + NG] = cas
    back = np.transpose(into, (0, 2, 1)).copy()
    order = np.arange(NG).reshape(NG // GROUP, GROUP).T.reshape(-1)
    mixed = cas[:, order]
    return split_table(into), split_table(back), split_table(mixed), split_table(mixed.T.copy())


def split_value(value):
    high = value.astype(jnp.bfloat16)
    low = (value - high.astype(jnp.float32)).astype(jnp.bfloat16)
    return high, low


def dot(a, b):
    return lax.dot_general(a, b, (((1,), (0,)), ((), ())), preferred_element_type=jnp.float32)


def dot3(a, b):
    return dot(a[0], b[0]) + (dot(a[0], b[1]) + dot(a[1], b[0]))


def is_ring(blocks):
    return blocks == STEPS + 1


def route(shift, blocks):
    return [(i, (i + shift) % blocks) for i in range(blocks)]


def plan_kernel(slots, orbs, late, own, step, remote, count, *refs):
    requests, (known, seen, hist) = refs[:STEPS], refs[STEPS:]
    for s in range(STEPS):
        for k in range(slots):
            requests[s][k] = 0
    for s in range(STEPS):
        hist[slots + s] = 0
        for k in range(orbs):
            seen[s * orbs + k] = -1
    for k in range(slots):
        hist[k] = 0

    def visit(j, carry):
        live = j < count[0]
        s = jnp.where(live, step[j], 0)
        k = remote[j]
        at = seen[s * orbs + k]
        used = hist[slots + s]
        rank = jnp.where(at < 0, used, at)

        @pl.when(live & (at < 0))
        def _():
            for i in range(STEPS):

                @pl.when(s == i)
                def _():
                    requests[i][used] = k

            seen[s * orbs + k] = used
            hist[slots + s] = used + 1

        @pl.when(live)
        def _():
            hist[rank] += 1

        known[j] = s
        known[slots + j] = jnp.where(live, rank, 0)
        known[2 * slots + j] = jnp.where(live, own[j], -1)
        return carry

    lax.fori_loop(0, slots, visit, 0)
    beyond = [jnp.int32(0)]
    for k in reversed(range(slots)):
        beyond.append(beyond[-1] + hist[k])
    beyond = beyond[::-1]
    fits = (beyond[FIRST] <= late) & (beyond[TOTALS[-1]] == 0)
    least = sum((beyond[total] > 0).astype(jnp.int32) for total in TOTALS[:-1])
    for s in range(STEPS):
        requests[s][slots] = jnp.where(fits, least, len(TOTALS))


def expand_kernel(half, full):
    rows, columns = full.shape[0], half.shape[1]
    place = lax.broadcasted_iota(jnp.int32, (rows, columns), 0)
    folded = jnp.minimum(place, rows - place)
    picker = (folded == lax.broadcasted_iota(jnp.int32, (rows, columns), 1)).astype(jnp.float32)
    tall = lax.dot_general(
        picker,
        half[0],
        (((1,), (0,)), ((), ())),
        precision=highest,
        preferred_element_type=jnp.float32,
    )
    full[...] = lax.dot_general(
        tall,
        picker,
        (((1,), (1,)), ((), ())),
        precision=highest,
        preferred_element_type=jnp.float32,
    ) * (1.0 / (NG * NG))


def place_kernel(slots, planes, shares, known, *refs):
    place, choice, order, start = refs[-4:]
    largest = refs[0][slots]
    for s in range(1, STEPS + 1):
        largest = jnp.maximum(largest, refs[s][slots])
    choice[0] = largest
    start[0] = 0

    def tally(j, count):
        return count + (known[slots + j] < FIRST).astype(jnp.int32)

    def visit(j, carry):
        chunk = (known[slots + j] >= FIRST).astype(jnp.int32)
        at = start[chunk]
        start[chunk] = at + 1
        order[at] = j
        return carry

    start[1] = lax.fori_loop(0, slots, tally, jnp.int32(0))
    lax.fori_loop(0, slots, visit, 0)
    me = lax.axis_index("plane")
    base = 0
    for size in shares:
        each = size // planes
        for k in range(planes):
            first = base + partner(me, k, planes) * each
            for q in range(each):
                j = order[first + q]
                to = base + k * each + q
                for part in range(3):
                    place[part * slots + to] = known[part * slots + j]
        base += size


def pack_kernel(lines, low, high, wanted, orbitals, sent):
    for c in range(low, high):
        row = wanted[c] * lines
        sent[pl.ds((c - low) * lines, lines), :] = orbitals[pl.ds(row, lines), :]


def own_kernel(slots, lines, base, size, place, orbitals, owned):
    for j in range(size):
        near = jnp.maximum(place[2 * slots + base + j], 0) * lines
        owned[pl.ds(j * lines, lines), :] = orbitals[pl.ds(near, lines), :]


def density_kernel(slots, lines, planes, bounds, base, size, place, owned, *refs):
    received, parts, kept = refs[: STEPS * len(bounds)], refs[-planes - 1 : -1], refs[-1]
    each = size // planes
    for j in range(size):
        s, rank = place[base + j], place[slots + base + j]
        for c, (low, high) in enumerate(zip((0,) + bounds, bounds)):
            row = jnp.clip(rank - low, 0, high - low - 1) * lines
            found = received[c * STEPS][pl.ds(row, lines), :]
            for i in range(1, STEPS):
                found = jnp.where(s == i, received[c * STEPS + i][pl.ds(row, lines), :], found)
            value = found if c == 0 else jnp.where(rank >= low, found, value)
        kept[pl.ds(j * lines, lines), :] = value
        parts[j // each][pl.ds(j % each * lines, lines), :] = (
            owned[pl.ds(j * lines, lines), :] * value
        )


def sum_kernel(slots, lines, planes, base, size, fresh, place, *refs):
    kept, parts = refs[0], refs[1 : 1 + planes]
    out = refs[-1]
    if fresh:
        out[...] = jnp.zeros_like(out)
    else:
        out[...] = refs[1 + planes][...]
    each = size // planes
    for j in range(size):
        near = place[2 * slots + base + j] * lines

        @pl.when(near >= 0)
        def _():
            out[pl.ds(near, lines), :] += (
                parts[j // each][pl.ds(j % each * lines, lines), :]
                * kept[pl.ds(j * lines, lines), :]
            )


def transform_kernel(pairs, lines, planes, *refs):
    parts = refs[:planes]
    into_hi, into_lo, back_hi, back_lo, mix_hi, mix_lo, unmix_hi, unmix_lo, kernel = refs[
        planes : planes + 9
    ]
    outs = refs[planes + 9 : 2 * planes + 9]
    cells, waves, result = refs[2 * planes + 9 :]
    whole = planes * lines
    rows = NG // GROUP
    me = lax.axis_index("plane")
    for k in range(planes):
        slab = partner(me, k, planes) * lines
        for p in range(pairs):
            cells[pl.ds(p * whole + slab, lines), :] = parts[k][pl.ds(p * lines, lines), :]
    line = [split_value(cells[pl.ds(t, pairs * rows, stride=LINES), :]) for t in range(LINES)]
    for r in range(GROUP):
        wide = [jnp.concatenate([line[r][i], line[r + 1][i]], axis=1) for i in range(2)]
        found = dot3(wide, (into_hi[r], into_lo[r]))
        for p in range(pairs):
            waves[p, r * rows : (r + 1) * rows, :] = found[p * rows : (p + 1) * rows, :]
    mix = (mix_hi[...], mix_lo[...])
    unmix = (unmix_hi[...], unmix_lo[...])
    together = 3 if pairs % 3 == 0 else 1

    def filter_some(i, carry):
        for p in range(together):
            at = i * together + p
            spectrum = dot3(mix, split_value(waves[at])) * kernel[...]
            waves[at] = dot3(unmix, split_value(spectrum))
        return carry

    lax.fori_loop(0, pairs // together, filter_some, 0)
    carried = None
    for r in range(GROUP):
        mine = jnp.concatenate(
            [waves[p, r * rows : (r + 1) * rows, :] for p in range(pairs)], axis=0
        )
        wide = dot3(split_value(mine), (back_hi[r], back_lo[r]))
        first = wide[:, :LANES] if carried is None else wide[:, :LANES] + carried
        carried = wide[:, LANES:]
        result[pl.ds(r, pairs * rows, stride=LINES), :] = first
    result[pl.ds(GROUP, pairs * rows, stride=LINES), :] = carried
    for k in range(planes):
        slab = partner(me, k, planes) * lines
        for p in range(pairs):
            outs[k][pl.ds(p * lines, lines), :] = result[pl.ds(p * whole + slab, lines), :]


def shares_for(slots, planes):
    shares = EARLY + LATE
    units = slots // planes
    cuts = [units * sum(shares[: i + 1]) // sum(shares) for i in range(len(shares))]
    sizes = [(b - a) * planes for a, b in zip([0] + cuts, cuts)]
    return sizes, sum(sizes[len(EARLY) :])


def params():
    return pltpu.CompilerParams(vmem_limit_bytes=VMEM_LIMIT)


def cost(microseconds, flops=0):
    moved = int(microseconds * 1e3)
    return pl.CostEstimate(flops=flops, bytes_accessed=moved, transcendentals=0)


def floats(rows):
    return jax.ShapeDtypeStruct((rows, LANES), jnp.float32)


def partner(i, k, size):
    return i ^ k if size & (size - 1) == 0 else (k - i) % size


def exchange(parts, size):
    return [parts[0] if size & (size - 1) == 0 else lax.ppermute(parts[0], "plane", pairs_of(0, size))] + [
        lax.ppermute(parts[k], "plane", pairs_of(k, size)) for k in range(1, size)
    ]


def pairs_of(k, size):
    return [(i, partner(i, k, size)) for i in range(size)]


def local(orbitals, kernel_half, pair_own, pair_step, pair_remote, pair_count):
    groups, blocks, planes = (lax.axis_size(name) for name in ("groups", "blk", "plane"))
    orbs, depth, cell_count = orbitals.shape
    slots = pair_own.shape[0]
    lines = cell_count // LANES
    flat = orbitals.reshape(orbs * lines, LANES)
    shares, late = shares_for(slots, planes)

    width = -(-(slots + 1) // LANES) * LANES
    *requests, known = pl.pallas_call(
        functools.partial(plan_kernel, slots, orbs, late),
        out_shape=(
            *[jax.ShapeDtypeStruct((width,), jnp.int32)] * STEPS,
            jax.ShapeDtypeStruct((3 * slots,), jnp.int32),
        ),
        in_specs=[smem] * 4,
        out_specs=(smem,) * (STEPS + 1),
        scratch_shapes=[
            pltpu.SMEM((STEPS * orbs,), jnp.int32),
            pltpu.SMEM((slots + STEPS,), jnp.int32),
        ],
        cost_estimate=cost(2.3),
        name="plan",
    )(pair_own, pair_step, pair_remote, pair_count)

    wanted = [lax.ppermute(requests[s], "blk", route(-s - 1, blocks)) for s in range(STEPS)]

    def send(low, high, flat, wanted):
        packs = [
            pl.pallas_call(
                functools.partial(pack_kernel, lines, low, high),
                out_shape=floats((high - low) * lines),
                in_specs=[smem, vmem],
                out_specs=vmem,
                compiler_params=params(),
                cost_estimate=cost(0.5),
                name="pack",
            )(wanted[s], flat)
            for s in range(STEPS)
        ]
        return packs, [lax.ppermute(packs[s], "blk", route(s + 1, blocks)) for s in range(STEPS)]

    def make_density(bounds, base, size, place, owned, received, after):
        each = size // planes
        return pl.pallas_call(
            functools.partial(density_kernel, slots, lines, planes, bounds, base, size),
            out_shape=[floats(each * lines)] * planes + [floats(size * lines)],
            in_specs=[smem, vmem] + [vmem] * len(received) + [hbm] * len(after),
            out_specs=[vmem] * (planes + 1),
            compiler_params=params(),
            cost_estimate=cost(0.05 * size),
            name="density",
        )(place, owned, *received, *after)

    def filter_parts(parts, kernel, tables):
        each = parts[0].shape[0] // lines
        backs = pl.pallas_call(
            functools.partial(transform_kernel, each, lines, planes),
            out_shape=[floats(each * lines)] * planes,
            in_specs=[vmem] * (planes + 9),
            out_specs=[vmem] * planes,
            scratch_shapes=[
                pltpu.VMEM((each * planes * lines, LANES), jnp.float32),
                pltpu.VMEM((each, NG, NG), jnp.float32),
                pltpu.VMEM((each * planes * lines, LANES), jnp.float32),
            ],
            compiler_params=params(),
            cost_estimate=cost(0.5 + 0.4 * each),
            name="transform",
        )(*exchange(parts, planes), *tables, kernel)
        return backs

    def add_up(base, size, place, kept, potentials, before):
        return pl.pallas_call(
            functools.partial(sum_kernel, slots, lines, planes, base, size, not before),
            out_shape=floats(orbs * lines),
            in_specs=[smem] + [vmem] * (planes + 1 + len(before)),
            out_specs=vmem,
            compiler_params=params(),
            cost_estimate=cost(0.9),
            name="sum",
        )(place, kept, *potentials, *before)

    def own_rows(c, place, flat):
        return pl.pallas_call(
            functools.partial(own_kernel, slots, lines, sum(shares[:c]), shares[c]),
            out_shape=floats(shares[c] * lines),
            in_specs=[smem, vmem],
            out_specs=vmem,
            compiler_params=params(),
            cost_estimate=cost(0.5),
            name="own",
        )(place, flat)

    def one_chunk(bounds, c, place, owned, kernel, tables, received, before, after=()):
        base, size = sum(shares[:c]), shares[c]
        *parts, kept = make_density(bounds, base, size, place, owned[c], received, after)
        backs = filter_parts(parts, kernel, tables)
        potentials = exchange(backs, planes)
        return add_up(base, size, place, kept, potentials, before), potentials

    packs, first = send(0, FIRST, flat, wanted)
    place, choice = pl.pallas_call(
        functools.partial(place_kernel, slots, planes, shares),
        out_shape=(
            jax.ShapeDtypeStruct((3 * slots,), jnp.int32),
            jax.ShapeDtypeStruct((1,), jnp.int32),
        ),
        in_specs=[smem] * (STEPS + 2) + [hbm] * STEPS,
        out_specs=(smem, smem),
        scratch_shapes=[pltpu.SMEM((slots,), jnp.int32), pltpu.SMEM((2,), jnp.int32)],
        cost_estimate=cost(2.8),
        name="place",
    )(known, requests[0], *wanted, *packs)
    owned = [own_rows(c, place, flat) for c in range(len(shares))]
    kernel = pl.pallas_call(
        expand_kernel,
        out_shape=jax.ShapeDtypeStruct((NG, NG), jnp.float32),
        in_specs=[vmem],
        out_specs=vmem,
        cost_estimate=cost(1.4),
        name="expand",
    )(kernel_half)
    if is_ring(blocks) and groups == 2:
        choice = jnp.maximum(choice, lax.ppermute(choice, "groups", [(0, 1), (1, 0)]))
    else:
        choice = lax.pmax(choice, ("groups", "blk"))
    tables = [jnp.asarray(part) for pair in make_tables(NG // planes) for part in pair]

    def finish(total, flat, wanted, place, owned, kernel, tables, first):
        packs, later = send(FIRST, total, flat, wanted)
        summed, after, formed = [], packs, []
        for c in range(len(shares)):
            early = c < len(EARLY)
            bounds = (FIRST,) if early else (FIRST, total)
            rows = first if early else first + later
            result, potentials = one_chunk(
                bounds, c, place, owned, kernel, tables, rows, summed, after
            )
            summed = [result]
            if early:
                formed += potentials[2:]
            if c + 1 == len(EARLY):
                after = formed
        return summed[0]

    def general(flat, wanted, place, owned, kernel, tables, first):
        rows = send(0, slots, flat, wanted)[1]
        summed = []
        for c in range(len(shares)):
            summed = [one_chunk((slots,), c, place, owned, kernel, tables, rows, summed)[0]]
        return summed[0]

    summed = lax.switch(
        choice[0],
        [functools.partial(finish, total) for total in TOTALS] + [general],
        flat,
        wanted,
        place,
        owned,
        kernel,
        tables,
        first,
    )
    return summed.reshape(orbs, depth, cell_count)


def solution(mesh):
    in_specs = (
        P(("groups", "blk"), None, "plane"),
        P(),
        P(("groups", "blk")),
        P(("groups", "blk")),
        P(("groups", "blk")),
        P(("groups", "blk")),
    )
    out_specs = P(("groups", "blk"), None, "plane")
    return jax.shard_map(local, mesh=mesh, in_specs=in_specs, out_specs=out_specs, check_vma=False)
```

```python
import functools

import jax
import jax.numpy as jnp
import ml_dtypes
import numpy as np
from jax import lax
from jax.experimental import pallas as pl
from jax.experimental.pallas import tpu as pltpu
from jax.sharding import PartitionSpec as P

NG = 160
STEPS = 3
LANES = 128
GROUP = 4
LINES = 5
FIRST = 8
TOTALS = (17, 19, 21, 24)
EARLY = (6,)
LATE = (3, 3)

VMEM_LIMIT = 48 * 1024 * 1024
highest = lax.Precision.HIGHEST
smem = pl.BlockSpec(memory_space=pltpu.SMEM)
vmem = pl.BlockSpec(memory_space=pltpu.VMEM)
hbm = pl.BlockSpec(memory_space=pl.ANY)


def split_table(table):
    high = table.astype(ml_dtypes.bfloat16)
    low = (table - high.astype(np.float64)).astype(ml_dtypes.bfloat16)
    return high, low


def make_tables(x_local):
    positions = np.arange(NG)
    angles = 2.0 * np.pi / NG * (positions[:, None] * positions[None, :] % NG)
    cas = np.cos(angles) + np.sin(angles)
    into = np.zeros((GROUP, 2 * LANES, NG))
    for r in range(GROUP):
        start = r * NG - r * LANES
        into[r, start : start + NG] = cas
    back = np.transpose(into, (0, 2, 1)).copy()
    order = np.arange(NG).reshape(NG // GROUP, GROUP).T.reshape(-1)
    mixed = cas[:, order]
    return split_table(into), split_table(back), split_table(mixed), split_table(mixed.T.copy())


def split_value(value):
    high = value.astype(jnp.bfloat16)
    low = (value - high.astype(jnp.float32)).astype(jnp.bfloat16)
    return high, low


def dot(a, b):
    return lax.dot_general(a, b, (((1,), (0,)), ((), ())), preferred_element_type=jnp.float32)


def dot3(a, b):
    return dot(a[0], b[0]) + (dot(a[0], b[1]) + dot(a[1], b[0]))


def is_ring(blocks):
    return blocks == STEPS + 1


def route(shift, blocks):
    return [(i, (i + shift) % blocks) for i in range(blocks)]


def plan_kernel(slots, orbs, late, own, step, remote, count, *refs):
    requests, (known, seen, hist) = refs[:STEPS], refs[STEPS:]
    for s in range(STEPS):
        for k in range(slots):
            requests[s][k] = 0
    for s in range(STEPS):
        hist[slots + s] = 0
        for k in range(orbs):
            seen[s * orbs + k] = -1
    for k in range(slots):
        hist[k] = 0

    def visit(j, carry):
        live = j < count[0]
        s = jnp.where(live, step[j], 0)
        k = remote[j]
        at = seen[s * orbs + k]
        used = hist[slots + s]
        rank = jnp.where(at < 0, used, at)

        @pl.when(live & (at < 0))
        def _():
            for i in range(STEPS):

                @pl.when(s == i)
                def _():
                    requests[i][used] = k

            seen[s * orbs + k] = used
            hist[slots + s] = used + 1

        @pl.when(live)
        def _():
            hist[rank] += 1

        known[j] = s
        known[slots + j] = jnp.where(live, rank, 0)
        known[2 * slots + j] = jnp.where(live, own[j], -1)
        return carry

    lax.fori_loop(0, slots, visit, 0)
    beyond = [jnp.int32(0)]
    for k in reversed(range(slots)):
        beyond.append(beyond[-1] + hist[k])
    beyond = beyond[::-1]
    fits = (beyond[FIRST] <= late) & (beyond[TOTALS[-1]] == 0)
    least = sum((beyond[total] > 0).astype(jnp.int32) for total in TOTALS[:-1])
    for s in range(STEPS):
        requests[s][slots] = jnp.where(fits, least, len(TOTALS))


def expand_kernel(half, full):
    rows, columns = full.shape[0], half.shape[1]
    place = lax.broadcasted_iota(jnp.int32, (rows, columns), 0)
    folded = jnp.minimum(place, rows - place)
    picker = (folded == lax.broadcasted_iota(jnp.int32, (rows, columns), 1)).astype(jnp.float32)
    tall = lax.dot_general(
        picker,
        half[0],
        (((1,), (0,)), ((), ())),
        precision=highest,
        preferred_element_type=jnp.float32,
    )
    full[...] = lax.dot_general(
        tall,
        picker,
        (((1,), (1,)), ((), ())),
        precision=highest,
        preferred_element_type=jnp.float32,
    ) * (1.0 / (NG * NG))


def place_kernel(slots, planes, shares, known, *refs):
    place, choice, order, start = refs[-4:]
    largest = refs[0][slots]
    for s in range(1, STEPS + 1):
        largest = jnp.maximum(largest, refs[s][slots])
    choice[0] = largest
    start[0] = 0

    def tally(j, count):
        return count + (known[slots + j] < FIRST).astype(jnp.int32)

    def visit(j, carry):
        chunk = (known[slots + j] >= FIRST).astype(jnp.int32)
        at = start[chunk]
        start[chunk] = at + 1
        order[at] = j
        return carry

    start[1] = lax.fori_loop(0, slots, tally, jnp.int32(0))
    lax.fori_loop(0, slots, visit, 0)
    me = lax.axis_index("plane")
    base = 0
    for size in shares:
        each = size // planes
        for k in range(planes):
            first = base + partner(me, k, planes) * each
            for q in range(each):
                j = order[first + q]
                to = base + k * each + q
                for part in range(3):
                    place[part * slots + to] = known[part * slots + j]
        base += size


def pack_kernel(lines, low, high, wanted, orbitals, sent):
    for c in range(low, high):
        row = wanted[c] * lines
        sent[pl.ds((c - low) * lines, lines), :] = orbitals[pl.ds(row, lines), :]


def packs_kernel(lines, *refs):
    wanted, orbitals, sent = refs[:STEPS], refs[STEPS], refs[STEPS + 1 :]
    for s in range(STEPS):
        for c in range(FIRST, TOTALS[-1]):
            row = orbitals[pl.ds(wanted[s][c] * lines, lines), :]
            for i, total in enumerate(TOTALS):
                if c < total:
                    sent[i * STEPS + s][pl.ds((c - FIRST) * lines, lines), :] = row


def own_kernel(slots, lines, base, size, place, orbitals, owned):
    for j in range(size):
        near = jnp.maximum(place[2 * slots + base + j], 0) * lines
        owned[pl.ds(j * lines, lines), :] = orbitals[pl.ds(near, lines), :]


def density_kernel(slots, lines, planes, bounds, base, size, place, owned, *refs):
    received, parts, kept = refs[: STEPS * len(bounds)], refs[-planes - 1 : -1], refs[-1]
    each = size // planes
    for j in range(size):
        s, rank = place[base + j], place[slots + base + j]
        for c, (low, high) in enumerate(zip((0,) + bounds, bounds)):
            row = jnp.clip(rank - low, 0, high - low - 1) * lines
            found = received[c * STEPS][pl.ds(row, lines), :]
            for i in range(1, STEPS):
                found = jnp.where(s == i, received[c * STEPS + i][pl.ds(row, lines), :], found)
            value = found if c == 0 else jnp.where(rank >= low, found, value)
        kept[pl.ds(j * lines, lines), :] = value
        parts[j // each][pl.ds(j % each * lines, lines), :] = (
            owned[pl.ds(j * lines, lines), :] * value
        )


def sum_kernel(slots, lines, planes, base, size, fresh, place, *refs):
    kept, parts = refs[0], refs[1 : 1 + planes]
    out = refs[-1]
    if fresh:
        out[...] = jnp.zeros_like(out)
    else:
        out[...] = refs[1 + planes][...]
    each = size // planes
    for j in range(size):
        near = place[2 * slots + base + j] * lines

        @pl.when(near >= 0)
        def _():
            out[pl.ds(near, lines), :] += (
                parts[j // each][pl.ds(j % each * lines, lines), :]
                * kept[pl.ds(j * lines, lines), :]
            )


def transform_kernel(pairs, lines, planes, *refs):
    parts = refs[:planes]
    into_hi, into_lo, back_hi, back_lo, mix_hi, mix_lo, unmix_hi, unmix_lo, kernel = refs[
        planes : planes + 9
    ]
    outs = refs[planes + 9 : 2 * planes + 9]
    cells, waves, result = refs[2 * planes + 9 :]
    whole = planes * lines
    rows = NG // GROUP
    me = lax.axis_index("plane")
    for k in range(planes):
        slab = partner(me, k, planes) * lines
        for p in range(pairs):
            cells[pl.ds(p * whole + slab, lines), :] = parts[k][pl.ds(p * lines, lines), :]
    line = [split_value(cells[pl.ds(t, pairs * rows, stride=LINES), :]) for t in range(LINES)]
    for r in range(GROUP):
        wide = [jnp.concatenate([line[r][i], line[r + 1][i]], axis=1) for i in range(2)]
        found = dot3(wide, (into_hi[r], into_lo[r]))
        for p in range(pairs):
            waves[p, r * rows : (r + 1) * rows, :] = found[p * rows : (p + 1) * rows, :]
    mix = (mix_hi[...], mix_lo[...])
    unmix = (unmix_hi[...], unmix_lo[...])
    together = 3 if pairs % 3 == 0 else 1

    def filter_some(i, carry):
        for p in range(together):
            at = i * together + p
            spectrum = dot3(mix, split_value(waves[at])) * kernel[...]
            waves[at] = dot3(unmix, split_value(spectrum))
        return carry

    lax.fori_loop(0, pairs // together, filter_some, 0)
    carried = None
    for r in range(GROUP):
        mine = jnp.concatenate(
            [waves[p, r * rows : (r + 1) * rows, :] for p in range(pairs)], axis=0
        )
        wide = dot3(split_value(mine), (back_hi[r], back_lo[r]))
        first = wide[:, :LANES] if carried is None else wide[:, :LANES] + carried
        carried = wide[:, LANES:]
        result[pl.ds(r, pairs * rows, stride=LINES), :] = first
    result[pl.ds(GROUP, pairs * rows, stride=LINES), :] = carried
    for k in range(planes):
        slab = partner(me, k, planes) * lines
        for p in range(pairs):
            outs[k][pl.ds(p * lines, lines), :] = result[pl.ds(p * whole + slab, lines), :]


def shares_for(slots, planes):
    shares = EARLY + LATE
    units = slots // planes
    cuts = [units * sum(shares[: i + 1]) // sum(shares) for i in range(len(shares))]
    sizes = [(b - a) * planes for a, b in zip([0] + cuts, cuts)]
    return sizes, sum(sizes[len(EARLY) :])


def params():
    return pltpu.CompilerParams(vmem_limit_bytes=VMEM_LIMIT)


def cost(microseconds, flops=0):
    moved = int(microseconds * 1e3)
    return pl.CostEstimate(flops=flops, bytes_accessed=moved, transcendentals=0)


def floats(rows):
    return jax.ShapeDtypeStruct((rows, LANES), jnp.float32)


def partner(i, k, size):
    return i ^ k if size & (size - 1) == 0 else (k - i) % size


def exchange(parts, size):
    return [parts[0] if size & (size - 1) == 0 else lax.ppermute(parts[0], "plane", pairs_of(0, size))] + [
        lax.ppermute(parts[k], "plane", pairs_of(k, size)) for k in range(1, size)
    ]


def pairs_of(k, size):
    return [(i, partner(i, k, size)) for i in range(size)]


def local(orbitals, kernel_half, pair_own, pair_step, pair_remote, pair_count):
    groups, blocks, planes = (lax.axis_size(name) for name in ("groups", "blk", "plane"))
    orbs, depth, cell_count = orbitals.shape
    slots = pair_own.shape[0]
    lines = cell_count // LANES
    flat = orbitals.reshape(orbs * lines, LANES)
    shares, late = shares_for(slots, planes)

    width = -(-(slots + 1) // LANES) * LANES
    *requests, known = pl.pallas_call(
        functools.partial(plan_kernel, slots, orbs, late),
        out_shape=(
            *[jax.ShapeDtypeStruct((width,), jnp.int32)] * STEPS,
            jax.ShapeDtypeStruct((3 * slots,), jnp.int32),
        ),
        in_specs=[smem] * 4,
        out_specs=(smem,) * (STEPS + 1),
        scratch_shapes=[
            pltpu.SMEM((STEPS * orbs,), jnp.int32),
            pltpu.SMEM((slots + STEPS,), jnp.int32),
        ],
        cost_estimate=cost(2.3),
        name="plan",
    )(pair_own, pair_step, pair_remote, pair_count)

    wanted = [lax.ppermute(requests[s], "blk", route(-s - 1, blocks)) for s in range(STEPS)]

    def send(low, high, flat, wanted):
        packs = [
            pl.pallas_call(
                functools.partial(pack_kernel, lines, low, high),
                out_shape=floats((high - low) * lines),
                in_specs=[smem, vmem],
                out_specs=vmem,
                compiler_params=params(),
                cost_estimate=cost(0.5),
                name="pack",
            )(wanted[s], flat)
            for s in range(STEPS)
        ]
        return packs, [lax.ppermute(packs[s], "blk", route(s + 1, blocks)) for s in range(STEPS)]

    def make_density(bounds, base, size, place, owned, received, after):
        each = size // planes
        return pl.pallas_call(
            functools.partial(density_kernel, slots, lines, planes, bounds, base, size),
            out_shape=[floats(each * lines)] * planes + [floats(size * lines)],
            in_specs=[smem, vmem] + [vmem] * len(received) + [hbm] * len(after),
            out_specs=[vmem] * (planes + 1),
            compiler_params=params(),
            cost_estimate=cost(0.05 * size),
            name="density",
        )(place, owned, *received, *after)

    def filter_parts(parts, kernel, tables):
        each = parts[0].shape[0] // lines
        backs = pl.pallas_call(
            functools.partial(transform_kernel, each, lines, planes),
            out_shape=[floats(each * lines)] * planes,
            in_specs=[vmem] * (planes + 9),
            out_specs=[vmem] * planes,
            scratch_shapes=[
                pltpu.VMEM((each * planes * lines, LANES), jnp.float32),
                pltpu.VMEM((each, NG, NG), jnp.float32),
                pltpu.VMEM((each * planes * lines, LANES), jnp.float32),
            ],
            compiler_params=params(),
            cost_estimate=cost(0.5 + 0.4 * each),
            name="transform",
        )(*exchange(parts, planes), *tables, kernel)
        return backs

    def add_up(base, size, place, kept, potentials, before):
        return pl.pallas_call(
            functools.partial(sum_kernel, slots, lines, planes, base, size, not before),
            out_shape=floats(orbs * lines),
            in_specs=[smem] + [vmem] * (planes + 1 + len(before)),
            out_specs=vmem,
            compiler_params=params(),
            cost_estimate=cost(0.9),
            name="sum",
        )(place, kept, *potentials, *before)

    def own_rows(c, place, flat):
        return pl.pallas_call(
            functools.partial(own_kernel, slots, lines, sum(shares[:c]), shares[c]),
            out_shape=floats(shares[c] * lines),
            in_specs=[smem, vmem],
            out_specs=vmem,
            compiler_params=params(),
            cost_estimate=cost(0.5),
            name="own",
        )(place, flat)

    def one_chunk(bounds, c, place, owned, kernel, tables, received, before, after=()):
        base, size = sum(shares[:c]), shares[c]
        *parts, kept = make_density(bounds, base, size, place, owned[c], received, after)
        backs = filter_parts(parts, kernel, tables)
        potentials = exchange(backs, planes)
        return add_up(base, size, place, kept, potentials, before), potentials

    packs, first = send(0, FIRST, flat, wanted)
    place, choice = pl.pallas_call(
        functools.partial(place_kernel, slots, planes, shares),
        out_shape=(
            jax.ShapeDtypeStruct((3 * slots,), jnp.int32),
            jax.ShapeDtypeStruct((1,), jnp.int32),
        ),
        in_specs=[smem] * (STEPS + 2) + [hbm] * STEPS,
        out_specs=(smem, smem),
        scratch_shapes=[pltpu.SMEM((slots,), jnp.int32), pltpu.SMEM((2,), jnp.int32)],
        cost_estimate=cost(2.8),
        name="place",
    )(known, requests[0], *wanted, *packs)
    packed = pl.pallas_call(
        functools.partial(packs_kernel, lines),
        out_shape=[floats((t - FIRST) * lines) for t in TOTALS for s in range(STEPS)],
        in_specs=[smem] * STEPS + [vmem],
        out_specs=[vmem] * (STEPS * len(TOTALS)),
        compiler_params=params(),
        cost_estimate=cost(2),
        name="packs",
    )(*wanted, flat)
    owned = [own_rows(c, place, flat) for c in range(len(shares))]
    kernel = pl.pallas_call(
        expand_kernel,
        out_shape=jax.ShapeDtypeStruct((NG, NG), jnp.float32),
        in_specs=[vmem],
        out_specs=vmem,
        cost_estimate=cost(1.4),
        name="expand",
    )(kernel_half)
    if is_ring(blocks) and groups == 2:
        choice = jnp.maximum(choice, lax.ppermute(choice, "groups", [(0, 1), (1, 0)]))
    else:
        choice = lax.pmax(choice, ("groups", "blk"))
    tables = [jnp.asarray(part) for pair in make_tables(NG // planes) for part in pair]

    def finish(total, flat, wanted, packed, place, owned, kernel, tables, first):
        i = TOTALS.index(total)
        packs = packed[i * STEPS : (i + 1) * STEPS]
        later = [lax.ppermute(packs[s], "blk", route(s + 1, blocks)) for s in range(STEPS)]
        summed, after, formed = [], [], []
        for c in range(len(shares)):
            early = c < len(EARLY)
            bounds = (FIRST,) if early else (FIRST, total)
            rows = first if early else first + later
            result, potentials = one_chunk(
                bounds, c, place, owned, kernel, tables, rows, summed, after
            )
            summed = [result]
            if early:
                formed += potentials[2:]
            if c + 1 == len(EARLY):
                after = formed
        return summed[0]

    def general(flat, wanted, packed, place, owned, kernel, tables, first):
        rows = send(0, slots, flat, wanted)[1]
        summed = []
        for c in range(len(shares)):
            summed = [one_chunk((slots,), c, place, owned, kernel, tables, rows, summed)[0]]
        return summed[0]

    summed = lax.switch(
        choice[0],
        [functools.partial(finish, total) for total in TOTALS] + [general],
        flat,
        wanted,
        packed,
        place,
        owned,
        kernel,
        tables,
        first,
    )
    return summed.reshape(orbs, depth, cell_count)


def solution(mesh):
    in_specs = (
        P(("groups", "blk"), None, "plane"),
        P(),
        P(("groups", "blk")),
        P(("groups", "blk")),
        P(("groups", "blk")),
        P(("groups", "blk")),
    )
    out_specs = P(("groups", "blk"), None, "plane")
    return jax.shard_map(local, mesh=mesh, in_specs=in_specs, out_specs=out_specs, check_vma=False)
```

```python
import functools

import jax
import jax.numpy as jnp
import ml_dtypes
import numpy as np
from jax import lax
from jax.experimental import pallas as pl
from jax.experimental.pallas import tpu as pltpu
from jax.sharding import PartitionSpec as P

NG = 160
STEPS = 3
LANES = 128
GROUP = 4
LINES = 5
FIRST = 8
MIDDLE = 14
TOTALS = (17, 19, 21, 24)
SHARES = (6, 3, 3)

VMEM_LIMIT = 48 * 1024 * 1024
highest = lax.Precision.HIGHEST
smem = pl.BlockSpec(memory_space=pltpu.SMEM)
vmem = pl.BlockSpec(memory_space=pltpu.VMEM)
hbm = pl.BlockSpec(memory_space=pl.ANY)


def split_table(table):
    high = table.astype(ml_dtypes.bfloat16)
    low = (table - high.astype(np.float64)).astype(ml_dtypes.bfloat16)
    return high, low


def make_tables(x_local):
    positions = np.arange(NG)
    angles = 2.0 * np.pi / NG * (positions[:, None] * positions[None, :] % NG)
    cas = np.cos(angles) + np.sin(angles)
    into = np.zeros((GROUP, 2 * LANES, NG))
    for r in range(GROUP):
        start = r * NG - r * LANES
        into[r, start : start + NG] = cas
    back = np.transpose(into, (0, 2, 1)).copy()
    order = np.arange(NG).reshape(NG // GROUP, GROUP).T.reshape(-1)
    mixed = cas[:, order]
    return split_table(into), split_table(back), split_table(mixed), split_table(mixed.T.copy())


def split_value(value):
    high = value.astype(jnp.bfloat16)
    low = (value - high.astype(jnp.float32)).astype(jnp.bfloat16)
    return high, low


def dot(a, b):
    return lax.dot_general(a, b, (((1,), (0,)), ((), ())), preferred_element_type=jnp.float32)


def dot3(a, b):
    return dot(a[0], b[0]) + (dot(a[0], b[1]) + dot(a[1], b[0]))


def is_ring(blocks):
    return blocks == STEPS + 1


def route(shift, blocks):
    return [(i, (i + shift) % blocks) for i in range(blocks)]


def plan_kernel(slots, orbs, shares, own, step, remote, count, *refs):
    requests, (known, seen, hist) = refs[:STEPS], refs[STEPS:]
    for s in range(STEPS):
        for k in range(slots):
            requests[s][k] = 0
    for s in range(STEPS):
        hist[slots + s] = 0
        for k in range(orbs):
            seen[s * orbs + k] = -1
    for k in range(slots):
        hist[k] = 0

    def visit(j, carry):
        live = j < count[0]
        s = jnp.where(live, step[j], 0)
        k = remote[j]
        at = seen[s * orbs + k]
        used = hist[slots + s]
        rank = jnp.where(at < 0, used, at)

        @pl.when(live & (at < 0))
        def _():
            for i in range(STEPS):

                @pl.when(s == i)
                def _():
                    requests[i][used] = k

            seen[s * orbs + k] = used
            hist[slots + s] = used + 1

        @pl.when(live)
        def _():
            hist[rank] += 1

        known[j] = s
        known[slots + j] = jnp.where(live, rank, 0)
        known[2 * slots + j] = jnp.where(live, own[j], -1)
        return carry

    lax.fori_loop(0, slots, visit, 0)
    beyond = [jnp.int32(0)]
    for k in reversed(range(slots)):
        beyond.append(beyond[-1] + hist[k])
    beyond = beyond[::-1]
    fits = (beyond[FIRST] <= shares[1] + shares[2]) & (beyond[MIDDLE] <= shares[2])
    fits = fits & (beyond[TOTALS[-1]] == 0)
    least = sum((beyond[total] > 0).astype(jnp.int32) for total in TOTALS[:-1])
    for s in range(STEPS):
        requests[s][slots] = jnp.where(fits, least, len(TOTALS))


def expand_kernel(half, full):
    rows, columns = full.shape[0], half.shape[1]
    place = lax.broadcasted_iota(jnp.int32, (rows, columns), 0)
    folded = jnp.minimum(place, rows - place)
    picker = (folded == lax.broadcasted_iota(jnp.int32, (rows, columns), 1)).astype(jnp.float32)
    tall = lax.dot_general(
        picker,
        half[0],
        (((1,), (0,)), ((), ())),
        precision=highest,
        preferred_element_type=jnp.float32,
    )
    full[...] = lax.dot_general(
        tall,
        picker,
        (((1,), (1,)), ((), ())),
        precision=highest,
        preferred_element_type=jnp.float32,
    ) * (1.0 / (NG * NG))


def place_kernel(slots, planes, shares, known, *refs):
    place, choice, order, start = refs[-4:]
    largest = refs[0][slots]
    for s in range(1, STEPS + 1):
        largest = jnp.maximum(largest, refs[s][slots])
    choice[0] = largest
    start[0] = 0

    def tally(j, counts):
        rank = known[slots + j]
        return tuple(
            n + (rank < bound).astype(jnp.int32) for n, bound in zip(counts, (FIRST, MIDDLE))
        )

    def visit(j, carry):
        rank = known[slots + j]
        chunk = (rank >= FIRST).astype(jnp.int32) + (rank >= MIDDLE).astype(jnp.int32)
        at = start[chunk]
        start[chunk] = at + 1
        order[at] = j
        return carry

    start[1], start[2] = lax.fori_loop(0, slots, tally, (jnp.int32(0), jnp.int32(0)))
    lax.fori_loop(0, slots, visit, 0)
    me = lax.axis_index("plane")
    base = 0
    for size in shares:
        each = size // planes
        for k in range(planes):
            first = base + partner(me, k, planes) * each
            for q in range(each):
                j = order[first + q]
                to = base + k * each + q
                for part in range(3):
                    place[part * slots + to] = known[part * slots + j]
        base += size


def pack_kernel(lines, low, high, *refs):
    wanted, orbitals, sent = refs[:STEPS], refs[STEPS], refs[STEPS + 1 :]

    def pack_row(s, c):
        row = orbitals[pl.ds(wanted[s][c] * lines, lines), :]
        sent[s][pl.ds((c - low) * lines, lines), :] = row

    for s in range(STEPS):
        for c in range(low, high):
            pack_row(s, c)


def packs_kernel(lines, *refs):
    wanted, orbitals, sent = refs[:STEPS], refs[STEPS], refs[STEPS + 1 :]
    for s in range(STEPS):
        for c in range(FIRST, TOTALS[-1]):
            row = orbitals[pl.ds(wanted[s][c] * lines, lines), :]
            if c < MIDDLE:
                sent[s][pl.ds((c - FIRST) * lines, lines), :] = row
            for i, total in enumerate(TOTALS, 1):
                if MIDDLE <= c < total:
                    sent[i * STEPS + s][pl.ds((c - MIDDLE) * lines, lines), :] = row


def tie_kernel(source, earlier, target):
    target[...] = source[...]


def own_kernel(slots, lines, base, size, place, orbitals, owned):
    for j in range(size):
        near = jnp.maximum(place[2 * slots + base + j], 0) * lines
        owned[pl.ds(j * lines, lines), :] = orbitals[pl.ds(near, lines), :]


def density_kernel(slots, lines, planes, bounds, base, size, place, owned, *refs):
    received, parts, kept = refs[: STEPS * len(bounds)], refs[-planes - 1 : -1], refs[-1]
    each = size // planes
    for j in range(size):
        s, rank = place[base + j], place[slots + base + j]
        for c, (low, high) in enumerate(zip((0,) + bounds, bounds)):
            row = jnp.clip(rank - low, 0, high - low - 1) * lines
            found = received[c * STEPS][pl.ds(row, lines), :]
            for i in range(1, STEPS):
                found = jnp.where(s == i, received[c * STEPS + i][pl.ds(row, lines), :], found)
            value = found if c == 0 else jnp.where(rank >= low, found, value)
        kept[pl.ds(j * lines, lines), :] = value
        parts[j // each][pl.ds(j % each * lines, lines), :] = (
            owned[pl.ds(j * lines, lines), :] * value
        )


def sum_kernel(slots, lines, planes, base, size, fresh, place, *refs):
    kept, parts = refs[0], refs[1 : 1 + planes]
    out = refs[-1]
    if fresh:
        out[...] = jnp.zeros_like(out)
    else:
        out[...] = refs[1 + planes][...]
    each = size // planes
    for j in range(size):
        near = place[2 * slots + base + j] * lines

        @pl.when(near >= 0)
        def _():
            out[pl.ds(near, lines), :] += (
                parts[j // each][pl.ds(j % each * lines, lines), :]
                * kept[pl.ds(j * lines, lines), :]
            )


def transform_kernel(pairs, lines, planes, *refs):
    parts = refs[:planes]
    into_hi, into_lo, back_hi, back_lo, mix_hi, mix_lo, unmix_hi, unmix_lo, kernel = refs[
        planes : planes + 9
    ]
    outs = refs[planes + 9 : 2 * planes + 9]
    cells, waves, result = refs[2 * planes + 9 :]
    whole = planes * lines
    rows = NG // GROUP
    me = lax.axis_index("plane")
    for k in range(planes):
        slab = partner(me, k, planes) * lines
        for p in range(pairs):
            cells[pl.ds(p * whole + slab, lines), :] = parts[k][pl.ds(p * lines, lines), :]
    line = [split_value(cells[pl.ds(t, pairs * rows, stride=LINES), :]) for t in range(LINES)]
    for r in range(GROUP):
        wide = [jnp.concatenate([line[r][i], line[r + 1][i]], axis=1) for i in range(2)]
        found = dot3(wide, (into_hi[r], into_lo[r]))
        for p in range(pairs):
            waves[p, r * rows : (r + 1) * rows, :] = found[p * rows : (p + 1) * rows, :]
    mix = (mix_hi[...], mix_lo[...])
    unmix = (unmix_hi[...], unmix_lo[...])
    together = 3 if pairs % 3 == 0 else 1

    def filter_some(i, carry):
        for p in range(together):
            at = i * together + p
            spectrum = dot3(mix, split_value(waves[at])) * kernel[...]
            waves[at] = dot3(unmix, split_value(spectrum))
        return carry

    lax.fori_loop(0, pairs // together, filter_some, 0)
    carried = None
    for r in range(GROUP):
        mine = jnp.concatenate(
            [waves[p, r * rows : (r + 1) * rows, :] for p in range(pairs)], axis=0
        )
        wide = dot3(split_value(mine), (back_hi[r], back_lo[r]))
        first = wide[:, :LANES] if carried is None else wide[:, :LANES] + carried
        carried = wide[:, LANES:]
        result[pl.ds(r, pairs * rows, stride=LINES), :] = first
    result[pl.ds(GROUP, pairs * rows, stride=LINES), :] = carried
    for k in range(planes):
        slab = partner(me, k, planes) * lines
        for p in range(pairs):
            outs[k][pl.ds(p * lines, lines), :] = result[pl.ds(p * whole + slab, lines), :]


def shares_for(slots, planes):
    units = slots // planes
    cuts = [units * sum(SHARES[: i + 1]) // sum(SHARES) for i in range(len(SHARES))]
    return [(b - a) * planes for a, b in zip([0] + cuts, cuts)]


def params():
    return pltpu.CompilerParams(vmem_limit_bytes=VMEM_LIMIT)


def cost(microseconds, flops=0):
    moved = int(microseconds * 1e3)
    return pl.CostEstimate(flops=flops, bytes_accessed=moved, transcendentals=0)


def floats(rows):
    return jax.ShapeDtypeStruct((rows, LANES), jnp.float32)


def partner(i, k, size):
    return i ^ k if size & (size - 1) == 0 else (k - i) % size


def exchange(parts, size):
    return [parts[0] if size & (size - 1) == 0 else lax.ppermute(parts[0], "plane", pairs_of(0, size))] + [
        lax.ppermute(parts[k], "plane", pairs_of(k, size)) for k in range(1, size)
    ]


def pairs_of(k, size):
    return [(i, partner(i, k, size)) for i in range(size)]


def local(orbitals, kernel_half, pair_own, pair_step, pair_remote, pair_count):
    groups, blocks, planes = (lax.axis_size(name) for name in ("groups", "blk", "plane"))
    orbs, depth, cell_count = orbitals.shape
    slots = pair_own.shape[0]
    lines = cell_count // LANES
    flat = orbitals.reshape(orbs * lines, LANES)
    shares = shares_for(slots, planes)

    width = -(-(slots + 1) // LANES) * LANES
    *requests, known = pl.pallas_call(
        functools.partial(plan_kernel, slots, orbs, shares),
        out_shape=(
            *[jax.ShapeDtypeStruct((width,), jnp.int32)] * STEPS,
            jax.ShapeDtypeStruct((3 * slots,), jnp.int32),
        ),
        in_specs=[smem] * 4,
        out_specs=(smem,) * (STEPS + 1),
        scratch_shapes=[
            pltpu.SMEM((STEPS * orbs,), jnp.int32),
            pltpu.SMEM((slots + STEPS,), jnp.int32),
        ],
        cost_estimate=cost(2.3),
        name="plan",
    )(pair_own, pair_step, pair_remote, pair_count)

    wanted = [lax.ppermute(requests[s], "blk", route(-s - 1, blocks)) for s in range(STEPS)]

    def forward(packs):
        return [lax.ppermute(packs[s], "blk", route(s + 1, blocks)) for s in range(STEPS)]

    def tie(packed, earlier):
        return pl.pallas_call(
            tie_kernel,
            out_shape=floats(packed.shape[0]),
            in_specs=[vmem, hbm],
            out_specs=vmem,
            compiler_params=params(),
            cost_estimate=cost(0.5),
            name="tie",
        )(packed, earlier)

    def send(low, high, flat, wanted):
        packs = pl.pallas_call(
            functools.partial(pack_kernel, lines, low, high),
            out_shape=[floats((high - low) * lines)] * STEPS,
            in_specs=[smem] * STEPS + [vmem],
            out_specs=[vmem] * STEPS,
            compiler_params=params(),
            cost_estimate=cost(0.5),
            name="pack",
        )(*wanted, flat)
        return packs, forward(packs)

    def make_density(bounds, base, size, place, owned, received, after):
        each = size // planes
        return pl.pallas_call(
            functools.partial(density_kernel, slots, lines, planes, bounds, base, size),
            out_shape=[floats(each * lines)] * planes + [floats(size * lines)],
            in_specs=[smem, vmem] + [vmem] * len(received) + [hbm] * len(after),
            out_specs=[vmem] * (planes + 1),
            compiler_params=params(),
            cost_estimate=cost(0.05 * size),
            name="density",
        )(place, owned, *received, *after)

    def filter_parts(parts, kernel, tables):
        each = parts[0].shape[0] // lines
        backs = pl.pallas_call(
            functools.partial(transform_kernel, each, lines, planes),
            out_shape=[floats(each * lines)] * planes,
            in_specs=[vmem] * (planes + 9),
            out_specs=[vmem] * planes,
            scratch_shapes=[
                pltpu.VMEM((each * planes * lines, LANES), jnp.float32),
                pltpu.VMEM((each, NG, NG), jnp.float32),
                pltpu.VMEM((each * planes * lines, LANES), jnp.float32),
            ],
            compiler_params=params(),
            cost_estimate=cost(0.5 + 0.4 * each),
            name="transform",
        )(*exchange(parts, planes), *tables, kernel)
        return backs

    def add_up(base, size, place, kept, potentials, before):
        return pl.pallas_call(
            functools.partial(sum_kernel, slots, lines, planes, base, size, not before),
            out_shape=floats(orbs * lines),
            in_specs=[smem] + [vmem] * (planes + 1 + len(before)),
            out_specs=vmem,
            compiler_params=params(),
            cost_estimate=cost(0.9),
            name="sum",
        )(place, kept, *potentials, *before)

    def own_rows(c, place, flat):
        return pl.pallas_call(
            functools.partial(own_kernel, slots, lines, sum(shares[:c]), shares[c]),
            out_shape=floats(shares[c] * lines),
            in_specs=[smem, vmem],
            out_specs=vmem,
            compiler_params=params(),
            cost_estimate=cost(0.5),
            name="own",
        )(place, flat)

    def one_chunk(bounds, c, place, owned, kernel, tables, received, before, after=()):
        base, size = sum(shares[:c]), shares[c]
        *parts, kept = make_density(bounds, base, size, place, owned[c], received, after)
        backs = filter_parts(parts, kernel, tables)
        potentials = exchange(backs, planes)
        return add_up(base, size, place, kept, potentials, before), backs, potentials

    packs, first = send(0, FIRST, flat, wanted)
    place, choice = pl.pallas_call(
        functools.partial(place_kernel, slots, planes, shares),
        out_shape=(
            jax.ShapeDtypeStruct((3 * slots,), jnp.int32),
            jax.ShapeDtypeStruct((1,), jnp.int32),
        ),
        in_specs=[smem] * (STEPS + 2) + [hbm] * STEPS,
        out_specs=(smem, smem),
        scratch_shapes=[pltpu.SMEM((slots,), jnp.int32), pltpu.SMEM((3,), jnp.int32)],
        cost_estimate=cost(2.8),
        name="place",
    )(known, requests[0], *wanted, *packs)
    packed = pl.pallas_call(
        functools.partial(packs_kernel, lines),
        out_shape=[floats((MIDDLE - FIRST) * lines)] * STEPS
        + [floats((t - MIDDLE) * lines) for t in TOTALS for s in range(STEPS)],
        in_specs=[smem] * STEPS + [vmem],
        out_specs=[vmem] * (STEPS * (len(TOTALS) + 1)),
        compiler_params=params(),
        cost_estimate=cost(2),
        name="packs",
    )(*wanted, flat)
    owned = [own_rows(c, place, flat) for c in range(len(shares))]
    kernel = pl.pallas_call(
        expand_kernel,
        out_shape=jax.ShapeDtypeStruct((NG, NG), jnp.float32),
        in_specs=[vmem],
        out_specs=vmem,
        cost_estimate=cost(1.4),
        name="expand",
    )(kernel_half)
    if is_ring(blocks) and groups == 2:
        choice = jnp.maximum(choice, lax.ppermute(choice, "groups", [(0, 1), (1, 0)]))
    else:
        choice = lax.pmax(choice, ("groups", "blk"))
    tables = [jnp.asarray(part) for pair in make_tables(NG // planes) for part in pair]

    def finish(total, flat, wanted, packed, place, owned, kernel, tables, first):
        i = TOTALS.index(total) + 1
        middle = forward(packed[:STEPS])
        last = forward(
            [tie(p, m) for p, m in zip(packed[i * STEPS : (i + 1) * STEPS], middle)]
        )
        rows, bounds = [first, middle, last], (FIRST, MIDDLE, total)
        summed, after = [], []
        for c in range(len(shares)):
            result, backs, potentials = one_chunk(
                bounds[: c + 1], c, place, owned, kernel, tables, sum(rows[: c + 1], []), summed, after
            )
            summed = [result]
            after = (backs[-1:], potentials[2:])[min(c, 1)]
            held = potentials[2:]
        return summed[0]

    def general(flat, wanted, packed, place, owned, kernel, tables, first):
        rows = send(0, slots, flat, wanted)[1]
        summed = []
        for c in range(len(shares)):
            summed = [one_chunk((slots,), c, place, owned, kernel, tables, rows, summed)[0]]
        return summed[0]

    summed = lax.switch(
        choice[0],
        [functools.partial(finish, total) for total in TOTALS] + [general],
        flat,
        wanted,
        packed,
        place,
        owned,
        kernel,
        tables,
        first,
    )
    return summed.reshape(orbs, depth, cell_count)


def solution(mesh):
    in_specs = (
        P(("groups", "blk"), None, "plane"),
        P(),
        P(("groups", "blk")),
        P(("groups", "blk")),
        P(("groups", "blk")),
        P(("groups", "blk")),
    )
    out_specs = P(("groups", "blk"), None, "plane")
    return jax.shard_map(local, mesh=mesh, in_specs=in_specs, out_specs=out_specs, check_vma=False)
```

```python
import functools

import jax
import jax.numpy as jnp
import ml_dtypes
import numpy as np
from jax import lax
from jax.experimental import pallas as pl
from jax.experimental.pallas import tpu as pltpu
from jax.sharding import PartitionSpec as P

NG = 160
STEPS = 3
LANES = 128
GROUP = 4
LINES = 5
FIRST = 8
TOTALS = (17, 19, 21, 24)
EARLY = (6,)
LATE = (3, 3)

VMEM_LIMIT = 16 * 1024 * 1024
highest = lax.Precision.HIGHEST
smem = pl.BlockSpec(memory_space=pltpu.SMEM)
vmem = pl.BlockSpec(memory_space=pltpu.VMEM)
hbm = pl.BlockSpec(memory_space=pl.ANY)


def split_table(table):
    high = table.astype(ml_dtypes.bfloat16)
    low = (table - high.astype(np.float64)).astype(ml_dtypes.bfloat16)
    return high, low


def make_tables(x_local):
    positions = np.arange(NG)
    angles = 2.0 * np.pi / NG * (positions[:, None] * positions[None, :] % NG)
    cas = np.cos(angles) + np.sin(angles)
    into = np.zeros((GROUP, 2 * LANES, NG))
    for r in range(GROUP):
        start = r * NG - r * LANES
        into[r, start : start + NG] = cas
    back = np.transpose(into, (0, 2, 1)).copy()
    order = np.arange(NG).reshape(NG // GROUP, GROUP).T.reshape(-1)
    mixed = cas[:, order]
    return split_table(into), split_table(back), split_table(mixed), split_table(mixed.T.copy())


def split_value(value):
    high = value.astype(jnp.bfloat16)
    low = (value - high.astype(jnp.float32)).astype(jnp.bfloat16)
    return high, low


def dot(a, b):
    return lax.dot_general(a, b, (((1,), (0,)), ((), ())), preferred_element_type=jnp.float32)


def dot3(a, b):
    return dot(a[0], b[0]) + (dot(a[0], b[1]) + dot(a[1], b[0]))


def is_ring(blocks):
    return blocks == STEPS + 1


def route(shift, blocks):
    return [(i, (i + shift) % blocks) for i in range(blocks)]


def plan_kernel(slots, orbs, late, own, step, remote, count, *refs):
    requests, (known, seen, hist) = refs[:STEPS], refs[STEPS:]
    for s in range(STEPS):
        for k in range(slots):
            requests[s][k] = 0
    for s in range(STEPS):
        hist[slots + s] = 0
        for k in range(orbs):
            seen[s * orbs + k] = -1
    for k in range(slots):
        hist[k] = 0

    def visit(j, carry):
        live = j < count[0]
        s = jnp.where(live, step[j], 0)
        k = remote[j]
        at = seen[s * orbs + k]
        used = hist[slots + s]
        rank = jnp.where(at < 0, used, at)

        @pl.when(live & (at < 0))
        def _():
            for i in range(STEPS):

                @pl.when(s == i)
                def _():
                    requests[i][used] = k

            seen[s * orbs + k] = used
            hist[slots + s] = used + 1

        @pl.when(live)
        def _():
            hist[rank] += 1

        known[j] = s
        known[slots + j] = jnp.where(live, rank, 0)
        known[2 * slots + j] = jnp.where(live, own[j], -1)
        return carry

    lax.fori_loop(0, slots, visit, 0)
    beyond = [jnp.int32(0)]
    for k in reversed(range(slots)):
        beyond.append(beyond[-1] + hist[k])
    beyond = beyond[::-1]
    fits = (beyond[FIRST] <= late) & (beyond[TOTALS[-1]] == 0)
    least = sum((beyond[total] > 0).astype(jnp.int32) for total in TOTALS[:-1])
    for s in range(STEPS):
        requests[s][slots] = jnp.where(fits, least, len(TOTALS))


def expand_kernel(half, full):
    rows, columns = full.shape[0], half.shape[1]
    place = lax.broadcasted_iota(jnp.int32, (rows, columns), 0)
    folded = jnp.minimum(place, rows - place)
    picker = (folded == lax.broadcasted_iota(jnp.int32, (rows, columns), 1)).astype(jnp.float32)
    tall = lax.dot_general(
        picker,
        half[0],
        (((1,), (0,)), ((), ())),
        precision=highest,
        preferred_element_type=jnp.float32,
    )
    full[...] = lax.dot_general(
        tall,
        picker,
        (((1,), (1,)), ((), ())),
        precision=highest,
        preferred_element_type=jnp.float32,
    ) * (1.0 / (NG * NG))


def place_kernel(slots, planes, shares, known, *refs):
    place, choice, order, start = refs[-4:]
    largest = refs[0][slots]
    for s in range(1, STEPS + 1):
        largest = jnp.maximum(largest, refs[s][slots])
    choice[0] = largest
    start[0] = 0

    def tally(j, count):
        return count + (known[slots + j] < FIRST).astype(jnp.int32)

    def visit(j, carry):
        chunk = (known[slots + j] >= FIRST).astype(jnp.int32)
        at = start[chunk]
        start[chunk] = at + 1
        order[at] = j
        return carry

    start[1] = lax.fori_loop(0, slots, tally, jnp.int32(0))
    lax.fori_loop(0, slots, visit, 0)
    me = lax.axis_index("plane")
    base = 0
    for size in shares:
        each = size // planes
        for k in range(planes):
            first = base + partner(me, k, planes) * each
            for q in range(each):
                j = order[first + q]
                to = base + k * each + q
                for part in range(3):
                    place[part * slots + to] = known[part * slots + j]
        base += size


def pack_kernel(lines, low, high, wanted, orbitals, sent):
    for c in range(low, high):
        row = wanted[c] * lines
        sent[pl.ds((c - low) * lines, lines), :] = orbitals[pl.ds(row, lines), :]


def packs_kernel(lines, *refs):
    wanted, orbitals, sent = refs[:STEPS], refs[STEPS], refs[STEPS + 1 :]
    for s in range(STEPS):
        for c in range(FIRST, TOTALS[-1]):
            row = orbitals[pl.ds(wanted[s][c] * lines, lines), :]
            for i, total in enumerate(TOTALS):
                if c < total:
                    sent[i * STEPS + s][pl.ds((c - FIRST) * lines, lines), :] = row


def own_kernel(slots, lines, base, size, place, orbitals, owned):
    for j in range(size):
        near = jnp.maximum(place[2 * slots + base + j], 0) * lines
        owned[pl.ds(j * lines, lines), :] = orbitals[pl.ds(near, lines), :]


def density_kernel(slots, lines, planes, bounds, base, size, place, owned, *refs):
    received, parts, kept = refs[: STEPS * len(bounds)], refs[-planes - 1 : -1], refs[-1]
    each = size // planes
    for j in range(size):
        s, rank = place[base + j], place[slots + base + j]
        for c, (low, high) in enumerate(zip((0,) + bounds, bounds)):
            row = jnp.clip(rank - low, 0, high - low - 1) * lines
            found = received[c * STEPS][pl.ds(row, lines), :]
            for i in range(1, STEPS):
                found = jnp.where(s == i, received[c * STEPS + i][pl.ds(row, lines), :], found)
            value = found if c == 0 else jnp.where(rank >= low, found, value)
        kept[pl.ds(j * lines, lines), :] = value
        parts[j // each][pl.ds(j % each * lines, lines), :] = (
            owned[pl.ds(j * lines, lines), :] * value
        )


def sum_kernel(slots, lines, planes, base, size, fresh, place, *refs):
    kept, parts = refs[0], refs[1 : 1 + planes]
    out = refs[-1]
    if fresh:
        out[...] = jnp.zeros_like(out)
    else:
        out[...] = refs[1 + planes][...]
    each = size // planes
    for j in range(size):
        near = place[2 * slots + base + j] * lines

        @pl.when(near >= 0)
        def _():
            out[pl.ds(near, lines), :] += (
                parts[j // each][pl.ds(j % each * lines, lines), :]
                * kept[pl.ds(j * lines, lines), :]
            )


def transform_kernel(pairs, lines, planes, *refs):
    parts = refs[:planes]
    into_hi, into_lo, back_hi, back_lo, mix_hi, mix_lo, unmix_hi, unmix_lo, kernel = refs[
        planes : planes + 9
    ]
    outs = refs[planes + 9 : 2 * planes + 9]
    cells, waves, result = refs[2 * planes + 9 :]
    whole = planes * lines
    rows = NG // GROUP
    me = lax.axis_index("plane")
    for k in range(planes):
        slab = partner(me, k, planes) * lines
        for p in range(pairs):
            cells[pl.ds(p * whole + slab, lines), :] = parts[k][pl.ds(p * lines, lines), :]
    line = [split_value(cells[pl.ds(t, pairs * rows, stride=LINES), :]) for t in range(LINES)]
    for r in range(GROUP):
        wide = [jnp.concatenate([line[r][i], line[r + 1][i]], axis=1) for i in range(2)]
        found = dot3(wide, (into_hi[r], into_lo[r]))
        for p in range(pairs):
            waves[p, r * rows : (r + 1) * rows, :] = found[p * rows : (p + 1) * rows, :]
    mix = (mix_hi[...], mix_lo[...])
    unmix = (unmix_hi[...], unmix_lo[...])
    together = 3 if pairs % 3 == 0 else 1

    def filter_some(i, carry):
        for p in range(together):
            at = i * together + p
            spectrum = dot3(mix, split_value(waves[at])) * kernel[...]
            waves[at] = dot3(unmix, split_value(spectrum))
        return carry

    lax.fori_loop(0, pairs // together, filter_some, 0)
    carried = None
    for r in range(GROUP):
        mine = jnp.concatenate(
            [waves[p, r * rows : (r + 1) * rows, :] for p in range(pairs)], axis=0
        )
        wide = dot3(split_value(mine), (back_hi[r], back_lo[r]))
        first = wide[:, :LANES] if carried is None else wide[:, :LANES] + carried
        carried = wide[:, LANES:]
        result[pl.ds(r, pairs * rows, stride=LINES), :] = first
    result[pl.ds(GROUP, pairs * rows, stride=LINES), :] = carried
    for k in range(planes):
        slab = partner(me, k, planes) * lines
        for p in range(pairs):
            outs[k][pl.ds(p * lines, lines), :] = result[pl.ds(p * whole + slab, lines), :]


def shares_for(slots, planes):
    shares = EARLY + LATE
    units = slots // planes
    cuts = [units * sum(shares[: i + 1]) // sum(shares) for i in range(len(shares))]
    sizes = [(b - a) * planes for a, b in zip([0] + cuts, cuts)]
    return sizes, sum(sizes[len(EARLY) :])


def params():
    return pltpu.CompilerParams(vmem_limit_bytes=VMEM_LIMIT)


def cost(microseconds, flops=0):
    moved = int(microseconds * 1e3)
    return pl.CostEstimate(flops=flops, bytes_accessed=moved, transcendentals=0)


def floats(rows):
    return jax.ShapeDtypeStruct((rows, LANES), jnp.float32)


def partner(i, k, size):
    return i ^ k if size & (size - 1) == 0 else (k - i) % size


def exchange(parts, size):
    return [parts[0] if size & (size - 1) == 0 else lax.ppermute(parts[0], "plane", pairs_of(0, size))] + [
        lax.ppermute(parts[k], "plane", pairs_of(k, size)) for k in range(1, size)
    ]


def pairs_of(k, size):
    return [(i, partner(i, k, size)) for i in range(size)]


def local(orbitals, kernel_half, pair_own, pair_step, pair_remote, pair_count):
    groups, blocks, planes = (lax.axis_size(name) for name in ("groups", "blk", "plane"))
    orbs, depth, cell_count = orbitals.shape
    slots = pair_own.shape[0]
    lines = cell_count // LANES
    flat = orbitals.reshape(orbs * lines, LANES)
    shares, late = shares_for(slots, planes)

    width = -(-(slots + 1) // LANES) * LANES
    *requests, known = pl.pallas_call(
        functools.partial(plan_kernel, slots, orbs, late),
        out_shape=(
            *[jax.ShapeDtypeStruct((width,), jnp.int32)] * STEPS,
            jax.ShapeDtypeStruct((3 * slots,), jnp.int32),
        ),
        in_specs=[smem] * 4,
        out_specs=(smem,) * (STEPS + 1),
        scratch_shapes=[
            pltpu.SMEM((STEPS * orbs,), jnp.int32),
            pltpu.SMEM((slots + STEPS,), jnp.int32),
        ],
        cost_estimate=cost(2.3),
        name="plan",
    )(pair_own, pair_step, pair_remote, pair_count)

    wanted = [lax.ppermute(requests[s], "blk", route(-s - 1, blocks)) for s in range(STEPS)]

    def send(low, high, flat, wanted):
        packs = [
            pl.pallas_call(
                functools.partial(pack_kernel, lines, low, high),
                out_shape=floats((high - low) * lines),
                in_specs=[smem, vmem],
                out_specs=vmem,
                compiler_params=params(),
                cost_estimate=cost(0.5),
                name="pack",
            )(wanted[s], flat)
            for s in range(STEPS)
        ]
        return packs, [lax.ppermute(packs[s], "blk", route(s + 1, blocks)) for s in range(STEPS)]

    def make_density(bounds, base, size, place, owned, received, after):
        each = size // planes
        return pl.pallas_call(
            functools.partial(density_kernel, slots, lines, planes, bounds, base, size),
            out_shape=[floats(each * lines)] * planes + [floats(size * lines)],
            in_specs=[smem, vmem] + [vmem] * len(received) + [hbm] * len(after),
            out_specs=[vmem] * (planes + 1),
            compiler_params=params(),
            cost_estimate=cost(0.05 * size),
            name="density",
        )(place, owned, *received, *after)

    def filter_parts(parts, kernel, tables):
        each = parts[0].shape[0] // lines
        backs = pl.pallas_call(
            functools.partial(transform_kernel, each, lines, planes),
            out_shape=[floats(each * lines)] * planes,
            in_specs=[vmem] * (planes + 9),
            out_specs=[vmem] * planes,
            scratch_shapes=[
                pltpu.VMEM((each * planes * lines, LANES), jnp.float32),
                pltpu.VMEM((each, NG, NG), jnp.float32),
                pltpu.VMEM((each * planes * lines, LANES), jnp.float32),
            ],
            compiler_params=params(),
            cost_estimate=cost(0.5 + 0.4 * each),
            name="transform",
        )(*exchange(parts, planes), *tables, kernel)
        return backs

    def add_up(base, size, place, kept, potentials, before):
        return pl.pallas_call(
            functools.partial(sum_kernel, slots, lines, planes, base, size, not before),
            out_shape=floats(orbs * lines),
            in_specs=[smem] + [vmem] * (planes + 1 + len(before)),
            out_specs=vmem,
            compiler_params=params(),
            cost_estimate=cost(0.9),
            name="sum",
        )(place, kept, *potentials, *before)

    def own_rows(c, place, flat):
        return pl.pallas_call(
            functools.partial(own_kernel, slots, lines, sum(shares[:c]), shares[c]),
            out_shape=floats(shares[c] * lines),
            in_specs=[smem, vmem],
            out_specs=vmem,
            compiler_params=params(),
            cost_estimate=cost(0.5),
            name="own",
        )(place, flat)

    def one_chunk(bounds, c, place, owned, kernel, tables, received, before, after=()):
        base, size = sum(shares[:c]), shares[c]
        *parts, kept = make_density(bounds, base, size, place, owned[c], received, after)
        backs = filter_parts(parts, kernel, tables)
        potentials = exchange(backs, planes)
        return add_up(base, size, place, kept, potentials, before), potentials

    packs, first = send(0, FIRST, flat, wanted)
    place, choice = pl.pallas_call(
        functools.partial(place_kernel, slots, planes, shares),
        out_shape=(
            jax.ShapeDtypeStruct((3 * slots,), jnp.int32),
            jax.ShapeDtypeStruct((1,), jnp.int32),
        ),
        in_specs=[smem] * (STEPS + 2) + [hbm] * STEPS,
        out_specs=(smem, smem),
        scratch_shapes=[pltpu.SMEM((slots,), jnp.int32), pltpu.SMEM((2,), jnp.int32)],
        cost_estimate=cost(2.8),
        name="place",
    )(known, requests[0], *wanted, *packs)
    packed = pl.pallas_call(
        functools.partial(packs_kernel, lines),
        out_shape=[floats((t - FIRST) * lines) for t in TOTALS for s in range(STEPS)],
        in_specs=[smem] * STEPS + [vmem],
        out_specs=[vmem] * (STEPS * len(TOTALS)),
        compiler_params=params(),
        cost_estimate=cost(2),
        name="packs",
    )(*wanted, flat)
    owned = [own_rows(c, place, flat) for c in range(len(shares))]
    kernel = pl.pallas_call(
        expand_kernel,
        out_shape=jax.ShapeDtypeStruct((NG, NG), jnp.float32),
        in_specs=[vmem],
        out_specs=vmem,
        cost_estimate=cost(1.4),
        name="expand",
    )(kernel_half)
    if is_ring(blocks) and groups == 2:
        choice = jnp.maximum(choice, lax.ppermute(choice, "groups", [(0, 1), (1, 0)]))
    else:
        choice = lax.pmax(choice, ("groups", "blk"))
    tables = [jnp.asarray(part) for pair in make_tables(NG // planes) for part in pair]

    def finish(total, flat, wanted, packed, place, owned, kernel, tables, first):
        i = TOTALS.index(total)
        packs = packed[i * STEPS : (i + 1) * STEPS]
        later = [lax.ppermute(packs[s], "blk", route(s + 1, blocks)) for s in range(STEPS)]
        summed, after, formed = [], [], []
        for c in range(len(shares)):
            early = c < len(EARLY)
            bounds = (FIRST,) if early else (FIRST, total)
            rows = first if early else first + later
            result, potentials = one_chunk(
                bounds, c, place, owned, kernel, tables, rows, summed, after
            )
            summed = [result]
            if early:
                formed += potentials[2:]
            if c + 1 == len(EARLY):
                after = formed
        return summed[0]

    def general(flat, wanted, packed, place, owned, kernel, tables, first):
        rows = send(0, slots, flat, wanted)[1]
        summed = []
        for c in range(len(shares)):
            summed = [one_chunk((slots,), c, place, owned, kernel, tables, rows, summed)[0]]
        return summed[0]

    summed = lax.switch(
        choice[0],
        [functools.partial(finish, total) for total in TOTALS] + [general],
        flat,
        wanted,
        packed,
        place,
        owned,
        kernel,
        tables,
        first,
    )
    return summed.reshape(orbs, depth, cell_count)


def solution(mesh):
    in_specs = (
        P(("groups", "blk"), None, "plane"),
        P(),
        P(("groups", "blk")),
        P(("groups", "blk")),
        P(("groups", "blk")),
        P(("groups", "blk")),
    )
    out_specs = P(("groups", "blk"), None, "plane")
    return jax.shard_map(local, mesh=mesh, in_specs=in_specs, out_specs=out_specs, check_vma=False)
```

```python
import functools

import jax
import jax.numpy as jnp
import ml_dtypes
import numpy as np
from jax import lax
from jax.experimental import pallas as pl
from jax.experimental.pallas import tpu as pltpu
from jax.sharding import PartitionSpec as P

NG = 160
STEPS = 3
LANES = 128
GROUP = 4
LINES = 5
FIRST = 8
TOTALS = (17, 18, 19, 21, 24)
EARLY = (6,)
LATE = (3, 3)

VMEM_LIMIT = 16 * 1024 * 1024
highest = lax.Precision.HIGHEST
smem = pl.BlockSpec(memory_space=pltpu.SMEM)
vmem = pl.BlockSpec(memory_space=pltpu.VMEM)
hbm = pl.BlockSpec(memory_space=pl.ANY)


def split_table(table):
    high = table.astype(ml_dtypes.bfloat16)
    low = (table - high.astype(np.float64)).astype(ml_dtypes.bfloat16)
    return high, low


def make_tables(x_local):
    positions = np.arange(NG)
    angles = 2.0 * np.pi / NG * (positions[:, None] * positions[None, :] % NG)
    cas = np.cos(angles) + np.sin(angles)
    into = np.zeros((GROUP, 2 * LANES, NG))
    for r in range(GROUP):
        start = r * NG - r * LANES
        into[r, start : start + NG] = cas
    back = np.transpose(into, (0, 2, 1)).copy()
    order = np.arange(NG).reshape(NG // GROUP, GROUP).T.reshape(-1)
    mixed = cas[:, order]
    return split_table(into), split_table(back), split_table(mixed), split_table(mixed.T.copy())


def split_value(value):
    high = value.astype(jnp.bfloat16)
    low = (value - high.astype(jnp.float32)).astype(jnp.bfloat16)
    return high, low


def dot(a, b):
    return lax.dot_general(a, b, (((1,), (0,)), ((), ())), preferred_element_type=jnp.float32)


def dot3(a, b):
    return dot(a[0], b[0]) + (dot(a[0], b[1]) + dot(a[1], b[0]))


def is_ring(blocks):
    return blocks == STEPS + 1


def route(shift, blocks):
    return [(i, (i + shift) % blocks) for i in range(blocks)]


def plan_kernel(slots, orbs, late, own, step, remote, count, *refs):
    requests, (known, seen, hist) = refs[:STEPS], refs[STEPS:]
    for s in range(STEPS):
        for k in range(slots):
            requests[s][k] = 0
    for s in range(STEPS):
        hist[slots + s] = 0
        for k in range(orbs):
            seen[s * orbs + k] = -1
    for k in range(slots):
        hist[k] = 0

    def visit(j, carry):
        live = j < count[0]
        s = jnp.where(live, step[j], 0)
        k = remote[j]
        at = seen[s * orbs + k]
        used = hist[slots + s]
        rank = jnp.where(at < 0, used, at)

        @pl.when(live & (at < 0))
        def _():
            for i in range(STEPS):

                @pl.when(s == i)
                def _():
                    requests[i][used] = k

            seen[s * orbs + k] = used
            hist[slots + s] = used + 1

        @pl.when(live)
        def _():
            hist[rank] += 1

        known[j] = s
        known[slots + j] = jnp.where(live, rank, 0)
        known[2 * slots + j] = jnp.where(live, own[j], -1)
        return carry

    lax.fori_loop(0, slots, visit, 0)
    beyond = [jnp.int32(0)]
    for k in reversed(range(slots)):
        beyond.append(beyond[-1] + hist[k])
    beyond = beyond[::-1]
    fits = (beyond[FIRST] <= late) & (beyond[TOTALS[-1]] == 0)
    least = sum((beyond[total] > 0).astype(jnp.int32) for total in TOTALS[:-1])
    for s in range(STEPS):
        requests[s][slots] = jnp.where(fits, least, len(TOTALS))


def expand_kernel(half, full):
    rows, columns = full.shape[0], half.shape[1]
    place = lax.broadcasted_iota(jnp.int32, (rows, columns), 0)
    folded = jnp.minimum(place, rows - place)
    picker = (folded == lax.broadcasted_iota(jnp.int32, (rows, columns), 1)).astype(jnp.float32)
    tall = lax.dot_general(
        picker,
        half[0],
        (((1,), (0,)), ((), ())),
        precision=highest,
        preferred_element_type=jnp.float32,
    )
    full[...] = lax.dot_general(
        tall,
        picker,
        (((1,), (1,)), ((), ())),
        precision=highest,
        preferred_element_type=jnp.float32,
    ) * (1.0 / (NG * NG))


def place_kernel(slots, planes, shares, known, *refs):
    place, choice, order, start = refs[-4:]
    largest = refs[0][slots]
    for s in range(1, STEPS + 1):
        largest = jnp.maximum(largest, refs[s][slots])
    choice[0] = largest
    start[0] = 0

    def tally(j, count):
        return count + (known[slots + j] < FIRST).astype(jnp.int32)

    def visit(j, carry):
        chunk = (known[slots + j] >= FIRST).astype(jnp.int32)
        at = start[chunk]
        start[chunk] = at + 1
        order[at] = j
        return carry

    start[1] = lax.fori_loop(0, slots, tally, jnp.int32(0))
    lax.fori_loop(0, slots, visit, 0)
    me = lax.axis_index("plane")
    base = 0
    for size in shares:
        each = size // planes
        for k in range(planes):
            first = base + partner(me, k, planes) * each
            for q in range(each):
                j = order[first + q]
                to = base + k * each + q
                for part in range(3):
                    place[part * slots + to] = known[part * slots + j]
        base += size


def pack_kernel(lines, low, high, wanted, orbitals, sent):
    for c in range(low, high):
        row = wanted[c] * lines
        sent[pl.ds((c - low) * lines, lines), :] = orbitals[pl.ds(row, lines), :]


def packs_kernel(lines, *refs):
    wanted, orbitals, sent = refs[:STEPS], refs[STEPS], refs[STEPS + 1 :]
    for s in range(STEPS):
        for c in range(FIRST, TOTALS[-1]):
            row = orbitals[pl.ds(wanted[s][c] * lines, lines), :]
            for i, total in enumerate(TOTALS):
                if c < total:
                    sent[i * STEPS + s][pl.ds((c - FIRST) * lines, lines), :] = row


def own_kernel(slots, lines, base, size, place, orbitals, owned):
    for j in range(size):
        near = jnp.maximum(place[2 * slots + base + j], 0) * lines
        owned[pl.ds(j * lines, lines), :] = orbitals[pl.ds(near, lines), :]


def density_kernel(slots, lines, planes, bounds, base, size, place, owned, *refs):
    received, parts, kept = refs[: STEPS * len(bounds)], refs[-planes - 1 : -1], refs[-1]
    each = size // planes
    for j in range(size):
        s, rank = place[base + j], place[slots + base + j]
        for c, (low, high) in enumerate(zip((0,) + bounds, bounds)):
            row = jnp.clip(rank - low, 0, high - low - 1) * lines
            found = received[c * STEPS][pl.ds(row, lines), :]
            for i in range(1, STEPS):
                found = jnp.where(s == i, received[c * STEPS + i][pl.ds(row, lines), :], found)
            value = found if c == 0 else jnp.where(rank >= low, found, value)
        kept[pl.ds(j * lines, lines), :] = value
        parts[j // each][pl.ds(j % each * lines, lines), :] = (
            owned[pl.ds(j * lines, lines), :] * value
        )


def sum_kernel(slots, lines, planes, base, size, fresh, place, *refs):
    kept, parts = refs[0], refs[1 : 1 + planes]
    out = refs[-1]
    if fresh:
        out[...] = jnp.zeros_like(out)
    else:
        out[...] = refs[1 + planes][...]
    each = size // planes
    for j in range(size):
        near = place[2 * slots + base + j] * lines

        @pl.when(near >= 0)
        def _():
            out[pl.ds(near, lines), :] += (
                parts[j // each][pl.ds(j % each * lines, lines), :]
                * kept[pl.ds(j * lines, lines), :]
            )


def transform_kernel(pairs, lines, planes, *refs):
    parts = refs[:planes]
    into_hi, into_lo, back_hi, back_lo, mix_hi, mix_lo, unmix_hi, unmix_lo, kernel = refs[
        planes : planes + 9
    ]
    outs = refs[planes + 9 : 2 * planes + 9]
    cells, waves, result = refs[2 * planes + 9 :]
    whole = planes * lines
    rows = NG // GROUP
    me = lax.axis_index("plane")
    for k in range(planes):
        slab = partner(me, k, planes) * lines
        for p in range(pairs):
            cells[pl.ds(p * whole + slab, lines), :] = parts[k][pl.ds(p * lines, lines), :]
    line = [split_value(cells[pl.ds(t, pairs * rows, stride=LINES), :]) for t in range(LINES)]
    for r in range(GROUP):
        wide = [jnp.concatenate([line[r][i], line[r + 1][i]], axis=1) for i in range(2)]
        found = dot3(wide, (into_hi[r], into_lo[r]))
        for p in range(pairs):
            waves[p, r * rows : (r + 1) * rows, :] = found[p * rows : (p + 1) * rows, :]
    mix = (mix_hi[...], mix_lo[...])
    unmix = (unmix_hi[...], unmix_lo[...])
    together = 3 if pairs % 3 == 0 else 1

    def filter_some(i, carry):
        for p in range(together):
            at = i * together + p
            spectrum = dot3(mix, split_value(waves[at])) * kernel[...]
            waves[at] = dot3(unmix, split_value(spectrum))
        return carry

    lax.fori_loop(0, pairs // together, filter_some, 0)
    carried = None
    for r in range(GROUP):
        mine = jnp.concatenate(
            [waves[p, r * rows : (r + 1) * rows, :] for p in range(pairs)], axis=0
        )
        wide = dot3(split_value(mine), (back_hi[r], back_lo[r]))
        first = wide[:, :LANES] if carried is None else wide[:, :LANES] + carried
        carried = wide[:, LANES:]
        result[pl.ds(r, pairs * rows, stride=LINES), :] = first
    result[pl.ds(GROUP, pairs * rows, stride=LINES), :] = carried
    for k in range(planes):
        slab = partner(me, k, planes) * lines
        for p in range(pairs):
            outs[k][pl.ds(p * lines, lines), :] = result[pl.ds(p * whole + slab, lines), :]


def shares_for(slots, planes):
    shares = EARLY + LATE
    units = slots // planes
    cuts = [units * sum(shares[: i + 1]) // sum(shares) for i in range(len(shares))]
    sizes = [(b - a) * planes for a, b in zip([0] + cuts, cuts)]
    return sizes, sum(sizes[len(EARLY) :])


def params():
    return pltpu.CompilerParams(vmem_limit_bytes=VMEM_LIMIT)


def cost(microseconds, flops=0):
    moved = int(microseconds * 1e3)
    return pl.CostEstimate(flops=flops, bytes_accessed=moved, transcendentals=0)


def floats(rows):
    return jax.ShapeDtypeStruct((rows, LANES), jnp.float32)


def partner(i, k, size):
    return i ^ k if size & (size - 1) == 0 else (k - i) % size


def exchange(parts, size):
    return [parts[0] if size & (size - 1) == 0 else lax.ppermute(parts[0], "plane", pairs_of(0, size))] + [
        lax.ppermute(parts[k], "plane", pairs_of(k, size)) for k in range(1, size)
    ]


def pairs_of(k, size):
    return [(i, partner(i, k, size)) for i in range(size)]


def local(orbitals, kernel_half, pair_own, pair_step, pair_remote, pair_count):
    groups, blocks, planes = (lax.axis_size(name) for name in ("groups", "blk", "plane"))
    orbs, depth, cell_count = orbitals.shape
    slots = pair_own.shape[0]
    lines = cell_count // LANES
    flat = orbitals.reshape(orbs * lines, LANES)
    shares, late = shares_for(slots, planes)

    width = -(-(slots + 1) // LANES) * LANES
    *requests, known = pl.pallas_call(
        functools.partial(plan_kernel, slots, orbs, late),
        out_shape=(
            *[jax.ShapeDtypeStruct((width,), jnp.int32)] * STEPS,
            jax.ShapeDtypeStruct((3 * slots,), jnp.int32),
        ),
        in_specs=[smem] * 4,
        out_specs=(smem,) * (STEPS + 1),
        scratch_shapes=[
            pltpu.SMEM((STEPS * orbs,), jnp.int32),
            pltpu.SMEM((slots + STEPS,), jnp.int32),
        ],
        cost_estimate=cost(2.3),
        name="plan",
    )(pair_own, pair_step, pair_remote, pair_count)

    wanted = [lax.ppermute(requests[s], "blk", route(-s - 1, blocks)) for s in range(STEPS)]

    def send(low, high, flat, wanted):
        packs = [
            pl.pallas_call(
                functools.partial(pack_kernel, lines, low, high),
                out_shape=floats((high - low) * lines),
                in_specs=[smem, vmem],
                out_specs=vmem,
                compiler_params=params(),
                cost_estimate=cost(0.5),
                name="pack",
            )(wanted[s], flat)
            for s in range(STEPS)
        ]
        return packs, [lax.ppermute(packs[s], "blk", route(s + 1, blocks)) for s in range(STEPS)]

    def make_density(bounds, base, size, place, owned, received, after):
        each = size // planes
        return pl.pallas_call(
            functools.partial(density_kernel, slots, lines, planes, bounds, base, size),
            out_shape=[floats(each * lines)] * planes + [floats(size * lines)],
            in_specs=[smem, vmem] + [vmem] * len(received) + [hbm] * len(after),
            out_specs=[vmem] * (planes + 1),
            compiler_params=params(),
            cost_estimate=cost(0.05 * size),
            name="density",
        )(place, owned, *received, *after)

    def filter_parts(parts, kernel, tables):
        each = parts[0].shape[0] // lines
        backs = pl.pallas_call(
            functools.partial(transform_kernel, each, lines, planes),
            out_shape=[floats(each * lines)] * planes,
            in_specs=[vmem] * (planes + 9),
            out_specs=[vmem] * planes,
            scratch_shapes=[
                pltpu.VMEM((each * planes * lines, LANES), jnp.float32),
                pltpu.VMEM((each, NG, NG), jnp.float32),
                pltpu.VMEM((each * planes * lines, LANES), jnp.float32),
            ],
            compiler_params=params(),
            cost_estimate=cost(0.5 + 0.4 * each),
            name="transform",
        )(*exchange(parts, planes), *tables, kernel)
        return backs

    def add_up(base, size, place, kept, potentials, before):
        return pl.pallas_call(
            functools.partial(sum_kernel, slots, lines, planes, base, size, not before),
            out_shape=floats(orbs * lines),
            in_specs=[smem] + [vmem] * (planes + 1 + len(before)),
            out_specs=vmem,
            compiler_params=params(),
            cost_estimate=cost(0.9),
            name="sum",
        )(place, kept, *potentials, *before)

    def own_rows(c, place, flat):
        return pl.pallas_call(
            functools.partial(own_kernel, slots, lines, sum(shares[:c]), shares[c]),
            out_shape=floats(shares[c] * lines),
            in_specs=[smem, vmem],
            out_specs=vmem,
            compiler_params=params(),
            cost_estimate=cost(0.5),
            name="own",
        )(place, flat)

    def one_chunk(bounds, c, place, owned, kernel, tables, received, before, after=()):
        base, size = sum(shares[:c]), shares[c]
        *parts, kept = make_density(bounds, base, size, place, owned[c], received, after)
        backs = filter_parts(parts, kernel, tables)
        potentials = exchange(backs, planes)
        return add_up(base, size, place, kept, potentials, before), potentials

    packs, first = send(0, FIRST, flat, wanted)
    place, choice = pl.pallas_call(
        functools.partial(place_kernel, slots, planes, shares),
        out_shape=(
            jax.ShapeDtypeStruct((3 * slots,), jnp.int32),
            jax.ShapeDtypeStruct((1,), jnp.int32),
        ),
        in_specs=[smem] * (STEPS + 2) + [hbm] * STEPS,
        out_specs=(smem, smem),
        scratch_shapes=[pltpu.SMEM((slots,), jnp.int32), pltpu.SMEM((2,), jnp.int32)],
        cost_estimate=cost(2.8),
        name="place",
    )(known, requests[0], *wanted, *packs)
    packed = pl.pallas_call(
        functools.partial(packs_kernel, lines),
        out_shape=[floats((t - FIRST) * lines) for t in TOTALS for s in range(STEPS)],
        in_specs=[smem] * STEPS + [vmem],
        out_specs=[vmem] * (STEPS * len(TOTALS)),
        compiler_params=params(),
        cost_estimate=cost(2),
        name="packs",
    )(*wanted, flat)
    owned = [own_rows(c, place, flat) for c in range(len(shares))]
    kernel = pl.pallas_call(
        expand_kernel,
        out_shape=jax.ShapeDtypeStruct((NG, NG), jnp.float32),
        in_specs=[vmem],
        out_specs=vmem,
        cost_estimate=cost(1.4),
        name="expand",
    )(kernel_half)
    if is_ring(blocks) and groups == 2:
        choice = jnp.maximum(choice, lax.ppermute(choice, "groups", [(0, 1), (1, 0)]))
    else:
        choice = lax.pmax(choice, ("groups", "blk"))
    tables = [jnp.asarray(part) for pair in make_tables(NG // planes) for part in pair]

    def finish(total, flat, wanted, packed, place, owned, kernel, tables, first):
        i = TOTALS.index(total)
        packs = packed[i * STEPS : (i + 1) * STEPS]
        later = [lax.ppermute(packs[s], "blk", route(s + 1, blocks)) for s in range(STEPS)]
        summed, after, formed = [], [], []
        for c in range(len(shares)):
            early = c < len(EARLY)
            bounds = (FIRST,) if early else (FIRST, total)
            rows = first if early else first + later
            result, potentials = one_chunk(
                bounds, c, place, owned, kernel, tables, rows, summed, after
            )
            summed = [result]
            if early:
                formed += potentials[1 if total - FIRST > 9 else 2 :]
            if c + 1 == len(EARLY):
                after = formed
        return summed[0]

    def general(flat, wanted, packed, place, owned, kernel, tables, first):
        rows = send(0, slots, flat, wanted)[1]
        summed = []
        for c in range(len(shares)):
            summed = [one_chunk((slots,), c, place, owned, kernel, tables, rows, summed)[0]]
        return summed[0]

    summed = lax.switch(
        choice[0],
        [functools.partial(finish, total) for total in TOTALS] + [general],
        flat,
        wanted,
        packed,
        place,
        owned,
        kernel,
        tables,
        first,
    )
    return summed.reshape(orbs, depth, cell_count)


def solution(mesh):
    in_specs = (
        P(("groups", "blk"), None, "plane"),
        P(),
        P(("groups", "blk")),
        P(("groups", "blk")),
        P(("groups", "blk")),
        P(("groups", "blk")),
    )
    out_specs = P(("groups", "blk"), None, "plane")
    return jax.shard_map(local, mesh=mesh, in_specs=in_specs, out_specs=out_specs, check_vma=False)
```

```python
import functools

import jax
import jax.numpy as jnp
import ml_dtypes
import numpy as np
from jax import lax
from jax.experimental import pallas as pl
from jax.experimental.pallas import tpu as pltpu
from jax.sharding import PartitionSpec as P

NG = 160
STEPS = 3
LANES = 128
GROUP = 4
LINES = 5
FIRST = 8
TOTALS = (17, 19, 21, 24)
EARLY = (6,)
LATE = (3, 3)

VMEM_LIMIT = 16 * 1024 * 1024
highest = lax.Precision.HIGHEST
smem = pl.BlockSpec(memory_space=pltpu.SMEM)
vmem = pl.BlockSpec(memory_space=pltpu.VMEM)
hbm = pl.BlockSpec(memory_space=pl.ANY)


def split_table(table):
    high = table.astype(ml_dtypes.bfloat16)
    low = (table - high.astype(np.float64)).astype(ml_dtypes.bfloat16)
    return high, low


def make_tables(x_local):
    positions = np.arange(NG)
    angles = 2.0 * np.pi / NG * (positions[:, None] * positions[None, :] % NG)
    cas = np.cos(angles) + np.sin(angles)
    into = np.zeros((GROUP, 2 * LANES, NG))
    for r in range(GROUP):
        start = r * NG - r * LANES
        into[r, start : start + NG] = cas
    back = np.transpose(into, (0, 2, 1)).copy()
    order = np.arange(NG).reshape(NG // GROUP, GROUP).T.reshape(-1)
    mixed = cas[:, order]
    return split_table(into), split_table(back), split_table(mixed), split_table(mixed.T.copy())


def split_value(value):
    high = value.astype(jnp.bfloat16)
    low = (value - high.astype(jnp.float32)).astype(jnp.bfloat16)
    return high, low


def dot(a, b):
    return lax.dot_general(a, b, (((1,), (0,)), ((), ())), preferred_element_type=jnp.float32)


def dot3(a, b):
    return dot(a[0], b[0]) + (dot(a[0], b[1]) + dot(a[1], b[0]))


def is_ring(blocks):
    return blocks == STEPS + 1


def route(shift, blocks):
    return [(i, (i + shift) % blocks) for i in range(blocks)]


def plan_kernel(slots, orbs, late, own, step, remote, count, *refs):
    requests, (known, seen, hist) = refs[:STEPS], refs[STEPS:]
    for s in range(STEPS):
        for k in range(slots):
            requests[s][k] = 0
    for s in range(STEPS):
        hist[slots + s] = 0
        for k in range(orbs):
            seen[s * orbs + k] = -1
    for k in range(slots):
        hist[k] = 0

    def visit(j, carry):
        live = j < count[0]
        s = jnp.where(live, step[j], 0)
        k = remote[j]
        at = seen[s * orbs + k]
        used = hist[slots + s]
        rank = jnp.where(at < 0, used, at)

        @pl.when(live & (at < 0))
        def _():
            for i in range(STEPS):

                @pl.when(s == i)
                def _():
                    requests[i][used] = k

            seen[s * orbs + k] = used
            hist[slots + s] = used + 1

        @pl.when(live)
        def _():
            hist[rank] += 1

        known[j] = s
        known[slots + j] = jnp.where(live, rank, 0)
        known[2 * slots + j] = jnp.where(live, own[j], -1)
        return carry

    lax.fori_loop(0, slots, visit, 0)
    beyond = [jnp.int32(0)]
    for k in reversed(range(slots)):
        beyond.append(beyond[-1] + hist[k])
    beyond = beyond[::-1]
    fits = (beyond[FIRST] <= late) & (beyond[TOTALS[-1]] == 0)
    least = sum((beyond[total] > 0).astype(jnp.int32) for total in TOTALS[:-1])
    for s in range(STEPS):
        requests[s][slots] = jnp.where(fits, least, len(TOTALS))


def expand_kernel(half, full):
    rows, columns = full.shape[0], half.shape[1]
    place = lax.broadcasted_iota(jnp.int32, (rows, columns), 0)
    folded = jnp.minimum(place, rows - place)
    picker = (folded == lax.broadcasted_iota(jnp.int32, (rows, columns), 1)).astype(jnp.float32)
    tall = lax.dot_general(
        picker,
        half[0],
        (((1,), (0,)), ((), ())),
        precision=highest,
        preferred_element_type=jnp.float32,
    )
    full[...] = lax.dot_general(
        tall,
        picker,
        (((1,), (1,)), ((), ())),
        precision=highest,
        preferred_element_type=jnp.float32,
    ) * (1.0 / (NG * NG))


def place_kernel(slots, planes, shares, known, *refs):
    place, choice, order, start = refs[-4:]
    largest = refs[0][slots]
    for s in range(1, STEPS + 1):
        largest = jnp.maximum(largest, refs[s][slots])
    choice[0] = largest
    start[0] = 0

    def tally(j, count):
        return count + (known[slots + j] < FIRST).astype(jnp.int32)

    def visit(j, carry):
        chunk = (known[slots + j] >= FIRST).astype(jnp.int32)
        at = start[chunk]
        start[chunk] = at + 1
        order[at] = j
        return carry

    start[1] = lax.fori_loop(0, slots, tally, jnp.int32(0))
    lax.fori_loop(0, slots, visit, 0)
    me = lax.axis_index("plane")
    base = 0
    for size in shares:
        each = size // planes
        for k in range(planes):
            first = base + partner(me, k, planes) * each
            for q in range(each):
                j = order[first + q]
                to = base + k * each + q
                for part in range(3):
                    place[part * slots + to] = known[part * slots + j]
        base += size


def pack_kernel(lines, low, high, wanted, orbitals, sent):
    for c in range(low, high):
        row = wanted[c] * lines
        sent[pl.ds((c - low) * lines, lines), :] = orbitals[pl.ds(row, lines), :]


def packs_kernel(lines, *refs):
    wanted, orbitals, sent = refs[:STEPS], refs[STEPS], refs[STEPS + 1 :]
    for s in range(STEPS):
        for c in range(FIRST, TOTALS[-1]):
            row = orbitals[pl.ds(wanted[s][c] * lines, lines), :]
            for i, total in enumerate(TOTALS):
                if c < total:
                    sent[i * STEPS + s][pl.ds((c - FIRST) * lines, lines), :] = row


def own_kernel(slots, lines, base, size, place, orbitals, owned):
    for j in range(size):
        near = jnp.maximum(place[2 * slots + base + j], 0) * lines
        owned[pl.ds(j * lines, lines), :] = orbitals[pl.ds(near, lines), :]


def density_kernel(slots, lines, planes, bounds, base, size, place, owned, *refs):
    received, parts, kept = refs[: STEPS * len(bounds)], refs[-planes - 1 : -1], refs[-1]
    each = size // planes
    for j in range(size):
        s, rank = place[base + j], place[slots + base + j]
        for c, (low, high) in enumerate(zip((0,) + bounds, bounds)):
            row = jnp.clip(rank - low, 0, high - low - 1) * lines
            found = received[c * STEPS][pl.ds(row, lines), :]
            for i in range(1, STEPS):
                found = jnp.where(s == i, received[c * STEPS + i][pl.ds(row, lines), :], found)
            value = found if c == 0 else jnp.where(rank >= low, found, value)
        kept[pl.ds(j * lines, lines), :] = value
        parts[j // each][pl.ds(j % each * lines, lines), :] = (
            owned[pl.ds(j * lines, lines), :] * value
        )


def sum_kernel(slots, lines, planes, base, size, fresh, place, *refs):
    kept, parts = refs[0], refs[1 : 1 + planes]
    out = refs[-1]
    if fresh:
        out[...] = jnp.zeros_like(out)
    else:
        out[...] = refs[1 + planes][...]
    each = size // planes
    for j in range(size):
        near = place[2 * slots + base + j] * lines

        @pl.when(near >= 0)
        def _():
            out[pl.ds(near, lines), :] += (
                parts[j // each][pl.ds(j % each * lines, lines), :]
                * kept[pl.ds(j * lines, lines), :]
            )


def transform_kernel(pairs, lines, planes, *refs):
    parts = refs[:planes]
    into_hi, into_lo, back_hi, back_lo, mix_hi, mix_lo, unmix_hi, unmix_lo, kernel = refs[
        planes : planes + 9
    ]
    outs = refs[planes + 9 : 2 * planes + 9]
    cells, waves, result = refs[2 * planes + 9 :]
    whole = planes * lines
    rows = NG // GROUP
    me = lax.axis_index("plane")
    for k in range(planes):
        slab = partner(me, k, planes) * lines
        for p in range(pairs):
            cells[pl.ds(p * whole + slab, lines), :] = parts[k][pl.ds(p * lines, lines), :]
    line = [split_value(cells[pl.ds(t, pairs * rows, stride=LINES), :]) for t in range(LINES)]
    for r in range(GROUP):
        wide = [jnp.concatenate([line[r][i], line[r + 1][i]], axis=1) for i in range(2)]
        found = dot3(wide, (into_hi[r], into_lo[r]))
        for p in range(pairs):
            waves[p, r * rows : (r + 1) * rows, :] = found[p * rows : (p + 1) * rows, :]
    mix = (mix_hi[...], mix_lo[...])
    unmix = (unmix_hi[...], unmix_lo[...])
    together = 3 if pairs % 3 == 0 else 1

    def filter_some(i, carry):
        for p in range(together):
            at = i * together + p
            spectrum = dot3(mix, split_value(waves[at])) * kernel[...]
            waves[at] = dot3(unmix, split_value(spectrum))
        return carry

    lax.fori_loop(0, pairs // together, filter_some, 0)
    carried = None
    for r in range(GROUP):
        mine = jnp.concatenate(
            [waves[p, r * rows : (r + 1) * rows, :] for p in range(pairs)], axis=0
        )
        wide = dot3(split_value(mine), (back_hi[r], back_lo[r]))
        first = wide[:, :LANES] if carried is None else wide[:, :LANES] + carried
        carried = wide[:, LANES:]
        result[pl.ds(r, pairs * rows, stride=LINES), :] = first
    result[pl.ds(GROUP, pairs * rows, stride=LINES), :] = carried
    for k in range(planes):
        slab = partner(me, k, planes) * lines
        for p in range(pairs):
            outs[k][pl.ds(p * lines, lines), :] = result[pl.ds(p * whole + slab, lines), :]


def shares_for(slots, planes):
    shares = EARLY + LATE
    units = slots // planes
    cuts = [units * sum(shares[: i + 1]) // sum(shares) for i in range(len(shares))]
    sizes = [(b - a) * planes for a, b in zip([0] + cuts, cuts)]
    return sizes, sum(sizes[len(EARLY) :])


def params():
    return pltpu.CompilerParams(vmem_limit_bytes=VMEM_LIMIT)


def cost(microseconds, flops=0):
    moved = int(microseconds * 1e3)
    return pl.CostEstimate(flops=flops, bytes_accessed=moved, transcendentals=0)


def floats(rows):
    return jax.ShapeDtypeStruct((rows, LANES), jnp.float32)


def partner(i, k, size):
    return i ^ k if size & (size - 1) == 0 else (k - i) % size


def exchange(parts, size):
    return [parts[0] if size & (size - 1) == 0 else lax.ppermute(parts[0], "plane", pairs_of(0, size))] + [
        lax.ppermute(parts[k], "plane", pairs_of(k, size)) for k in range(1, size)
    ]


def pairs_of(k, size):
    return [(i, partner(i, k, size)) for i in range(size)]


def local(orbitals, kernel_half, pair_own, pair_step, pair_remote, pair_count):
    groups, blocks, planes = (lax.axis_size(name) for name in ("groups", "blk", "plane"))
    orbs, depth, cell_count = orbitals.shape
    slots = pair_own.shape[0]
    lines = cell_count // LANES
    flat = orbitals.reshape(orbs * lines, LANES)
    shares, late = shares_for(slots, planes)

    width = -(-(slots + 1) // LANES) * LANES
    *requests, known = pl.pallas_call(
        functools.partial(plan_kernel, slots, orbs, late),
        out_shape=(
            *[jax.ShapeDtypeStruct((width,), jnp.int32)] * STEPS,
            jax.ShapeDtypeStruct((3 * slots,), jnp.int32),
        ),
        in_specs=[smem] * 4,
        out_specs=(smem,) * (STEPS + 1),
        scratch_shapes=[
            pltpu.SMEM((STEPS * orbs,), jnp.int32),
            pltpu.SMEM((slots + STEPS,), jnp.int32),
        ],
        cost_estimate=cost(2.3),
        name="plan",
    )(pair_own, pair_step, pair_remote, pair_count)

    wanted = [lax.ppermute(requests[s], "blk", route(-s - 1, blocks)) for s in range(STEPS)]

    def send(low, high, flat, wanted):
        packs = [
            pl.pallas_call(
                functools.partial(pack_kernel, lines, low, high),
                out_shape=floats((high - low) * lines),
                in_specs=[smem, vmem],
                out_specs=vmem,
                compiler_params=params(),
                cost_estimate=cost(0.5),
                name="pack",
            )(wanted[s], flat)
            for s in range(STEPS)
        ]
        return packs, [lax.ppermute(packs[s], "blk", route(s + 1, blocks)) for s in range(STEPS)]

    def make_density(bounds, base, size, place, owned, received, after):
        each = size // planes
        return pl.pallas_call(
            functools.partial(density_kernel, slots, lines, planes, bounds, base, size),
            out_shape=[floats(each * lines)] * planes + [floats(size * lines)],
            in_specs=[smem, vmem] + [vmem] * len(received) + [hbm] * len(after),
            out_specs=[vmem] * (planes + 1),
            compiler_params=params(),
            cost_estimate=cost(0.05 * size),
            name="density",
        )(place, owned, *received, *after)

    def filter_parts(parts, kernel, tables):
        each = parts[0].shape[0] // lines
        backs = pl.pallas_call(
            functools.partial(transform_kernel, each, lines, planes),
            out_shape=[floats(each * lines)] * planes,
            in_specs=[vmem] * (planes + 9),
            out_specs=[vmem] * planes,
            scratch_shapes=[
                pltpu.VMEM((each * planes * lines, LANES), jnp.float32),
                pltpu.VMEM((each, NG, NG), jnp.float32),
                pltpu.VMEM((each * planes * lines, LANES), jnp.float32),
            ],
            compiler_params=params(),
            cost_estimate=cost(0.5 + 0.4 * each),
            name="transform",
        )(*exchange(parts, planes), *tables, kernel)
        return backs

    def add_up(base, size, place, kept, potentials, before):
        return pl.pallas_call(
            functools.partial(sum_kernel, slots, lines, planes, base, size, not before),
            out_shape=floats(orbs * lines),
            in_specs=[smem] + [vmem] * (planes + 1 + len(before)),
            out_specs=vmem,
            compiler_params=params(),
            cost_estimate=cost(0.9),
            name="sum",
        )(place, kept, *potentials, *before)

    def own_rows(c, place, flat):
        return pl.pallas_call(
            functools.partial(own_kernel, slots, lines, sum(shares[:c]), shares[c]),
            out_shape=floats(shares[c] * lines),
            in_specs=[smem, vmem],
            out_specs=vmem,
            compiler_params=params(),
            cost_estimate=cost(0.5),
            name="own",
        )(place, flat)

    def one_chunk(bounds, c, place, owned, kernel, tables, received, before, after=()):
        base, size = sum(shares[:c]), shares[c]
        *parts, kept = make_density(bounds, base, size, place, owned[c], received, after)
        backs = filter_parts(parts, kernel, tables)
        potentials = exchange(backs, planes)
        return add_up(base, size, place, kept, potentials, before), potentials

    packs, first = send(0, FIRST, flat, wanted)
    place, choice = pl.pallas_call(
        functools.partial(place_kernel, slots, planes, shares),
        out_shape=(
            jax.ShapeDtypeStruct((3 * slots,), jnp.int32),
            jax.ShapeDtypeStruct((1,), jnp.int32),
        ),
        in_specs=[smem] * (STEPS + 2) + [hbm] * STEPS,
        out_specs=(smem, smem),
        scratch_shapes=[pltpu.SMEM((slots,), jnp.int32), pltpu.SMEM((2,), jnp.int32)],
        cost_estimate=cost(2.8),
        name="place",
    )(known, requests[0], *wanted, *packs)
    packed = pl.pallas_call(
        functools.partial(packs_kernel, lines),
        out_shape=[floats((t - FIRST) * lines) for t in TOTALS for s in range(STEPS)],
        in_specs=[smem] * STEPS + [vmem],
        out_specs=[vmem] * (STEPS * len(TOTALS)),
        compiler_params=params(),
        cost_estimate=cost(2),
        name="packs",
    )(*wanted, flat)
    owned = [own_rows(c, place, flat) for c in range(len(shares))]
    kernel = pl.pallas_call(
        expand_kernel,
        out_shape=jax.ShapeDtypeStruct((NG, NG), jnp.float32),
        in_specs=[vmem],
        out_specs=vmem,
        cost_estimate=cost(1.4),
        name="expand",
    )(kernel_half)
    if is_ring(blocks) and groups == 2:
        choice = jnp.maximum(choice, lax.ppermute(choice, "groups", [(0, 1), (1, 0)]))
    else:
        choice = lax.pmax(choice, ("groups", "blk"))
    tables = [jnp.asarray(part) for pair in make_tables(NG // planes) for part in pair]

    def finish(total, flat, wanted, packed, place, owned, kernel, tables, first):
        i = TOTALS.index(total)
        packs = packed[i * STEPS : (i + 1) * STEPS]
        later = [lax.ppermute(packs[s], "blk", route(s + 1, blocks)) for s in range(STEPS)]
        summed, after, formed = [], [], []
        for c in range(len(shares)):
            early = c < len(EARLY)
            bounds = (FIRST,) if early else (FIRST, total)
            rows = first if early else first + later
            result, potentials = one_chunk(
                bounds, c, place, owned, kernel, tables, rows, summed, after
            )
            summed = [result]
            if early:
                formed += potentials[1 if total - FIRST > 9 else 2 :]
            if c + 1 == len(EARLY):
                after = formed
        return summed[0]

    def general(flat, wanted, packed, place, owned, kernel, tables, first):
        rows = send(0, slots, flat, wanted)[1]
        summed = []
        for c in range(len(shares)):
            summed = [one_chunk((slots,), c, place, owned, kernel, tables, rows, summed)[0]]
        return summed[0]

    summed = lax.switch(
        choice[0],
        [functools.partial(finish, total) for total in TOTALS] + [general],
        flat,
        wanted,
        packed,
        place,
        owned,
        kernel,
        tables,
        first,
    )
    return summed.reshape(orbs, depth, cell_count)


def solution(mesh):
    in_specs = (
        P(("groups", "blk"), None, "plane"),
        P(),
        P(("groups", "blk")),
        P(("groups", "blk")),
        P(("groups", "blk")),
        P(("groups", "blk")),
    )
    out_specs = P(("groups", "blk"), None, "plane")
    return jax.shard_map(local, mesh=mesh, in_specs=in_specs, out_specs=out_specs, check_vma=False)
```

```python
import functools

import jax
import jax.numpy as jnp
import ml_dtypes
import numpy as np
from jax import lax
from jax.experimental import pallas as pl
from jax.experimental.pallas import tpu as pltpu
from jax.sharding import PartitionSpec as P

NG = 160
STEPS = 3
LANES = 128
GROUP = 4
LINES = 5
FIRST = 8
TOTALS = (17, 19, 21, 24)
EARLY = (6,)
LATE = (3, 3)

VMEM_LIMIT = 16 * 1024 * 1024
highest = lax.Precision.HIGHEST
smem = pl.BlockSpec(memory_space=pltpu.SMEM)
vmem = pl.BlockSpec(memory_space=pltpu.VMEM)
hbm = pl.BlockSpec(memory_space=pl.ANY)


def split_table(table):
    high = table.astype(ml_dtypes.bfloat16)
    low = (table - high.astype(np.float64)).astype(ml_dtypes.bfloat16)
    return high, low


def make_tables(x_local):
    positions = np.arange(NG)
    angles = 2.0 * np.pi / NG * (positions[:, None] * positions[None, :] % NG)
    cas = np.cos(angles) + np.sin(angles)
    into = np.zeros((GROUP, 2 * LANES, NG))
    for r in range(GROUP):
        start = r * NG - r * LANES
        into[r, start : start + NG] = cas
    back = np.transpose(into, (0, 2, 1)).copy()
    order = np.arange(NG).reshape(NG // GROUP, GROUP).T.reshape(-1)
    mixed = cas[:, order]
    return split_table(into), split_table(back), split_table(mixed), split_table(mixed.T.copy())


def split_value(value):
    high = value.astype(jnp.bfloat16)
    low = (value - high.astype(jnp.float32)).astype(jnp.bfloat16)
    return high, low


def dot(a, b):
    return lax.dot_general(a, b, (((1,), (0,)), ((), ())), preferred_element_type=jnp.float32)


def dot3(a, b):
    return dot(a[0], b[0]) + (dot(a[0], b[1]) + dot(a[1], b[0]))


def is_ring(blocks):
    return blocks == STEPS + 1


def route(shift, blocks):
    return [(i, (i + shift) % blocks) for i in range(blocks)]


def plan_kernel(slots, orbs, late, own, step, remote, count, *refs):
    requests, (known, seen, hist) = refs[:STEPS], refs[STEPS:]
    for s in range(STEPS):
        for k in range(slots):
            requests[s][k] = 0
    for s in range(STEPS):
        hist[slots + s] = 0
        for k in range(orbs):
            seen[s * orbs + k] = -1
    for k in range(slots):
        hist[k] = 0

    def visit(j, carry):
        live = j < count[0]
        s = jnp.where(live, step[j], 0)
        k = remote[j]
        at = seen[s * orbs + k]
        used = hist[slots + s]
        rank = jnp.where(at < 0, used, at)

        @pl.when(live & (at < 0))
        def _():
            for i in range(STEPS):

                @pl.when(s == i)
                def _():
                    requests[i][used] = k

            seen[s * orbs + k] = used
            hist[slots + s] = used + 1

        @pl.when(live)
        def _():
            hist[rank] += 1

        known[j] = s
        known[slots + j] = jnp.where(live, rank, 0)
        known[2 * slots + j] = jnp.where(live, own[j], -1)
        return carry

    lax.fori_loop(0, slots, visit, 0)
    beyond = [jnp.int32(0)]
    for k in reversed(range(slots)):
        beyond.append(beyond[-1] + hist[k])
    beyond = beyond[::-1]
    fits = (beyond[FIRST] <= late) & (beyond[TOTALS[-1]] == 0)
    least = sum((beyond[total] > 0).astype(jnp.int32) for total in TOTALS[:-1])
    for s in range(STEPS):
        requests[s][slots] = jnp.where(fits, least, len(TOTALS))


def expand_kernel(half, full):
    rows, columns = full.shape[0], half.shape[1]
    place = lax.broadcasted_iota(jnp.int32, (rows, columns), 0)
    folded = jnp.minimum(place, rows - place)
    picker = (folded == lax.broadcasted_iota(jnp.int32, (rows, columns), 1)).astype(jnp.float32)
    tall = lax.dot_general(
        picker,
        half[0],
        (((1,), (0,)), ((), ())),
        precision=highest,
        preferred_element_type=jnp.float32,
    )
    full[...] = lax.dot_general(
        tall,
        picker,
        (((1,), (1,)), ((), ())),
        precision=highest,
        preferred_element_type=jnp.float32,
    ) * (1.0 / (NG * NG))


def place_kernel(slots, planes, shares, known, *refs):
    place, choice, order, start = refs[-4:]
    largest = refs[0][slots]
    for s in range(1, STEPS + 1):
        largest = jnp.maximum(largest, refs[s][slots])
    choice[0] = largest
    start[0] = 0

    def tally(j, count):
        return count + (known[slots + j] < FIRST).astype(jnp.int32)

    def visit(j, carry):
        chunk = (known[slots + j] >= FIRST).astype(jnp.int32)
        at = start[chunk]
        start[chunk] = at + 1
        order[at] = j
        return carry

    start[1] = lax.fori_loop(0, slots, tally, jnp.int32(0))
    lax.fori_loop(0, slots, visit, 0)
    me = lax.axis_index("plane")
    base = 0
    for size in shares:
        each = size // planes
        for k in range(planes):
            first = base + partner(me, k, planes) * each
            for q in range(each):
                j = order[first + q]
                to = base + k * each + q
                for part in range(3):
                    place[part * slots + to] = known[part * slots + j]
        base += size


def pieces(lines):
    whole = lines // 8 * 8
    return [(0, whole)] + ([(lines - 8, 8)] if whole < lines else [])


def move_row(source, at, target, to, lines):
    for start, size in pieces(lines):
        target[pl.ds(to + start, size), :] = source[pl.ds(at + start, size), :]


def pack_kernel(lines, low, high, wanted, orbitals, sent):
    for c in range(low, high):
        move_row(orbitals, wanted[c] * lines, sent, (c - low) * lines, lines)


def packs_kernel(lines, *refs):
    wanted, orbitals, sent = refs[:STEPS], refs[STEPS], refs[STEPS + 1 :]
    for s in range(STEPS):
        for c in range(FIRST, TOTALS[-1]):
            for start, size in pieces(lines):
                value = orbitals[pl.ds(wanted[s][c] * lines + start, size), :]
                to = (c - FIRST) * lines + start
                for i, total in enumerate(TOTALS):
                    if c < total:
                        sent[i * STEPS + s][pl.ds(to, size), :] = value


def own_kernel(slots, lines, base, size, place, orbitals, owned):
    for j in range(size):
        near = jnp.maximum(place[2 * slots + base + j], 0) * lines
        move_row(orbitals, near, owned, j * lines, lines)


def density_kernel(slots, lines, planes, bounds, base, size, place, owned, *refs):
    received, parts, kept = refs[: STEPS * len(bounds)], refs[-planes - 1 : -1], refs[-1]
    each = size // planes
    for j in range(size):
        s, rank = place[base + j], place[slots + base + j]
        for start, count in pieces(lines):
            for c, (low, high) in enumerate(zip((0,) + bounds, bounds)):
                row = jnp.clip(rank - low, 0, high - low - 1) * lines + start
                found = received[c * STEPS][pl.ds(row, count), :]
                for i in range(1, STEPS):
                    other = received[c * STEPS + i][pl.ds(row, count), :]
                    found = jnp.where(s == i, other, found)
                value = found if c == 0 else jnp.where(rank >= low, found, value)
            kept[pl.ds(j * lines + start, count), :] = value
            parts[j // each][pl.ds(j % each * lines + start, count), :] = (
                owned[pl.ds(j * lines + start, count), :] * value
            )


def sum_kernel(slots, lines, planes, base, size, fresh, place, *refs):
    kept, parts = refs[0], refs[1 : 1 + planes]
    out = refs[-1]
    if fresh:
        out[...] = jnp.zeros_like(out)
    else:
        out[...] = refs[1 + planes][...]
    each = size // planes
    for j in range(size):
        near = place[2 * slots + base + j] * lines

        @pl.when(near >= 0)
        def _():
            part, first = parts[j // each], j % each * lines
            added = [
                out[pl.ds(near + start, count), :]
                + part[pl.ds(first + start, count), :] * kept[pl.ds(j * lines + start, count), :]
                for start, count in pieces(lines)
            ]
            for (start, count), value in zip(pieces(lines), added):
                out[pl.ds(near + start, count), :] = value


def transform_kernel(pairs, lines, planes, *refs):
    parts = refs[:planes]
    into_hi, into_lo, back_hi, back_lo, mix_hi, mix_lo, unmix_hi, unmix_lo, kernel = refs[
        planes : planes + 9
    ]
    outs = refs[planes + 9 : 2 * planes + 9]
    cells, waves, result = refs[2 * planes + 9 :]
    whole = planes * lines
    rows = NG // GROUP
    me = lax.axis_index("plane")
    for k in range(planes):
        slab = partner(me, k, planes) * lines
        for p in range(pairs):
            move_row(parts[k], p * lines, cells, p * whole + slab, lines)
    line = [split_value(cells[pl.ds(t, pairs * rows, stride=LINES), :]) for t in range(LINES)]
    for r in range(GROUP):
        wide = [jnp.concatenate([line[r][i], line[r + 1][i]], axis=1) for i in range(2)]
        found = dot3(wide, (into_hi[r], into_lo[r]))
        for p in range(pairs):
            waves[p, r * rows : (r + 1) * rows, :] = found[p * rows : (p + 1) * rows, :]
    mix = (mix_hi[...], mix_lo[...])
    unmix = (unmix_hi[...], unmix_lo[...])
    together = 3 if pairs % 3 == 0 else 1

    def filter_some(i, carry):
        for p in range(together):
            at = i * together + p
            spectrum = dot3(mix, split_value(waves[at])) * kernel[...]
            waves[at] = dot3(unmix, split_value(spectrum))
        return carry

    lax.fori_loop(0, pairs // together, filter_some, 0)
    carried = None
    for r in range(GROUP):
        mine = jnp.concatenate(
            [waves[p, r * rows : (r + 1) * rows, :] for p in range(pairs)], axis=0
        )
        wide = dot3(split_value(mine), (back_hi[r], back_lo[r]))
        first = wide[:, :LANES] if carried is None else wide[:, :LANES] + carried
        carried = wide[:, LANES:]
        result[pl.ds(r, pairs * rows, stride=LINES), :] = first
    result[pl.ds(GROUP, pairs * rows, stride=LINES), :] = carried
    for k in range(planes):
        slab = partner(me, k, planes) * lines
        for p in range(pairs):
            move_row(result, p * whole + slab, outs[k], p * lines, lines)


def shares_for(slots, planes):
    shares = EARLY + LATE
    units = slots // planes
    cuts = [units * sum(shares[: i + 1]) // sum(shares) for i in range(len(shares))]
    sizes = [(b - a) * planes for a, b in zip([0] + cuts, cuts)]
    return sizes, sum(sizes[len(EARLY) :])


def params():
    return pltpu.CompilerParams(vmem_limit_bytes=VMEM_LIMIT)


def cost(microseconds, flops=0):
    moved = int(microseconds * 1e3)
    return pl.CostEstimate(flops=flops, bytes_accessed=moved, transcendentals=0)


def floats(rows):
    return jax.ShapeDtypeStruct((rows, LANES), jnp.float32)


def partner(i, k, size):
    return i ^ k if size & (size - 1) == 0 else (k - i) % size


def exchange(parts, size):
    return [parts[0] if size & (size - 1) == 0 else lax.ppermute(parts[0], "plane", pairs_of(0, size))] + [
        lax.ppermute(parts[k], "plane", pairs_of(k, size)) for k in range(1, size)
    ]


def pairs_of(k, size):
    return [(i, partner(i, k, size)) for i in range(size)]


def local(orbitals, kernel_half, pair_own, pair_step, pair_remote, pair_count):
    groups, blocks, planes = (lax.axis_size(name) for name in ("groups", "blk", "plane"))
    orbs, depth, cell_count = orbitals.shape
    slots = pair_own.shape[0]
    lines = cell_count // LANES
    flat = orbitals.reshape(orbs * lines, LANES)
    shares, late = shares_for(slots, planes)

    width = -(-(slots + 1) // LANES) * LANES
    *requests, known = pl.pallas_call(
        functools.partial(plan_kernel, slots, orbs, late),
        out_shape=(
            *[jax.ShapeDtypeStruct((width,), jnp.int32)] * STEPS,
            jax.ShapeDtypeStruct((3 * slots,), jnp.int32),
        ),
        in_specs=[smem] * 4,
        out_specs=(smem,) * (STEPS + 1),
        scratch_shapes=[
            pltpu.SMEM((STEPS * orbs,), jnp.int32),
            pltpu.SMEM((slots + STEPS,), jnp.int32),
        ],
        cost_estimate=cost(2.3),
        name="plan",
    )(pair_own, pair_step, pair_remote, pair_count)

    wanted = [lax.ppermute(requests[s], "blk", route(-s - 1, blocks)) for s in range(STEPS)]

    def send(low, high, flat, wanted):
        packs = [
            pl.pallas_call(
                functools.partial(pack_kernel, lines, low, high),
                out_shape=floats((high - low) * lines),
                in_specs=[smem, vmem],
                out_specs=vmem,
                compiler_params=params(),
                cost_estimate=cost(0.5),
                name="pack",
            )(wanted[s], flat)
            for s in range(STEPS)
        ]
        return packs, [lax.ppermute(packs[s], "blk", route(s + 1, blocks)) for s in range(STEPS)]

    def make_density(bounds, base, size, place, owned, received, after):
        each = size // planes
        return pl.pallas_call(
            functools.partial(density_kernel, slots, lines, planes, bounds, base, size),
            out_shape=[floats(each * lines)] * planes + [floats(size * lines)],
            in_specs=[smem, vmem] + [vmem] * len(received) + [hbm] * len(after),
            out_specs=[vmem] * (planes + 1),
            compiler_params=params(),
            cost_estimate=cost(0.05 * size),
            name="density",
        )(place, owned, *received, *after)

    def filter_parts(parts, kernel, tables):
        each = parts[0].shape[0] // lines
        backs = pl.pallas_call(
            functools.partial(transform_kernel, each, lines, planes),
            out_shape=[floats(each * lines)] * planes,
            in_specs=[vmem] * (planes + 9),
            out_specs=[vmem] * planes,
            scratch_shapes=[
                pltpu.VMEM((each * planes * lines, LANES), jnp.float32),
                pltpu.VMEM((each, NG, NG), jnp.float32),
                pltpu.VMEM((each * planes * lines, LANES), jnp.float32),
            ],
            compiler_params=params(),
            cost_estimate=cost(0.5 + 0.4 * each),
            name="transform",
        )(*exchange(parts, planes), *tables, kernel)
        return backs

    def add_up(base, size, place, kept, potentials, before):
        return pl.pallas_call(
            functools.partial(sum_kernel, slots, lines, planes, base, size, not before),
            out_shape=floats(orbs * lines),
            in_specs=[smem] + [vmem] * (planes + 1 + len(before)),
            out_specs=vmem,
            compiler_params=params(),
            cost_estimate=cost(0.9),
            name="sum",
        )(place, kept, *potentials, *before)

    def own_rows(c, place, flat):
        return pl.pallas_call(
            functools.partial(own_kernel, slots, lines, sum(shares[:c]), shares[c]),
            out_shape=floats(shares[c] * lines),
            in_specs=[smem, vmem],
            out_specs=vmem,
            compiler_params=params(),
            cost_estimate=cost(0.5),
            name="own",
        )(place, flat)

    def one_chunk(bounds, c, place, owned, kernel, tables, received, before, after=()):
        base, size = sum(shares[:c]), shares[c]
        *parts, kept = make_density(bounds, base, size, place, owned[c], received, after)
        backs = filter_parts(parts, kernel, tables)
        potentials = exchange(backs, planes)
        return add_up(base, size, place, kept, potentials, before), potentials

    packs, first = send(0, FIRST, flat, wanted)
    place, choice = pl.pallas_call(
        functools.partial(place_kernel, slots, planes, shares),
        out_shape=(
            jax.ShapeDtypeStruct((3 * slots,), jnp.int32),
            jax.ShapeDtypeStruct((1,), jnp.int32),
        ),
        in_specs=[smem] * (STEPS + 2) + [hbm] * STEPS,
        out_specs=(smem, smem),
        scratch_shapes=[pltpu.SMEM((slots,), jnp.int32), pltpu.SMEM((2,), jnp.int32)],
        cost_estimate=cost(2.8),
        name="place",
    )(known, requests[0], *wanted, *packs)
    packed = pl.pallas_call(
        functools.partial(packs_kernel, lines),
        out_shape=[floats((t - FIRST) * lines) for t in TOTALS for s in range(STEPS)],
        in_specs=[smem] * STEPS + [vmem],
        out_specs=[vmem] * (STEPS * len(TOTALS)),
        compiler_params=params(),
        cost_estimate=cost(2),
        name="packs",
    )(*wanted, flat)
    owned = [own_rows(c, place, flat) for c in range(len(shares))]
    kernel = pl.pallas_call(
        expand_kernel,
        out_shape=jax.ShapeDtypeStruct((NG, NG), jnp.float32),
        in_specs=[vmem],
        out_specs=vmem,
        cost_estimate=cost(1.4),
        name="expand",
    )(kernel_half)
    if is_ring(blocks) and groups == 2:
        choice = jnp.maximum(choice, lax.ppermute(choice, "groups", [(0, 1), (1, 0)]))
    else:
        choice = lax.pmax(choice, ("groups", "blk"))
    tables = [jnp.asarray(part) for pair in make_tables(NG // planes) for part in pair]

    def finish(total, flat, wanted, packed, place, owned, kernel, tables, first):
        i = TOTALS.index(total)
        packs = packed[i * STEPS : (i + 1) * STEPS]
        later = [lax.ppermute(packs[s], "blk", route(s + 1, blocks)) for s in range(STEPS)]
        summed, after, formed = [], [], []
        for c in range(len(shares)):
            early = c < len(EARLY)
            bounds = (FIRST,) if early else (FIRST, total)
            rows = first if early else first + later
            result, potentials = one_chunk(
                bounds, c, place, owned, kernel, tables, rows, summed, after
            )
            summed = [result]
            if early:
                formed += potentials[1 if total - FIRST > 9 else 2 :]
            if c + 1 == len(EARLY):
                after = formed
        return summed[0]

    def general(flat, wanted, packed, place, owned, kernel, tables, first):
        rows = send(0, slots, flat, wanted)[1]
        summed = []
        for c in range(len(shares)):
            summed = [one_chunk((slots,), c, place, owned, kernel, tables, rows, summed)[0]]
        return summed[0]

    summed = lax.switch(
        choice[0],
        [functools.partial(finish, total) for total in TOTALS] + [general],
        flat,
        wanted,
        packed,
        place,
        owned,
        kernel,
        tables,
        first,
    )
    return summed.reshape(orbs, depth, cell_count)


def solution(mesh):
    in_specs = (
        P(("groups", "blk"), None, "plane"),
        P(),
        P(("groups", "blk")),
        P(("groups", "blk")),
        P(("groups", "blk")),
        P(("groups", "blk")),
    )
    out_specs = P(("groups", "blk"), None, "plane")
    return jax.shard_map(local, mesh=mesh, in_specs=in_specs, out_specs=out_specs, check_vma=False)
```

```python
import functools

import jax
import jax.numpy as jnp
import ml_dtypes
import numpy as np
from jax import lax
from jax.experimental import pallas as pl
from jax.experimental.pallas import tpu as pltpu
from jax.sharding import PartitionSpec as P

NG = 160
STEPS = 3
LANES = 128
GROUP = 4
LINES = 5
FIRST = 8
TOTALS = (17, 19, 21, 24)
EARLY = (6,)
LATE = (3, 3)

VMEM_LIMIT = 16 * 1024 * 1024
highest = lax.Precision.HIGHEST
smem = pl.BlockSpec(memory_space=pltpu.SMEM)
vmem = pl.BlockSpec(memory_space=pltpu.VMEM)
hbm = pl.BlockSpec(memory_space=pl.ANY)


def split_table(table):
    high = table.astype(ml_dtypes.bfloat16)
    low = (table - high.astype(np.float64)).astype(ml_dtypes.bfloat16)
    return high, low


def make_tables(x_local):
    positions = np.arange(NG)
    angles = 2.0 * np.pi / NG * (positions[:, None] * positions[None, :] % NG)
    cas = np.cos(angles) + np.sin(angles)
    into = np.zeros((GROUP, 2 * LANES, NG))
    for r in range(GROUP):
        start = r * NG - r * LANES
        into[r, start : start + NG] = cas
    back = np.transpose(into, (0, 2, 1)).copy()
    order = np.arange(NG).reshape(NG // GROUP, GROUP).T.reshape(-1)
    mixed = cas[:, order]
    return split_table(into), split_table(back), split_table(mixed), split_table(mixed.T.copy())


def split_value(value):
    high = value.astype(jnp.bfloat16)
    low = (value - high.astype(jnp.float32)).astype(jnp.bfloat16)
    return high, low


def dot(a, b):
    return lax.dot_general(a, b, (((1,), (0,)), ((), ())), preferred_element_type=jnp.float32)


def dot3(a, b):
    return dot(a[0], b[0]) + (dot(a[0], b[1]) + dot(a[1], b[0]))


def is_ring(blocks):
    return blocks == STEPS + 1


def route(shift, blocks):
    return [(i, (i + shift) % blocks) for i in range(blocks)]


def plan_kernel(slots, orbs, late, own, step, remote, count, *refs):
    requests, (known, seen, hist) = refs[:STEPS], refs[STEPS:]
    for s in range(STEPS):
        for k in range(slots):
            requests[s][k] = 0
    for s in range(STEPS):
        hist[slots + s] = 0
        for k in range(orbs):
            seen[s * orbs + k] = -1
    for k in range(slots):
        hist[k] = 0

    def visit(j, carry):
        live = j < count[0]
        s = jnp.where(live, step[j], 0)
        k = remote[j]
        at = seen[s * orbs + k]
        used = hist[slots + s]
        rank = jnp.where(at < 0, used, at)

        @pl.when(live & (at < 0))
        def _():
            for i in range(STEPS):

                @pl.when(s == i)
                def _():
                    requests[i][used] = k

            seen[s * orbs + k] = used
            hist[slots + s] = used + 1

        @pl.when(live)
        def _():
            hist[rank] += 1

        known[j] = s
        known[slots + j] = jnp.where(live, rank, 0)
        known[2 * slots + j] = jnp.where(live, own[j], -1)
        return carry

    lax.fori_loop(0, slots, visit, 0)
    beyond = [jnp.int32(0)]
    for k in reversed(range(slots)):
        beyond.append(beyond[-1] + hist[k])
    beyond = beyond[::-1]
    fits = (beyond[FIRST] <= late) & (beyond[TOTALS[-1]] == 0)
    least = sum((beyond[total] > 0).astype(jnp.int32) for total in TOTALS[:-1])
    for s in range(STEPS):
        requests[s][slots] = jnp.where(fits, least, len(TOTALS))


def expand_kernel(half, full):
    rows, columns = full.shape[0], half.shape[1]
    place = lax.broadcasted_iota(jnp.int32, (rows, columns), 0)
    folded = jnp.minimum(place, rows - place)
    picker = (folded == lax.broadcasted_iota(jnp.int32, (rows, columns), 1)).astype(jnp.float32)
    tall = lax.dot_general(
        picker,
        half[0],
        (((1,), (0,)), ((), ())),
        precision=highest,
        preferred_element_type=jnp.float32,
    )
    full[...] = lax.dot_general(
        tall,
        picker,
        (((1,), (1,)), ((), ())),
        precision=highest,
        preferred_element_type=jnp.float32,
    ) * (1.0 / (NG * NG))


def place_kernel(slots, planes, shares, known, *refs):
    place, choice, order, start = refs[-4:]
    largest = refs[0][slots]
    for s in range(1, STEPS + 1):
        largest = jnp.maximum(largest, refs[s][slots])
    choice[0] = largest
    start[0] = 0

    def tally(j, count):
        return count + (known[slots + j] < FIRST).astype(jnp.int32)

    def visit(j, carry):
        chunk = (known[slots + j] >= FIRST).astype(jnp.int32)
        at = start[chunk]
        start[chunk] = at + 1
        order[at] = j
        return carry

    start[1] = lax.fori_loop(0, slots, tally, jnp.int32(0))
    lax.fori_loop(0, slots, visit, 0)
    me = lax.axis_index("plane")
    base = 0
    for size in shares:
        each = size // planes
        for k in range(planes):
            first = base + partner(me, k, planes) * each
            for q in range(each):
                j = order[first + q]
                to = base + k * each + q
                for part in range(3):
                    place[part * slots + to] = known[part * slots + j]
        base += size


def pieces(lines):
    whole = lines // 8 * 8
    return [(0, whole)] + ([(lines - 8, 8)] if whole < lines else [])


def move_row(source, at, target, to, lines):
    for start, size in pieces(lines):
        target[pl.ds(to + start, size), :] = source[pl.ds(at + start, size), :]


def pack_kernel(lines, low, high, wanted, orbitals, sent):
    for c in range(low, high):
        move_row(orbitals, wanted[c] * lines, sent, (c - low) * lines, lines)


def packs_kernel(lines, *refs):
    wanted, orbitals, sent = refs[:STEPS], refs[STEPS], refs[STEPS + 1 :]
    for s in range(STEPS):
        for c in range(FIRST, TOTALS[-1]):
            for start, size in pieces(lines):
                value = orbitals[pl.ds(wanted[s][c] * lines + start, size), :]
                to = (c - FIRST) * lines + start
                for i, total in enumerate(TOTALS):
                    if c < total:
                        sent[i * STEPS + s][pl.ds(to, size), :] = value


def own_kernel(slots, lines, base, size, place, orbitals, owned):
    for j in range(size):
        near = jnp.maximum(place[2 * slots + base + j], 0) * lines
        move_row(orbitals, near, owned, j * lines, lines)


def density_kernel(slots, lines, planes, bounds, base, size, place, owned, *refs):
    received, parts, kept = refs[: STEPS * len(bounds)], refs[-planes - 1 : -1], refs[-1]
    each = size // planes
    for j in range(size):
        s, rank = place[base + j], place[slots + base + j]
        for start, count in pieces(lines):
            for c, (low, high) in enumerate(zip((0,) + bounds, bounds)):
                row = jnp.clip(rank - low, 0, high - low - 1) * lines + start
                found = received[c * STEPS][pl.ds(row, count), :]
                for i in range(1, STEPS):
                    other = received[c * STEPS + i][pl.ds(row, count), :]
                    found = jnp.where(s == i, other, found)
                value = found if c == 0 else jnp.where(rank >= low, found, value)
            kept[pl.ds(j * lines + start, count), :] = value
            parts[j // each][pl.ds(j % each * lines + start, count), :] = (
                owned[pl.ds(j * lines + start, count), :] * value
            )


def sum_kernel(slots, lines, planes, base, size, fresh, place, *refs):
    kept, parts = refs[0], refs[1 : 1 + planes]
    out = refs[-1]
    if fresh:
        out[...] = jnp.zeros_like(out)
    else:
        out[...] = refs[1 + planes][...]
    each = size // planes
    for j in range(size):
        near = place[2 * slots + base + j] * lines

        @pl.when(near >= 0)
        def _():
            part, first = parts[j // each], j % each * lines
            added = [
                out[pl.ds(near + start, count), :]
                + part[pl.ds(first + start, count), :] * kept[pl.ds(j * lines + start, count), :]
                for start, count in pieces(lines)
            ]
            for (start, count), value in zip(pieces(lines), added):
                out[pl.ds(near + start, count), :] = value


def transform_kernel(pairs, lines, planes, *refs):
    parts = refs[:planes]
    into_hi, into_lo, back_hi, back_lo, mix_hi, mix_lo, unmix_hi, unmix_lo, kernel = refs[
        planes : planes + 9
    ]
    outs = refs[planes + 9 : 2 * planes + 9]
    cells, waves, result = refs[2 * planes + 9 :]
    whole = planes * lines
    rows = NG // GROUP
    me = lax.axis_index("plane")
    for k in range(planes):
        slab = partner(me, k, planes) * lines
        for p in range(pairs):
            move_row(parts[k], p * lines, cells, p * whole + slab, lines)
    line = [split_value(cells[pl.ds(t, pairs * rows, stride=LINES), :]) for t in range(LINES)]
    for r in range(GROUP):
        wide = [jnp.concatenate([line[r][i], line[r + 1][i]], axis=1) for i in range(2)]
        found = dot3(wide, (into_hi[r], into_lo[r]))
        for p in range(pairs):
            waves[p, r * rows : (r + 1) * rows, :] = found[p * rows : (p + 1) * rows, :]
    mix = (mix_hi[...], mix_lo[...])
    unmix = (unmix_hi[...], unmix_lo[...])
    together = 3 if pairs % 3 == 0 else 1

    def filter_some(i, carry):
        for p in range(together):
            at = i * together + p
            spectrum = dot3(mix, split_value(waves[at])) * kernel[...]
            waves[at] = dot3(unmix, split_value(spectrum))
        return carry

    lax.fori_loop(0, pairs // together, filter_some, 0)
    carried = None
    for r in range(GROUP):
        mine = jnp.concatenate(
            [waves[p, r * rows : (r + 1) * rows, :] for p in range(pairs)], axis=0
        )
        wide = dot3(split_value(mine), (back_hi[r], back_lo[r]))
        first = wide[:, :LANES] if carried is None else wide[:, :LANES] + carried
        carried = wide[:, LANES:]
        result[pl.ds(r, pairs * rows, stride=LINES), :] = first
    result[pl.ds(GROUP, pairs * rows, stride=LINES), :] = carried
    for k in range(planes):
        slab = partner(me, k, planes) * lines
        for p in range(pairs):
            move_row(result, p * whole + slab, outs[k], p * lines, lines)


def shares_for(slots, planes):
    shares = EARLY + LATE
    units = slots // planes
    cuts = [units * sum(shares[: i + 1]) // sum(shares) for i in range(len(shares))]
    sizes = [(b - a) * planes for a, b in zip([0] + cuts, cuts)]
    return sizes, sum(sizes[len(EARLY) :])


def params():
    return pltpu.CompilerParams(vmem_limit_bytes=VMEM_LIMIT)


def cost(microseconds, flops=0):
    moved = int(microseconds * 1e3)
    return pl.CostEstimate(flops=flops, bytes_accessed=moved, transcendentals=0)


def floats(rows):
    return jax.ShapeDtypeStruct((rows, LANES), jnp.float32)


def partner(i, k, size):
    return i ^ k if size & (size - 1) == 0 else (k - i) % size


def exchange(parts, size):
    return [parts[0] if size & (size - 1) == 0 else lax.ppermute(parts[0], "plane", pairs_of(0, size))] + [
        lax.ppermute(parts[k], "plane", pairs_of(k, size)) for k in range(1, size)
    ]


def pairs_of(k, size):
    return [(i, partner(i, k, size)) for i in range(size)]


def local(orbitals, kernel_half, pair_own, pair_step, pair_remote, pair_count):
    groups, blocks, planes = (lax.axis_size(name) for name in ("groups", "blk", "plane"))
    orbs, depth, cell_count = orbitals.shape
    slots = pair_own.shape[0]
    lines = cell_count // LANES
    flat = orbitals.reshape(orbs * lines, LANES)
    shares, late = shares_for(slots, planes)

    width = -(-(slots + 1) // LANES) * LANES
    *requests, known = pl.pallas_call(
        functools.partial(plan_kernel, slots, orbs, late),
        out_shape=(
            *[jax.ShapeDtypeStruct((width,), jnp.int32)] * STEPS,
            jax.ShapeDtypeStruct((3 * slots,), jnp.int32),
        ),
        in_specs=[smem] * 4,
        out_specs=(smem,) * (STEPS + 1),
        scratch_shapes=[
            pltpu.SMEM((STEPS * orbs,), jnp.int32),
            pltpu.SMEM((slots + STEPS,), jnp.int32),
        ],
        cost_estimate=cost(2.3),
        name="plan",
    )(pair_own, pair_step, pair_remote, pair_count)

    wanted = [lax.ppermute(requests[s], "blk", route(-s - 1, blocks)) for s in range(STEPS)]

    def send(low, high, flat, wanted):
        packs = [
            pl.pallas_call(
                functools.partial(pack_kernel, lines, low, high),
                out_shape=floats((high - low) * lines),
                in_specs=[smem, vmem],
                out_specs=vmem,
                compiler_params=params(),
                cost_estimate=cost(0.5),
                name="pack",
            )(wanted[s], flat)
            for s in range(STEPS)
        ]
        return packs, [lax.ppermute(packs[s], "blk", route(s + 1, blocks)) for s in range(STEPS)]

    def make_density(bounds, base, size, place, owned, received, after):
        each = size // planes
        return pl.pallas_call(
            functools.partial(density_kernel, slots, lines, planes, bounds, base, size),
            out_shape=[floats(each * lines)] * planes + [floats(size * lines)],
            in_specs=[smem, vmem] + [vmem] * len(received) + [hbm] * len(after),
            out_specs=[vmem] * (planes + 1),
            compiler_params=params(),
            cost_estimate=cost(0.05 * size),
            name="density",
        )(place, owned, *received, *after)

    def filter_parts(parts, kernel, tables):
        each = parts[0].shape[0] // lines
        backs = pl.pallas_call(
            functools.partial(transform_kernel, each, lines, planes),
            out_shape=[floats(each * lines)] * planes,
            in_specs=[vmem] * (planes + 9),
            out_specs=[vmem] * planes,
            scratch_shapes=[
                pltpu.VMEM((each * planes * lines, LANES), jnp.float32),
                pltpu.VMEM((each, NG, NG), jnp.float32),
                pltpu.VMEM((each * planes * lines, LANES), jnp.float32),
            ],
            compiler_params=params(),
            cost_estimate=cost(0.5 + 0.4 * each),
            name="transform",
        )(*exchange(parts, planes), *tables, kernel)
        return backs

    def add_up(base, size, place, kept, potentials, before):
        return pl.pallas_call(
            functools.partial(sum_kernel, slots, lines, planes, base, size, not before),
            out_shape=floats(orbs * lines),
            in_specs=[smem] + [vmem] * (planes + 1 + len(before)),
            out_specs=vmem,
            compiler_params=params(),
            cost_estimate=cost(0.9),
            name="sum",
        )(place, kept, *potentials, *before)

    def own_rows(c, place, flat):
        return pl.pallas_call(
            functools.partial(own_kernel, slots, lines, sum(shares[:c]), shares[c]),
            out_shape=floats(shares[c] * lines),
            in_specs=[smem, vmem],
            out_specs=vmem,
            compiler_params=params(),
            cost_estimate=cost(0.5),
            name="own",
        )(place, flat)

    def one_chunk(bounds, c, place, owned, kernel, tables, received, before, after=()):
        base, size = sum(shares[:c]), shares[c]
        *parts, kept = make_density(bounds, base, size, place, owned[c], received, after)
        backs = filter_parts(parts, kernel, tables)
        potentials = exchange(backs, planes)
        return add_up(base, size, place, kept, potentials, before), potentials

    packs, first = send(0, FIRST, flat, wanted)
    place, choice = pl.pallas_call(
        functools.partial(place_kernel, slots, planes, shares),
        out_shape=(
            jax.ShapeDtypeStruct((3 * slots,), jnp.int32),
            jax.ShapeDtypeStruct((1,), jnp.int32),
        ),
        in_specs=[smem] * (STEPS + 2) + [hbm] * STEPS,
        out_specs=(smem, smem),
        scratch_shapes=[pltpu.SMEM((slots,), jnp.int32), pltpu.SMEM((2,), jnp.int32)],
        cost_estimate=cost(2.8),
        name="place",
    )(known, requests[0], *wanted, *packs)
    packed = pl.pallas_call(
        functools.partial(packs_kernel, lines),
        out_shape=[floats((t - FIRST) * lines) for t in TOTALS for s in range(STEPS)],
        in_specs=[smem] * STEPS + [vmem],
        out_specs=[vmem] * (STEPS * len(TOTALS)),
        compiler_params=params(),
        cost_estimate=cost(2),
        name="packs",
    )(*wanted, flat)
    owned = [own_rows(c, place, flat) for c in range(len(shares))]
    kernel = pl.pallas_call(
        expand_kernel,
        out_shape=jax.ShapeDtypeStruct((NG, NG), jnp.float32),
        in_specs=[vmem],
        out_specs=vmem,
        cost_estimate=cost(1.4),
        name="expand",
    )(kernel_half)
    if is_ring(blocks) and groups == 2:
        choice = jnp.maximum(choice, lax.ppermute(choice, "groups", [(0, 1), (1, 0)]))
    else:
        choice = lax.pmax(choice, ("groups", "blk"))
    tables = [jnp.asarray(part) for pair in make_tables(NG // planes) for part in pair]

    def finish(total, flat, wanted, packed, place, owned, kernel, tables, first):
        i = TOTALS.index(total)
        packs = packed[i * STEPS : (i + 1) * STEPS]
        later = [lax.ppermute(packs[s], "blk", route(s + 1, blocks)) for s in range(STEPS)]
        summed, after, formed = [], [], []
        for c in range(len(shares)):
            early = c < len(EARLY)
            bounds = (FIRST,) if early else (FIRST, total)
            rows = first if early else first + later
            result, potentials = one_chunk(
                bounds, c, place, owned, kernel, tables, rows, summed, after
            )
            summed = [result]
            if early:
                formed += potentials[1:]
            if c + 1 == len(EARLY):
                after = formed
        return summed[0]

    def general(flat, wanted, packed, place, owned, kernel, tables, first):
        rows = send(0, slots, flat, wanted)[1]
        summed = []
        for c in range(len(shares)):
            summed = [one_chunk((slots,), c, place, owned, kernel, tables, rows, summed)[0]]
        return summed[0]

    summed = lax.switch(
        choice[0],
        [functools.partial(finish, total) for total in TOTALS] + [general],
        flat,
        wanted,
        packed,
        place,
        owned,
        kernel,
        tables,
        first,
    )
    return summed.reshape(orbs, depth, cell_count)


def solution(mesh):
    in_specs = (
        P(("groups", "blk"), None, "plane"),
        P(),
        P(("groups", "blk")),
        P(("groups", "blk")),
        P(("groups", "blk")),
        P(("groups", "blk")),
    )
    out_specs = P(("groups", "blk"), None, "plane")
    return jax.shard_map(local, mesh=mesh, in_specs=in_specs, out_specs=out_specs, check_vma=False)
```

```python
import functools

import jax
import jax.numpy as jnp
import ml_dtypes
import numpy as np
from jax import lax
from jax.experimental import pallas as pl
from jax.experimental.pallas import tpu as pltpu
from jax.sharding import PartitionSpec as P

NG = 160
STEPS = 3
LANES = 128
GROUP = 4
LINES = 5
FIRST = 8
TOTALS = (17, 19, 21, 24)
EARLY = (6,)
LATE = (3, 3)

VMEM_LIMIT = 16 * 1024 * 1024
highest = lax.Precision.HIGHEST
smem = pl.BlockSpec(memory_space=pltpu.SMEM)
vmem = pl.BlockSpec(memory_space=pltpu.VMEM)
hbm = pl.BlockSpec(memory_space=pl.ANY)


def split_table(table):
    high = table.astype(ml_dtypes.bfloat16)
    low = (table - high.astype(np.float64)).astype(ml_dtypes.bfloat16)
    return high, low


def make_tables(x_local):
    positions = np.arange(NG)
    angles = 2.0 * np.pi / NG * (positions[:, None] * positions[None, :] % NG)
    cas = np.cos(angles) + np.sin(angles)
    into = np.zeros((GROUP, 2 * LANES, NG))
    for r in range(GROUP):
        start = r * NG - r * LANES
        into[r, start : start + NG] = cas
    back = np.transpose(into, (0, 2, 1)).copy()
    order = np.arange(NG).reshape(NG // GROUP, GROUP).T.reshape(-1)
    mixed = cas[:, order]
    return split_table(into), split_table(back), split_table(mixed), split_table(mixed.T.copy())


def split_value(value):
    high = value.astype(jnp.bfloat16)
    low = (value - high.astype(jnp.float32)).astype(jnp.bfloat16)
    return high, low


def dot(a, b):
    return lax.dot_general(a, b, (((1,), (0,)), ((), ())), preferred_element_type=jnp.float32)


def dot3(a, b):
    return dot(a[0], b[0]) + (dot(a[0], b[1]) + dot(a[1], b[0]))


def is_ring(blocks):
    return blocks == STEPS + 1


def route(shift, blocks):
    return [(i, (i + shift) % blocks) for i in range(blocks)]


def plan_kernel(slots, orbs, late, own, step, remote, count, *refs):
    requests, (known, seen, hist) = refs[:STEPS], refs[STEPS:]
    for s in range(STEPS):
        for k in range(slots):
            requests[s][k] = 0
    for s in range(STEPS):
        hist[slots + s] = 0
        for k in range(orbs):
            seen[s * orbs + k] = -1
    for k in range(slots):
        hist[k] = 0

    def visit(j, carry):
        live = j < count[0]
        s = jnp.where(live, step[j], 0)
        k = remote[j]
        at = seen[s * orbs + k]
        used = hist[slots + s]
        rank = jnp.where(at < 0, used, at)

        @pl.when(live & (at < 0))
        def _():
            for i in range(STEPS):

                @pl.when(s == i)
                def _():
                    requests[i][used] = k

            seen[s * orbs + k] = used
            hist[slots + s] = used + 1

        @pl.when(live)
        def _():
            hist[rank] += 1

        known[j] = s
        known[slots + j] = jnp.where(live, rank, 0)
        known[2 * slots + j] = jnp.where(live, own[j], -1)
        return carry

    lax.fori_loop(0, slots, visit, 0)
    beyond = [jnp.int32(0)]
    for k in reversed(range(slots)):
        beyond.append(beyond[-1] + hist[k])
    beyond = beyond[::-1]
    fits = (beyond[FIRST] <= late) & (beyond[TOTALS[-1]] == 0)
    least = sum((beyond[total] > 0).astype(jnp.int32) for total in TOTALS[:-1])
    for s in range(STEPS):
        requests[s][slots] = jnp.where(fits, least, len(TOTALS))


def expand_kernel(half, full):
    rows, columns = full.shape[0], half.shape[1]
    place = lax.broadcasted_iota(jnp.int32, (rows, columns), 0)
    folded = jnp.minimum(place, rows - place)
    picker = (folded == lax.broadcasted_iota(jnp.int32, (rows, columns), 1)).astype(jnp.float32)
    tall = lax.dot_general(
        picker,
        half[0],
        (((1,), (0,)), ((), ())),
        precision=highest,
        preferred_element_type=jnp.float32,
    )
    full[...] = lax.dot_general(
        tall,
        picker,
        (((1,), (1,)), ((), ())),
        precision=highest,
        preferred_element_type=jnp.float32,
    ) * (1.0 / (NG * NG))


def place_kernel(slots, planes, shares, known, *refs):
    place, choice, order, start = refs[-4:]
    largest = refs[0][slots]
    for s in range(1, STEPS + 1):
        largest = jnp.maximum(largest, refs[s][slots])
    choice[0] = largest
    start[0] = 0

    def tally(j, count):
        return count + (known[slots + j] < FIRST).astype(jnp.int32)

    def visit(j, carry):
        chunk = (known[slots + j] >= FIRST).astype(jnp.int32)
        at = start[chunk]
        start[chunk] = at + 1
        order[at] = j
        return carry

    start[1] = lax.fori_loop(0, slots, tally, jnp.int32(0))
    lax.fori_loop(0, slots, visit, 0)
    me = lax.axis_index("plane")
    base = 0
    for size in shares:
        each = size // planes
        for k in range(planes):
            first = base + partner(me, k, planes) * each
            for q in range(each):
                j = order[first + q]
                to = base + k * each + q
                for part in range(3):
                    place[part * slots + to] = known[part * slots + j]
        base += size


def pieces(lines):
    whole = lines // 8 * 8
    return [(0, whole)] + ([(lines - 8, 8)] if whole < lines else [])


def move_row(source, at, target, to, lines):
    for start, size in pieces(lines):
        target[pl.ds(to + start, size), :] = source[pl.ds(at + start, size), :]


def pack_kernel(lines, low, high, wanted, orbitals, sent):
    for c in range(low, high):
        move_row(orbitals, wanted[c] * lines, sent, (c - low) * lines, lines)


def packs_kernel(lines, *refs):
    wanted, orbitals, sent = refs[:STEPS], refs[STEPS], refs[STEPS + 1 :]
    for s in range(STEPS):
        for c in range(FIRST, TOTALS[-1]):
            for start, size in pieces(lines):
                value = orbitals[pl.ds(wanted[s][c] * lines + start, size), :]
                to = (c - FIRST) * lines + start
                for i, total in enumerate(TOTALS):
                    if c < total:
                        sent[i * STEPS + s][pl.ds(to, size), :] = value


def stage_kernel(orbitals, known, staged):
    staged[...] = orbitals[...]


def own_kernel(slots, lines, base, size, place, orbitals, owned):
    for j in range(size):
        near = jnp.maximum(place[2 * slots + base + j], 0) * lines
        move_row(orbitals, near, owned, j * lines, lines)


def density_kernel(slots, lines, planes, bounds, base, size, place, owned, *refs):
    received, parts, kept = refs[: STEPS * len(bounds)], refs[-planes - 1 : -1], refs[-1]
    each = size // planes
    for j in range(size):
        s, rank = place[base + j], place[slots + base + j]
        for start, count in pieces(lines):
            for c, (low, high) in enumerate(zip((0,) + bounds, bounds)):
                row = jnp.clip(rank - low, 0, high - low - 1) * lines + start
                found = received[c * STEPS][pl.ds(row, count), :]
                for i in range(1, STEPS):
                    other = received[c * STEPS + i][pl.ds(row, count), :]
                    found = jnp.where(s == i, other, found)
                value = found if c == 0 else jnp.where(rank >= low, found, value)
            kept[pl.ds(j * lines + start, count), :] = value
            parts[j // each][pl.ds(j % each * lines + start, count), :] = (
                owned[pl.ds(j * lines + start, count), :] * value
            )


def sum_kernel(slots, lines, planes, base, size, fresh, place, *refs):
    kept, parts = refs[0], refs[1 : 1 + planes]
    out = refs[-1]
    if fresh:
        out[...] = jnp.zeros_like(out)
    else:
        out[...] = refs[1 + planes][...]
    each = size // planes
    for j in range(size):
        near = place[2 * slots + base + j] * lines

        @pl.when(near >= 0)
        def _():
            part, first = parts[j // each], j % each * lines
            added = [
                out[pl.ds(near + start, count), :]
                + part[pl.ds(first + start, count), :] * kept[pl.ds(j * lines + start, count), :]
                for start, count in pieces(lines)
            ]
            for (start, count), value in zip(pieces(lines), added):
                out[pl.ds(near + start, count), :] = value


def transform_kernel(pairs, lines, planes, *refs):
    parts = refs[:planes]
    into_hi, into_lo, back_hi, back_lo, mix_hi, mix_lo, unmix_hi, unmix_lo, kernel = refs[
        planes : planes + 9
    ]
    outs = refs[planes + 9 : 2 * planes + 9]
    cells, waves, result = refs[2 * planes + 9 :]
    whole = planes * lines
    rows = NG // GROUP
    me = lax.axis_index("plane")
    for k in range(planes):
        slab = partner(me, k, planes) * lines
        for p in range(pairs):
            move_row(parts[k], p * lines, cells, p * whole + slab, lines)
    line = [split_value(cells[pl.ds(t, pairs * rows, stride=LINES), :]) for t in range(LINES)]
    for r in range(GROUP):
        wide = [jnp.concatenate([line[r][i], line[r + 1][i]], axis=1) for i in range(2)]
        found = dot3(wide, (into_hi[r], into_lo[r]))
        for p in range(pairs):
            waves[p, r * rows : (r + 1) * rows, :] = found[p * rows : (p + 1) * rows, :]
    mix = (mix_hi[...], mix_lo[...])
    unmix = (unmix_hi[...], unmix_lo[...])
    together = 3 if pairs % 3 == 0 else 1

    def filter_some(i, carry):
        for p in range(together):
            at = i * together + p
            spectrum = dot3(mix, split_value(waves[at])) * kernel[...]
            waves[at] = dot3(unmix, split_value(spectrum))
        return carry

    lax.fori_loop(0, pairs // together, filter_some, 0)
    carried = None
    for r in range(GROUP):
        mine = jnp.concatenate(
            [waves[p, r * rows : (r + 1) * rows, :] for p in range(pairs)], axis=0
        )
        wide = dot3(split_value(mine), (back_hi[r], back_lo[r]))
        first = wide[:, :LANES] if carried is None else wide[:, :LANES] + carried
        carried = wide[:, LANES:]
        result[pl.ds(r, pairs * rows, stride=LINES), :] = first
    result[pl.ds(GROUP, pairs * rows, stride=LINES), :] = carried
    for k in range(planes):
        slab = partner(me, k, planes) * lines
        for p in range(pairs):
            move_row(result, p * whole + slab, outs[k], p * lines, lines)


def shares_for(slots, planes):
    shares = EARLY + LATE
    units = slots // planes
    cuts = [units * sum(shares[: i + 1]) // sum(shares) for i in range(len(shares))]
    sizes = [(b - a) * planes for a, b in zip([0] + cuts, cuts)]
    return sizes, sum(sizes[len(EARLY) :])


def params():
    return pltpu.CompilerParams(vmem_limit_bytes=VMEM_LIMIT)


def cost(microseconds, flops=0):
    moved = int(microseconds * 1e3)
    return pl.CostEstimate(flops=flops, bytes_accessed=moved, transcendentals=0)


def floats(rows):
    return jax.ShapeDtypeStruct((rows, LANES), jnp.float32)


def partner(i, k, size):
    return i ^ k if size & (size - 1) == 0 else (k - i) % size


def exchange(parts, size):
    return [parts[0] if size & (size - 1) == 0 else lax.ppermute(parts[0], "plane", pairs_of(0, size))] + [
        lax.ppermute(parts[k], "plane", pairs_of(k, size)) for k in range(1, size)
    ]


def pairs_of(k, size):
    return [(i, partner(i, k, size)) for i in range(size)]


def local(orbitals, kernel_half, pair_own, pair_step, pair_remote, pair_count):
    groups, blocks, planes = (lax.axis_size(name) for name in ("groups", "blk", "plane"))
    orbs, depth, cell_count = orbitals.shape
    slots = pair_own.shape[0]
    lines = cell_count // LANES
    flat = orbitals.reshape(orbs * lines, LANES)
    shares, late = shares_for(slots, planes)

    width = -(-(slots + 1) // LANES) * LANES
    *requests, known = pl.pallas_call(
        functools.partial(plan_kernel, slots, orbs, late),
        out_shape=(
            *[jax.ShapeDtypeStruct((width,), jnp.int32)] * STEPS,
            jax.ShapeDtypeStruct((3 * slots,), jnp.int32),
        ),
        in_specs=[smem] * 4,
        out_specs=(smem,) * (STEPS + 1),
        scratch_shapes=[
            pltpu.SMEM((STEPS * orbs,), jnp.int32),
            pltpu.SMEM((slots + STEPS,), jnp.int32),
        ],
        cost_estimate=cost(2.3),
        name="plan",
    )(pair_own, pair_step, pair_remote, pair_count)

    wanted = [lax.ppermute(requests[s], "blk", route(-s - 1, blocks)) for s in range(STEPS)]
    flat = pl.pallas_call(
        stage_kernel,
        out_shape=floats(orbs * lines),
        in_specs=[vmem, smem],
        out_specs=vmem,
        compiler_params=params(),
        cost_estimate=cost(0.9),
        name="stage",
    )(flat, known)

    def send(low, high, flat, wanted):
        packs = [
            pl.pallas_call(
                functools.partial(pack_kernel, lines, low, high),
                out_shape=floats((high - low) * lines),
                in_specs=[smem, vmem],
                out_specs=vmem,
                compiler_params=params(),
                cost_estimate=cost(0.5),
                name="pack",
            )(wanted[s], flat)
            for s in range(STEPS)
        ]
        return packs, [lax.ppermute(packs[s], "blk", route(s + 1, blocks)) for s in range(STEPS)]

    def make_density(bounds, base, size, place, owned, received, after):
        each = size // planes
        return pl.pallas_call(
            functools.partial(density_kernel, slots, lines, planes, bounds, base, size),
            out_shape=[floats(each * lines)] * planes + [floats(size * lines)],
            in_specs=[smem, vmem] + [vmem] * len(received) + [hbm] * len(after),
            out_specs=[vmem] * (planes + 1),
            compiler_params=params(),
            cost_estimate=cost(0.05 * size),
            name="density",
        )(place, owned, *received, *after)

    def filter_parts(parts, kernel, tables):
        each = parts[0].shape[0] // lines
        backs = pl.pallas_call(
            functools.partial(transform_kernel, each, lines, planes),
            out_shape=[floats(each * lines)] * planes,
            in_specs=[vmem] * (planes + 9),
            out_specs=[vmem] * planes,
            scratch_shapes=[
                pltpu.VMEM((each * planes * lines, LANES), jnp.float32),
                pltpu.VMEM((each, NG, NG), jnp.float32),
                pltpu.VMEM((each * planes * lines, LANES), jnp.float32),
            ],
            compiler_params=params(),
            cost_estimate=cost(0.5 + 0.4 * each),
            name="transform",
        )(*exchange(parts, planes), *tables, kernel)
        return backs

    def add_up(base, size, place, kept, potentials, before):
        return pl.pallas_call(
            functools.partial(sum_kernel, slots, lines, planes, base, size, not before),
            out_shape=floats(orbs * lines),
            in_specs=[smem] + [vmem] * (planes + 1 + len(before)),
            out_specs=vmem,
            compiler_params=params(),
            cost_estimate=cost(0.9),
            name="sum",
        )(place, kept, *potentials, *before)

    def own_rows(c, place, flat):
        return pl.pallas_call(
            functools.partial(own_kernel, slots, lines, sum(shares[:c]), shares[c]),
            out_shape=floats(shares[c] * lines),
            in_specs=[smem, vmem],
            out_specs=vmem,
            compiler_params=params(),
            cost_estimate=cost(0.5),
            name="own",
        )(place, flat)

    def one_chunk(bounds, c, place, owned, kernel, tables, received, before, after=()):
        base, size = sum(shares[:c]), shares[c]
        *parts, kept = make_density(bounds, base, size, place, owned[c], received, after)
        backs = filter_parts(parts, kernel, tables)
        potentials = exchange(backs, planes)
        return add_up(base, size, place, kept, potentials, before), potentials

    packs, first = send(0, FIRST, flat, wanted)
    place, choice = pl.pallas_call(
        functools.partial(place_kernel, slots, planes, shares),
        out_shape=(
            jax.ShapeDtypeStruct((3 * slots,), jnp.int32),
            jax.ShapeDtypeStruct((1,), jnp.int32),
        ),
        in_specs=[smem] * (STEPS + 2) + [hbm] * STEPS,
        out_specs=(smem, smem),
        scratch_shapes=[pltpu.SMEM((slots,), jnp.int32), pltpu.SMEM((2,), jnp.int32)],
        cost_estimate=cost(2.8),
        name="place",
    )(known, requests[0], *wanted, *packs)
    packed = pl.pallas_call(
        functools.partial(packs_kernel, lines),
        out_shape=[floats((t - FIRST) * lines) for t in TOTALS for s in range(STEPS)],
        in_specs=[smem] * STEPS + [vmem],
        out_specs=[vmem] * (STEPS * len(TOTALS)),
        compiler_params=params(),
        cost_estimate=cost(2),
        name="packs",
    )(*wanted, flat)
    owned = [own_rows(c, place, flat) for c in range(len(shares))]
    kernel = pl.pallas_call(
        expand_kernel,
        out_shape=jax.ShapeDtypeStruct((NG, NG), jnp.float32),
        in_specs=[vmem],
        out_specs=vmem,
        cost_estimate=cost(1.4),
        name="expand",
    )(kernel_half)
    if is_ring(blocks) and groups == 2:
        choice = jnp.maximum(choice, lax.ppermute(choice, "groups", [(0, 1), (1, 0)]))
    else:
        choice = lax.pmax(choice, ("groups", "blk"))
    tables = [jnp.asarray(part) for pair in make_tables(NG // planes) for part in pair]

    def finish(total, flat, wanted, packed, place, owned, kernel, tables, first):
        i = TOTALS.index(total)
        packs = packed[i * STEPS : (i + 1) * STEPS]
        later = [lax.ppermute(packs[s], "blk", route(s + 1, blocks)) for s in range(STEPS)]
        summed, after, formed = [], [], []
        for c in range(len(shares)):
            early = c < len(EARLY)
            bounds = (FIRST,) if early else (FIRST, total)
            rows = first if early else first + later
            result, potentials = one_chunk(
                bounds, c, place, owned, kernel, tables, rows, summed, after
            )
            summed = [result]
            if early:
                formed += potentials[1:]
            if c + 1 == len(EARLY):
                after = formed
        return summed[0]

    def general(flat, wanted, packed, place, owned, kernel, tables, first):
        rows = send(0, slots, flat, wanted)[1]
        summed = []
        for c in range(len(shares)):
            summed = [one_chunk((slots,), c, place, owned, kernel, tables, rows, summed)[0]]
        return summed[0]

    summed = lax.switch(
        choice[0],
        [functools.partial(finish, total) for total in TOTALS] + [general],
        flat,
        wanted,
        packed,
        place,
        owned,
        kernel,
        tables,
        first,
    )
    return summed.reshape(orbs, depth, cell_count)


def solution(mesh):
    in_specs = (
        P(("groups", "blk"), None, "plane"),
        P(),
        P(("groups", "blk")),
        P(("groups", "blk")),
        P(("groups", "blk")),
        P(("groups", "blk")),
    )
    out_specs = P(("groups", "blk"), None, "plane")
    return jax.shard_map(local, mesh=mesh, in_specs=in_specs, out_specs=out_specs, check_vma=False)
```
